32 devices in a mesh: dp: 16 (over z, y, x), seq: 2 (over core).
Axes of the slice: x: 2, y: 2, z: 4, core: 2. Of those that a mesh axis runs over, the one named last changes fastest.
Arguments:
- dec_in: bfloat16 [2, 32, 256, 512], P(None, 'dp', 'seq'), may hold values from -6 to 6
- enc_out: bfloat16 [2, 32, 256, 512], P(None, 'dp', 'seq'), may hold values from -6 to 6
- out_grad: bfloat16 [2, 32, 256, 512], P(None, 'dp', 'seq'), may hold values from -6 to 6
- tgt_len: int32 [2, 32], P(None, 'dp'), may hold values from 4 to 256, as said below
- src_len: int32 [2, 32], P(None, 'dp'), may hold values from 4 to 256, as said below
- pair_id: int32 [2], replicated, may hold values from 0 to 7
- self_qkv: bfloat16 [512, 1536], replicated, may hold values from -0.25 to 0.25
- self_out: bfloat16 [512, 512], replicated, may hold values from -1 to 1
- cross_q: bfloat16 [512, 512], replicated, may hold values from -0.25 to 0.25
- cross_kv: bfloat16 [512, 1024], replicated, may hold values from -0.25 to 0.25
- cross_out: bfloat16 [512, 512], replicated, may hold values from -1 to 1
- ff_in: bfloat16 [512, 2048], replicated, may hold values from -0.25 to 0.25
- ff_out: bfloat16 [2048, 512], replicated, may hold values from -0.125 to 0.125
- norm_gain: bfloat16 [3, 512], replicated, may hold values from 0.5 to 1.5
- norm_bias: bfloat16 [3, 512], replicated, may hold values from -2 to 2
- lang_table: bfloat16 [8, 512], replicated, may hold values from -3 to 3
Outputs:
- output: bfloat16 [2, 32, 256, 512], P(None, 'dp', 'seq')
- grad_input: bfloat16 [2, 32, 256, 512], P(None, 'dp', 'seq')
- grad_encoder: bfloat16 [2, 32, 256, 512], P(None, 'dp', 'seq')
- grad_self_qkv: float32 [512, 1536], P(None, 'seq')
- grad_self_out: float32 [512, 512], P(None, 'seq')
- grad_cross_q: float32 [512, 512], P(None, 'seq')
- grad_cross_kv: float32 [512, 1024], P(None, 'seq')
- grad_cross_out: float32 [512, 512], P(None, 'seq')
- grad_ff_in: float32 [512, 2048], P(None, 'seq')
- grad_ff_out: float32 [2048, 512], P(None, 'seq')
- grad_norm_gain: float32 [3, 512], P(None, 'seq')
- grad_norm_bias: float32 [3, 512], P(None, 'seq')
- grad_lang_table: float32 [8, 512], P(None, 'seq')
The draws below stay inside these ranges and needn't reach their ends.
Inputs may be any that keep to these rules, and one draw needn't show every extreme that they name: `tgt_len`: in each group of sentences on one index of dp (all micro-batches together) one sentence has exactly 256 positions. `src_len`: in each group of sentences on one index of dp (all micro-batches together) one sentence has exactly 256 positions.
All inputs are finite; a program needn't handle non-finite values.
Results may differ from the reference program's by a relative error of at most 0.02.
Values may be sent and summed in bfloat16 or wider, within the bound.
No kernel may reach another device: no remote copies, remote signals or barrier semaphores. Data moves between devices by JAX's collectives and lax.ppermute only.
A program may use at most 128 MiB of HBM per device.

```python
import math
import jax
import jax.numpy as jnp
from jax import lax

D = 512
HEADS = 8
FF = 2048
SEQ_LEN = 256
SRC_LEN = 256
MICRO = 2
PAIRS = 8
SENT_MB = 2
BATCH = 32


def ragged_lengths(key, longest):
    first_key, second_key = jax.random.split(key)
    lengths = jax.random.randint(first_key, (MICRO, BATCH), 4, longest + 1)
    groups = BATCH // SENT_MB
    chosen = jax.random.randint(second_key, (groups,), 0, MICRO * SENT_MB)
    slot_index = jnp.arange(MICRO)[:, None, None] * SENT_MB + jnp.arange(SENT_MB)[None, None, :]
    is_full = (slot_index == chosen[None, :, None]).reshape(MICRO, BATCH)
    return jnp.where(is_full, longest, lengths).astype(jnp.int32)


def draw_tgt_len(key, part):
    key = jax.random.fold_in(key, 11)
    return ragged_lengths(key, SEQ_LEN)


def draw_src_len(key, part):
    key = jax.random.fold_in(key, 12)
    return ragged_lengths(key, SRC_LEN)


def level_of(key, shape, shards, smallest, top_value):
    gain = 1.0
    for axis_at, shards_of in shards:
        draws = jax.random.uniform(jax.random.fold_in(jax.random.fold_in(key, 6), axis_at), (shards_of,), jnp.float32, smallest / len(shards), top_value / len(shards))
        gain = gain * jnp.repeat(jnp.exp(draws), shape[axis_at] // shards_of).reshape((-1,) + (1,) * (len(shape) - 1 - axis_at))
    return gain


def normal_values(own_key, shape, deviation, reach, shards=(), held_as=jnp.bfloat16):
    drawn = jax.random.normal(own_key, shape, jnp.float32) * deviation
    if len(shards) > 0:
        drawn = level_of(own_key, shape, shards, -0.22, 0.18) * drawn
    return jnp.clip(drawn, min=-reach, max=reach).astype(held_as)


def setup_inputs(seed: int = 0) -> dict:
    key_of = jax.random.split(jax.random.key(seed), 17)
    dec_in = normal_values(key_of[0], (MICRO, BATCH, SEQ_LEN, D), 1.0, 6.0, ((1, 16), (2, 2)))
    enc_out = normal_values(key_of[1], (MICRO, BATCH, SRC_LEN, D), 1.0, 6.0, ((1, 16), (2, 2)))
    out_grad = normal_values(key_of[2], (MICRO, BATCH, SEQ_LEN, D), 1.0, 6.0, ((1, 16), (2, 2)))
    tgt_len = draw_tgt_len(jax.random.fold_in(key_of[16], 71), 0)
    src_len = draw_src_len(jax.random.fold_in(key_of[16], 71), 0)
    pair_id = jax.random.randint(key_of[5], (MICRO,), 0, PAIRS).astype(jnp.int32)
    self_qkv = normal_values(key_of[6], (D, 3 * D), D ** -0.5, 0.25)
    self_out = normal_values(key_of[7], (D, D), (D // 16) ** -0.5, 1.0)
    cross_q = normal_values(key_of[8], (D, D), D ** -0.5, 0.25)
    cross_kv = normal_values(key_of[9], (D, 2 * D), D ** -0.5, 0.25)
    cross_out = normal_values(key_of[10], (D, D), (D // 16) ** -0.5, 1.0)
    ff_in = normal_values(key_of[11], (D, FF), D ** -0.5, 0.25)
    ff_out = normal_values(key_of[12], (FF, D), FF ** -0.5, 0.125)
    norm_gain = jnp.clip(1.0 + 0.1 * jax.random.normal(key_of[13], (3, D), jnp.float32), 0.5, 1.5).astype(jnp.bfloat16)
    norm_bias = normal_values(key_of[14], (3, D), 0.3, 2.0)
    lang_table = normal_values(key_of[15], (PAIRS, D), 0.5, 3.0)
    return {"dec_in": dec_in, "enc_out": enc_out, "out_grad": out_grad, "tgt_len": tgt_len, "src_len": src_len, "pair_id": pair_id, "self_qkv": self_qkv, "self_out": self_out, "cross_q": cross_q, "cross_kv": cross_kv, "cross_out": cross_out, "ff_in": ff_in, "ff_out": ff_out, "norm_gain": norm_gain, "norm_bias": norm_bias, "lang_table": lang_table}


@jax.custom_vjp
def low(v):
    return lax.optimization_barrier(v.astype(jnp.bfloat16)).astype(jnp.float32)

@jax.custom_vjp
def low_back(v):
    return v

def low_keep(v):
    return (low(v), None)

def low_pass(kept, grad):
    return (grad,)

def back_keep(v):
    return (v, None)

def back_low(kept, grad):
    return (low(grad),)
low.defvjp(low_keep, low_pass)
low_back.defvjp(back_keep, back_low)
NORM_EPS = 1e-05
NEG_FILL = -1e+30

def layer_norm(values, gain_row, bias_row):
    center = values - lax.optimization_barrier(jnp.mean(values, -1, keepdims=True))
    spread = lax.optimization_barrier(jnp.mean(center * center, -1, keepdims=True))
    return center * lax.rsqrt(spread + NORM_EPS) * gain_row + bias_row

def smooth_gelu(values):
    return 0.5 * values * (1.0 + jnp.tanh(0.7978845608028654 * (values + 0.044715 * values * values * values)))

def matmul_full(values, weight):
    return jnp.einsum('btd,de->bte', values, weight, precision=lax.Precision.HIGHEST)

def split_heads(values):
    return values.reshape(values.shape[:-1] + (HEADS, values.shape[-1] // HEADS))

def attention(queries, keys, values, key_mask):
    head_scale = 1.0 / math.sqrt(queries.shape[-1] // HEADS)
    scores = jnp.einsum('bqhd,bkhd->bhqk', split_heads(queries), split_heads(keys), precision=lax.Precision.HIGHEST) * head_scale
    scores = low_back(scores)
    scores = jnp.where(key_mask[:, None], scores, NEG_FILL)
    row_top = lax.optimization_barrier(jnp.max(scores, -1, keepdims=True))
    exp_scores = jnp.exp(scores - row_top)
    probability = exp_scores / lax.optimization_barrier(jnp.sum(exp_scores, -1, keepdims=True))
    mixed_out = jnp.einsum('bhqk,bkhd->bqhd', low(probability), split_heads(values), precision=lax.Precision.HIGHEST)
    return mixed_out.reshape(queries.shape)

def decoder_layer(weights, inputs, encoded, self_mask, cross_mask, pair_pick):
    self_qkv, self_out, cross_q, cross_kv, cross_out, ff_in, ff_out, norm_gain, norm_bias, lang_table = weights
    model_width = inputs.shape[-1]
    embedded = inputs + jnp.dot(pair_pick, lang_table, precision=lax.Precision.HIGHEST)[None, None, :]
    packed = low_back(low(matmul_full(low(embedded), self_qkv)))
    queries = packed[..., :model_width]
    keys = packed[..., model_width:2 * model_width]
    values = packed[..., 2 * model_width:]
    attended = low_back(low(attention(queries, keys, values, self_mask)))
    first_sum = embedded + low_back(matmul_full(attended, self_out))
    first_norm = layer_norm(first_sum, norm_gain[0], norm_bias[0])
    cross_queries = low_back(low(matmul_full(low(first_norm), cross_q)))
    cross_packed = low_back(low(matmul_full(encoded, cross_kv)))
    crossed = low_back(low(attention(cross_queries, cross_packed[..., :model_width], cross_packed[..., model_width:], cross_mask)))
    second_sum = first_norm + low_back(matmul_full(crossed, cross_out))
    second_norm = layer_norm(second_sum, norm_gain[1], norm_bias[1])
    ff_inner = low_back(matmul_full(low(second_norm), ff_in))
    hidden = low_back(low(smooth_gelu(ff_inner)))
    third_sum = second_norm + low_back(matmul_full(hidden, ff_out))
    return layer_norm(third_sum, norm_gain[2], norm_bias[2])

def reference(dec_in, enc_out, out_grad, tgt_len, src_len, pair_id, self_qkv, self_out, cross_q, cross_kv, cross_out, ff_in, ff_out, norm_gain, norm_bias, lang_table):
    group_size = math.gcd(BATCH, 16)
    group_count = MICRO * BATCH // group_size
    inputs = dec_in.astype(jnp.float32).reshape(group_count, group_size, SEQ_LEN, D)
    encoded = enc_out.astype(jnp.float32).reshape(group_count, group_size, SRC_LEN, D)
    cotangent = out_grad.astype(jnp.float32).reshape(group_count, group_size, SEQ_LEN, D)
    target_lengths = tgt_len.reshape(group_count, group_size)
    source_lengths = src_len.reshape(group_count, group_size)
    group_pairs = jnp.repeat(pair_id, BATCH // group_size)
    weights = tuple((weight.astype(jnp.float32) for weight in (self_qkv, self_out, cross_q, cross_kv, cross_out, ff_in, ff_out, norm_gain, norm_bias, lang_table)))
    zero_grads = tuple((jnp.zeros(weight.shape, jnp.float32) for weight in weights))
    target_pos = jnp.arange(SEQ_LEN)
    source_pos = jnp.arange(SRC_LEN)

    def group_step(grad_totals, group_item):
        group_inputs, group_encoded, group_cot, group_tgt, group_src, group_pair = group_item
        self_mask = (target_pos[None, None, :] <= target_pos[None, :, None]) & (target_pos[None, None, :] < group_tgt[:, None, None])
        cross_mask = jnp.broadcast_to(source_pos[None, None, :] < group_src[:, None, None], (group_size, SEQ_LEN, SRC_LEN))
        pair_pick = (jnp.arange(PAIRS) == group_pair).astype(jnp.float32)

        def forward(layer_weights, layer_inputs, layer_encoded):
            return decoder_layer(layer_weights, layer_inputs, layer_encoded, self_mask, cross_mask, pair_pick)
        result, pullback = jax.vjp(forward, weights, group_inputs, group_encoded)
        grad_weights, grad_inputs, grad_encoded = pullback(group_cot)
        grad_totals = tuple((total + grad_term for total, grad_term in zip(grad_totals, grad_weights)))
        return (grad_totals, (result.astype(jnp.bfloat16), grad_inputs.astype(jnp.bfloat16), grad_encoded.astype(jnp.bfloat16)))
    grad_totals, (results, input_grads, encoder_grads) = lax.scan(group_step, zero_grads, (inputs, encoded, cotangent, target_lengths, source_lengths, group_pairs))
    return (results.reshape(MICRO, BATCH, SEQ_LEN, D), input_grads.reshape(MICRO, BATCH, SEQ_LEN, D), encoder_grads.reshape(MICRO, BATCH, SRC_LEN, D), grad_totals[0], grad_totals[1], grad_totals[2], grad_totals[3], grad_totals[4], grad_totals[5], grad_totals[6], grad_totals[7], grad_totals[8], grad_totals[9])
```

```python
import functools

import jax
import jax.numpy as jnp
from jax import lax
from jax.experimental import pallas as pl
from jax.experimental.pallas import tpu as pltpu
from jax.sharding import PartitionSpec as P

HEADS = 8
NORM_EPS = 1e-05
NEG_FILL = -1e30
BF = jnp.bfloat16
F32 = jnp.float32
MIB = 1 << 20
LANES = 1024


def mm(a, b):
    return lax.dot_general(a, b, (((1,), (0,)), ((), ())), preferred_element_type=F32)


def mm_bt(a, b):
    return lax.dot_general(a, b, (((1,), (1,)), ((), ())), preferred_element_type=F32)


def mm_at(a, b):
    return lax.dot_general(a, b, (((0,), (0,)), ((), ())), preferred_element_type=F32)


def norm_forward(values, gain, bias):
    center = values - jnp.mean(values, -1, keepdims=True)
    rstd = lax.rsqrt(jnp.mean(center * center, -1, keepdims=True) + NORM_EPS)
    xhat = center * rstd
    return xhat, rstd, xhat * gain + bias


def norm_backward(xhat, rstd, gain, upstream):
    scaled = upstream * gain
    first = jnp.mean(scaled, -1, keepdims=True)
    second = jnp.mean(scaled * xhat, -1, keepdims=True)
    grad = rstd * (scaled - first - xhat * second)
    return grad, jnp.sum(upstream * xhat, 0, keepdims=True), jnp.sum(upstream, 0, keepdims=True)


def lane_half(shape, half):
    lane = lax.broadcasted_iota(jnp.int32, shape, 1)
    return (lane < 64) if half == 0 else (lane >= 64)


def attend(q_ref, k_ref, v_ref, k_at, v_at, bias_ref, p_ref, out_ref, length):
    pairs = HEADS // 2

    def body(index, _):
        sentence = index // pairs
        pair = index - sentence * pairs
        rows = pl.ds(pl.multiple_of(sentence * length, length), length)
        lanes = pl.multiple_of(pair * 128, 128)
        queries = q_ref[rows, pl.ds(lanes, 128)]
        keys = k_ref[rows, pl.ds(pl.multiple_of(k_at + lanes, 128), 128)]
        values = v_ref[rows, pl.ds(pl.multiple_of(v_at + lanes, 128), 128)]
        bias = bias_ref[sentence]
        mixed = []
        for half in range(2):
            mine = lane_half(queries.shape, half)
            scores = mm_bt(jnp.where(mine, queries, jnp.zeros_like(queries)), keys) + bias
            top = jnp.max(scores, -1, keepdims=True)
            grown = jnp.exp(scores - top)
            probs = (grown * (1.0 / jnp.sum(grown, -1, keepdims=True))).astype(BF)
            p_ref[2 * index + half] = probs
            mixed.append(mm(probs, values))
        out_ref[rows, pl.ds(lanes, 128)] = jnp.where(
            lane_half(mixed[0].shape, 0), mixed[0], mixed[1]
        ).astype(BF)
        return 0

    lax.fori_loop(0, 2 * pairs, body, 0)


def attend_back(q_ref, k_ref, v_ref, k_at, v_at, p_ref, go_ref, gq_ref, gk_ref, gv_ref, gk_at, gv_at, length):
    pairs = HEADS // 2

    def body(index, _):
        sentence = index // pairs
        pair = index - sentence * pairs
        rows = pl.ds(pl.multiple_of(sentence * length, length), length)
        lanes = pl.multiple_of(pair * 128, 128)
        queries = q_ref[rows, pl.ds(lanes, 128)]
        keys = k_ref[rows, pl.ds(pl.multiple_of(k_at + lanes, 128), 128)]
        values = v_ref[rows, pl.ds(pl.multiple_of(v_at + lanes, 128), 128)]
        grads = go_ref[rows, pl.ds(lanes, 128)]
        gq, gk, gv = [], [], []
        for half in range(2):
            mine = lane_half(grads.shape, half)
            probs_low = p_ref[2 * index + half]
            probs = probs_low.astype(F32)
            grad_probs = mm_bt(jnp.where(mine, grads, jnp.zeros_like(grads)), values)
            row_dot = jnp.sum(probs * grad_probs, -1, keepdims=True)
            grad_scores = (probs * (grad_probs - row_dot)).astype(BF)
            gq.append(mm(grad_scores, keys))
            gk.append(mm_at(grad_scores, queries))
            gv.append(mm_at(probs_low, grads))
        first = lane_half(gq[0].shape, 0)
        gq_ref[rows, pl.ds(lanes, 128)] = (jnp.where(first, gq[0], gq[1]) * 0.125).astype(BF)
        gk_ref[rows, pl.ds(pl.multiple_of(gk_at + lanes, 128), 128)] = jnp.where(first, gk[0], gk[1]).astype(BF)
        gv_ref[rows, pl.ds(pl.multiple_of(gv_at + lanes, 128), 128)] = jnp.where(first, gv[0], gv[1]).astype(BF)
        return 0

    lax.fori_loop(0, 2 * pairs, body, 0)


def gather_rows(out_ref, place, own, other, length, change):
    half = length // 2
    for sentence in range(2):
        out_ref[pl.ds(pl.multiple_of(sentence * length + place * half, half), half), :] = change(own[sentence])
        out_ref[pl.ds(pl.multiple_of(sentence * length + (1 - place) * half, half), half), :] = change(other[sentence])


def part_rows(ref, place, own_ref, other_ref, length):
    half = length // 2
    for sentence in range(2):
        own_ref[sentence] = ref[pl.ds(pl.multiple_of(sentence * length + place * half, half), half), :]
        other_ref[sentence] = ref[pl.ds(pl.multiple_of(sentence * length + (1 - place) * half, half), half), :]


def forward_kernel(
    place_ref, tgt_ref, src_ref, pair_ref,
    dec_ref, dec2_ref, enc_ref, enc2_ref, og_ref, og2_ref,
    w_qkv, w_so, w_cq, w_ckv, w_co, w_fi, w_fo, gain_ref, nbias_ref, table_ref,
    out_own, out_oth, send_ref, keep_ref, gss_ref, dnorm_ref,
    elow, qkv, p_self, att, xhat1, rstd1, flow, encs, cq, ckv, p_cross, crossed,
    e_ref, bias_ref, fnorm, xhat2, rstd2, snorm, slow, hidden, slope, third, gff, ginner, og_s, outs, tr, trh,
):
    place = place_ref[0]
    length = 2 * dec_ref.shape[2]
    width = dec_ref.shape[3]
    inner = w_fi.shape[1]
    sents = range(2)
    rows_of = lambda s: pl.ds(s * length, length)
    gain = gain_ref[...].astype(F32)
    nbias = nbias_ref[...].astype(F32)
    picked = lax.broadcasted_iota(jnp.int32, table_ref.shape, 0) == pair_ref[place]
    row = jnp.sum(jnp.where(picked, table_ref[...].astype(F32), 0.0), 0, keepdims=True)

    gather_rows(e_ref, place, dec_ref[place], dec2_ref[place], length, lambda v: v.astype(F32) + row)
    gather_rows(encs, place, enc_ref[place], enc2_ref[place], length, lambda v: v)
    gather_rows(og_s, place, og_ref[place], og2_ref[place], length, lambda v: v)
    keys_at = lax.broadcasted_iota(jnp.int32, (length, length), 1)
    query_at = lax.broadcasted_iota(jnp.int32, (length, length), 0)
    for s in sents:
        bias_ref[s] = jnp.where((keys_at <= query_at) & (keys_at < tgt_ref[place, s]), 0.0, NEG_FILL)
    for s in sents:
        low = e_ref[rows_of(s), :].astype(BF)
        elow[rows_of(s), :] = low
        qkv[rows_of(s), 0:width] = (mm(low, w_qkv[:, 0:width]) * 0.125).astype(BF)
        qkv[rows_of(s), width : 3 * width] = mm(low, w_qkv[:, width : 3 * width]).astype(BF)
        ckv[rows_of(s), :] = mm(encs[rows_of(s), :], w_ckv[...]).astype(BF)
    attend(qkv, qkv, qkv, width, 2 * width, bias_ref, p_self, att, length)
    for s in sents:
        total = e_ref[rows_of(s), :] + mm(att[rows_of(s), :], w_so[...])
        xhat, rstd, normed = norm_forward(total, gain[0:1], nbias[0:1])
        xhat1[rows_of(s), :] = xhat
        rstd1[rows_of(s), :] = jnp.broadcast_to(rstd, (length, 128))
        fnorm[rows_of(s), :] = normed
        low = normed.astype(BF)
        flow[rows_of(s), :] = low
        cq[rows_of(s), :] = (mm(low, w_cq[...]).astype(BF).astype(F32) * 0.125).astype(BF)
    for s in sents:
        bias_ref[s] = jnp.where(keys_at < src_ref[place, s], 0.0, NEG_FILL)
    attend(cq, ckv, ckv, 0, width, bias_ref, p_cross, crossed, length)
    for s in sents:
        total = fnorm[rows_of(s), :] + mm(crossed[rows_of(s), :], w_co[...])
        xhat, rstd, normed = norm_forward(total, gain[1:2], nbias[1:2])
        xhat2[rows_of(s), :] = xhat
        rstd2[rows_of(s), :] = jnp.broadcast_to(rstd, (length, 128))
        snorm[rows_of(s), :] = normed
        slow[rows_of(s), :] = normed.astype(BF)
        third[rows_of(s), :] = normed
    step = 512

    def feed(index, _):
        cols = pl.ds(pl.multiple_of(index * step, step), step)
        for s in sents:
            v = mm(slow[rows_of(s), :], w_fi[:, cols])
            square = v * v
            bent = jnp.tanh(v * (0.7978845608028654 + (0.7978845608028654 * 0.044715) * square))
            half = 0.5 * (1.0 + bent)
            hid = (v * half).astype(BF)
            hidden[rows_of(s), cols] = hid
            slope[rows_of(s), cols] = (
                half
                + 0.5 * v * (1.0 - bent * bent) * (0.7978845608028654 + (3 * 0.7978845608028654 * 0.044715) * square)
            ).astype(BF)
            third[rows_of(s), :] += mm(hid, w_fo[cols, :])
        return 0

    lax.fori_loop(0, inner // step, feed, 0)
    gains_three = jnp.zeros((1, width), F32)
    biases_three = jnp.zeros((1, width), F32)
    for s in sents:
        xhat, rstd, normed = norm_forward(third[rows_of(s), :], gain[2:3], nbias[2:3])
        outs[rows_of(s), :] = normed.astype(BF)
        grad, dgain, dbias = norm_backward(xhat, rstd, gain[2:3], og_s[rows_of(s), :].astype(F32))
        gains_three += dgain
        biases_three += dbias
        third[rows_of(s), :] = grad
        gff[rows_of(s), :] = grad.astype(BF)
    part_rows(outs, place, out_own, out_oth, length)

    def feed_back(index, _):
        cols = pl.ds(pl.multiple_of(index * step, step), step)
        for s in sents:
            grad_hidden = mm_bt(gff[rows_of(s), :], w_fo[cols, :]).astype(BF)
            grad_inner = (grad_hidden.astype(F32) * slope[rows_of(s), cols].astype(F32)).astype(BF)
            ginner[rows_of(s), cols] = grad_inner
            third[rows_of(s), :] += mm_bt(grad_inner, w_fi[:, cols])
        trh[cols, :] = hidden[:, cols].T
        return 0

    lax.fori_loop(0, inner // step, feed_back, 0)
    tr[...] = slow[...].T
    half_in = inner // 2
    half_out = width // 2
    for which, ref in ((1 - place, send_ref), (place, keep_ref)):

        def block(index, _, which=which, ref=ref):
            cols = pl.ds(pl.multiple_of(which * half_in + index * 256, 256), 256)
            there = pl.ds(pl.multiple_of(index * 256, 256), 256)
            ref[0:width, there] = mm(tr[...], ginner[:, cols]).astype(BF)
            cols = pl.ds(pl.multiple_of(which * half_out, half_out), half_out)
            tall = pl.ds(pl.multiple_of(index * width, width), width)
            ref[width : 2 * width, there] = mm(trh[tall, :], gff[:, cols]).astype(BF)
            return 0

        lax.fori_loop(0, half_in // 256, block, 0)
    gains_two = jnp.zeros((1, width), F32)
    biases_two = jnp.zeros((1, width), F32)
    for s in sents:
        grad, dgain, dbias = norm_backward(xhat2[rows_of(s), :], rstd2[rows_of(s), 0:1], gain[1:2], third[rows_of(s), :])
        gains_two += dgain
        biases_two += dbias
        gss_ref[rows_of(s), :] = grad
    dnorm_ref[...] = jnp.zeros(dnorm_ref.shape, F32)
    dnorm_ref[1:2, :] = gains_two
    dnorm_ref[2:3, :] = gains_three
    dnorm_ref[4:5, :] = biases_two
    dnorm_ref[5:6, :] = biases_three


def cross_kernel(
    place_ref, gss_ref, dnorm_in, xhat1, rstd1, flow, encs, cq, ckv, p_cross, crossed, w_cq, w_ckv, w_co, gain_ref,
    genc_own, genc_oth, send_ref, keep_ref, gfs_ref, dnorm_ref,
    branch, gcrossed, gcq, gckv, genc, tr,
):
    place = place_ref[0]
    tokens, width = gss_ref.shape
    length = tokens // 2
    sents = range(2)
    rows_of = lambda s: pl.ds(s * length, length)
    gain = gain_ref[...].astype(F32)
    for s in sents:
        low = gss_ref[rows_of(s), :].astype(BF)
        branch[rows_of(s), :] = low
        gcrossed[rows_of(s), :] = mm_bt(low, w_co[...]).astype(BF)
    attend_back(cq, ckv, ckv, 0, width, p_cross, gcrossed, gcq, gckv, gckv, 0, width, length)
    gains_one = jnp.zeros((1, width), F32)
    biases_one = jnp.zeros((1, width), F32)
    for s in sents:
        genc[rows_of(s), :] = mm_bt(gckv[rows_of(s), :], w_ckv[...]).astype(BF)
        first = gss_ref[rows_of(s), :] + mm_bt(gcq[rows_of(s), :], w_cq[...])
        grad, dgain, dbias = norm_backward(xhat1[rows_of(s), :], rstd1[rows_of(s), 0:1], gain[0:1], first)
        gains_one += dgain
        biases_one += dbias
        gfs_ref[rows_of(s), :] = grad
    part_rows(genc, place, genc_own, genc_oth, length)
    dnorm_ref[...] = dnorm_in[...]
    dnorm_ref[0:1, :] = gains_one
    dnorm_ref[3:4, :] = biases_one
    half = width // 2
    for source, grads, at, cols in ((crossed, branch, 0, half), (flow, gcq, half, half), (encs, gckv, width, width)):
        tr[...] = source[...].T
        for which, ref in ((1 - place, send_ref), (place, keep_ref)):
            ref[:, at : at + cols] = mm(tr[...], grads[:, pl.ds(pl.multiple_of(which * cols, cols), cols)]).astype(BF)


def self_kernel(
    place_ref, pair_ref, gfs_ref, dnorm_in, elow, qkv, p_self, att, w_qkv, w_so,
    gin_own, gin_oth, send_ref, keep_ref,
    branch, gatt, gqkv, gin, tr, small,
):
    place = place_ref[0]
    tokens, width = gfs_ref.shape
    length = tokens // 2
    sents = range(2)
    rows_of = lambda s: pl.ds(s * length, length)
    for s in sents:
        low = gfs_ref[rows_of(s), :].astype(BF)
        branch[rows_of(s), :] = low
        gatt[rows_of(s), :] = mm_bt(low, w_so[...]).astype(BF)
    attend_back(qkv, qkv, qkv, width, 2 * width, p_self, gatt, gqkv, gqkv, gqkv, width, 2 * width, length)
    table_row = jnp.zeros((1, width), F32)
    for s in sents:
        start = gfs_ref[rows_of(s), :] + mm_bt(gqkv[rows_of(s), :], w_qkv[...])
        gin[rows_of(s), :] = start.astype(BF)
        table_row += jnp.sum(start, 0, keepdims=True)
    part_rows(gin, place, gin_own, gin_oth, length)
    small[0:8, :] = dnorm_in[...]
    picked = lax.broadcasted_iota(jnp.int32, (8, width), 0) == pair_ref[place]
    small[8:16, :] = jnp.where(picked, jnp.broadcast_to(table_row, (8, width)), 0.0)
    half = width // 2
    for which, ref in ((1 - place, send_ref), (place, keep_ref)):
        ref[width : width + 16, :] = jnp.zeros((16, ref.shape[1]), BF)
        ref[width : width + 16, 0:half] = small[:, pl.ds(pl.multiple_of(which * half, half), half)].astype(BF)
    for source, grads, at, cols in ((att, branch, 3 * half, half), (elow, gqkv, 0, 3 * half)):
        tr[...] = source[...].T
        for which, ref in ((1 - place, send_ref), (place, keep_ref)):
            ref[0:width, at : at + cols] = mm(tr[...], grads[:, pl.ds(pl.multiple_of(which * cols, half), cols)]).astype(BF)


def add_split_kernel(tail, bit_ref, a_ref, b_ref, send_ref, keep_ref):
    half = send_ref.shape[0] - tail
    bit = bit_ref[0]
    for which, ref in ((1 - bit, send_ref), (bit, keep_ref)):
        rows = pl.ds(pl.multiple_of(which * half, 16), half)
        ref[0:half, :] = (a_ref[rows, :].astype(F32) + b_ref[rows, :].astype(F32)).astype(BF)
        if tail:
            last = pl.ds(2 * half, tail)
            ref[half : half + tail, :] = (a_ref[last, :].astype(F32) + b_ref[last, :].astype(F32)).astype(BF)


def add_spread_kernel(tail, index_ref, a_ref, b_ref, *outs):
    rows = outs[0].shape[0] - tail
    for j, out in enumerate(outs):
        at = pl.ds(pl.multiple_of((index_ref[0] ^ j) * rows, 16), rows)
        out[0:rows, :] = (a_ref[at, :].astype(F32) + b_ref[at, :].astype(F32)).astype(BF)
        if tail:
            last = pl.ds(len(outs) * rows, tail)
            out[rows : rows + tail, :] = (a_ref[last, :].astype(F32) + b_ref[last, :].astype(F32)).astype(BF)


def add_all_kernel(*refs):
    total = refs[0][...].astype(F32)
    for ref in refs[1:-1]:
        total = total + ref[...].astype(F32)
    refs[-1][...] = total.astype(BF)


def join_kernel(index_ref, *refs):
    out = refs[-1]
    rows = refs[0].shape[0]
    for j, ref in enumerate(refs[:-1]):
        out[pl.ds(pl.multiple_of((index_ref[0] ^ j) * rows, 16), rows), :] = ref[...]


def unpack_kernel(unpack, index_ref, mine_ref, got_ref, *outs):
    @pl.when(index_ref[0] == 0)
    def _():
        unpack(mine_ref, got_ref, *outs)

    @pl.when(index_ref[0] != 0)
    def _():
        unpack(got_ref, mine_ref, *outs)


def unpack_ff(low_ref, high_ref, in_ref, out_ref):
    in_ref[...] = low_ref[...].astype(F32)
    width, cols = low_ref.shape[0], out_ref.shape[1]
    for j in range(out_ref.shape[0] // width):
        out_ref[j * width : (j + 1) * width, :] = high_ref[:, j * cols : (j + 1) * cols].astype(F32)


def unpack_columns(low_ref, high_ref, *outs):
    half, at = low_ref.shape[0], 0
    for out in outs:
        cols = pl.ds(at, out.shape[1])
        out[0:half, :] = low_ref[:, cols].astype(F32)
        out[half : 2 * half, :] = high_ref[:, cols].astype(F32)
        at += out.shape[1]


def smem():
    return pl.BlockSpec(memory_space=pltpu.SMEM)


def vmem():
    return pl.BlockSpec(memory_space=pltpu.VMEM)


def call(kernel, scalars, arrays, outs, scratch=(), limit=56, flops=0, name=None):
    moved = sum(a.size * a.dtype.itemsize for a in arrays)
    return pl.pallas_call(
        kernel,
        out_shape=tuple(jax.ShapeDtypeStruct(s, d) for s, d in outs),
        in_specs=[smem() for _ in scalars] + [vmem() for _ in arrays],
        out_specs=tuple(vmem() for _ in outs),
        scratch_shapes=[pltpu.VMEM(s, d) for s, d in scratch],
        compiler_params=pltpu.CompilerParams(vmem_limit_bytes=limit * MIB),
        cost_estimate=pl.CostEstimate(flops=flops, bytes_accessed=moved, transcendentals=0),
        name=name,
    )(*scalars, *arrays)


def local(
    dec_in, enc_out, out_grad, tgt_len, src_len, pair_id,
    self_qkv, self_out, cross_q, cross_kv, cross_out, ff_in, ff_out, norm_gain, norm_bias, lang_table,
):
    micro_count, sent_count, local_len, width = dec_in.shape
    seq_count = lax.axis_size("seq")
    dp_count = lax.axis_size("dp")
    place = lax.axis_index("seq")
    dp_place = lax.axis_index("dp")
    inner = ff_in.shape[1]
    length = local_len * seq_count
    tokens = sent_count * length
    half = width // 2
    place_arr = place.reshape(1)
    swap = [(0, 1), (1, 0)]

    dec2 = lax.ppermute(dec_in, "seq", swap)
    enc2 = lax.ppermute(enc_out, "seq", swap)
    og2 = lax.ppermute(out_grad, "seq", swap)

    rows = (sent_count, local_len, width)
    whole = (tokens, width)
    probs = (sent_count * HEADS, length, length)
    (
        out_own, out_oth, send_a, keep_a, gss, dnorm,
        elow, qkv, p_self, att, xhat1, rstd1, flow, encs, cq, ckv, p_cross, crossed,
    ) = call(
        forward_kernel,
        (place_arr, tgt_len, src_len, pair_id),
        (dec_in, dec2, enc_out, enc2, out_grad, og2, self_qkv, self_out, cross_q, cross_kv, cross_out, ff_in, ff_out,
         norm_gain, norm_bias, lang_table),
        [
            (rows, BF), (rows, BF), ((2 * width, LANES), BF), ((2 * width, LANES), BF), (whole, F32), ((8, width), F32),
            (whole, BF), ((tokens, 3 * width), BF), (probs, BF), (whole, BF), (whole, F32), ((tokens, 128), F32),
            (whole, BF), (whole, BF), (whole, BF), ((tokens, 2 * width), BF), (probs, BF), (whole, BF),
        ],
        [
            (whole, F32), ((sent_count, length, length), F32), (whole, F32), (whole, F32), ((tokens, 128), F32),
            (whole, F32), (whole, BF), ((tokens, inner), BF), ((tokens, inner), BF), (whole, F32), (whole, BF),
            ((tokens, inner), BF), (whole, BF), (whole, BF), ((width, tokens), BF), ((inner, tokens), BF),
        ],
        name="forward",
    )
    genc_own, genc_oth, send_b, keep_b, gfs, dnorm = call(
        cross_kernel,
        (place_arr,),
        (gss, dnorm, xhat1, rstd1, flow, encs, cq, ckv, p_cross, crossed, cross_q, cross_kv, cross_out, norm_gain),
        [(rows, BF), (rows, BF), ((width, LANES), BF), ((width, LANES), BF), (whole, F32), ((8, width), F32)],
        [(whole, BF), (whole, BF), (whole, BF), ((tokens, 2 * width), BF), (whole, BF), ((width, tokens), BF)],
        limit=40,
        name="cross_back",
    )
    gin_own, gin_oth, send_c, keep_c = call(
        self_kernel,
        (place_arr, pair_id),
        (gfs, dnorm, elow, qkv, p_self, att, self_qkv, self_out),
        [(rows, BF), (rows, BF), ((width + 16, LANES), BF), ((width + 16, LANES), BF)],
        [(whole, BF), (whole, BF), ((tokens, 3 * width), BF), (whole, BF), ((width, tokens), BF), ((16, width), F32)],
        limit=40,
        name="self_back",
    )

    def both(own, other):
        got = lax.ppermute(other, "seq", swap)
        return jnp.where(place == 0, jnp.stack([own, got]), jnp.stack([got, own]))

    output = both(out_own, out_oth)
    grad_encoder = both(genc_own, genc_oth)
    grad_input = both(gin_own, gin_oth)

    first_bit = jnp.where(place == 0, dp_place & 1, (dp_place >> 1) & 1).reshape(1)
    second_bit = jnp.where(place == 0, (dp_place >> 1) & 1, dp_place & 1).reshape(1)
    line_place = (dp_place >> 2).reshape(1)

    def flips(core_zero, core_one):
        return [(2 * d, 2 * (d ^ core_zero)) for d in range(dp_count)] + [
            (2 * d + 1, 2 * (d ^ core_one) + 1) for d in range(dp_count)
        ]

    def travel(array, core_zero, core_one):
        return lax.ppermute(array, ("dp", "seq"), flips(core_zero, core_one))

    def reduce_all(keep, send, outs, unpack, tail=0):
        rows, lanes = keep.shape
        body = rows - tail
        got = lax.ppermute(send, "seq", swap)
        if dp_count != 16:
            (total,) = call(add_all_kernel, (), (keep, got), [((rows, lanes), BF)], name="add_core")
            total = lax.psum(total, "dp")
            mine, other = total[: body // 2], total[body // 2 : body]
            last = total[body:]
            index = jnp.zeros_like(first_bit)
        else:
            shape = (body // 2 + tail, lanes)
            send, keep = call(functools.partial(add_split_kernel, tail), (first_bit,), (keep, got), [(shape, BF)] * 2, limit=16, name="add_core")
            got = travel(send, 1, 2)
            shape = (body // 4 + tail, lanes)
            send, keep = call(functools.partial(add_split_kernel, tail), (second_bit,), (keep, got), [(shape, BF)] * 2, limit=16, name="add_one")
            got = travel(send, 2, 1)
            shape = (body // 16 + tail, lanes)
            pieces = call(functools.partial(add_spread_kernel, tail), (line_place,), (keep, got), [(shape, BF)] * 4, limit=16, name="add_two")
            got = [travel(pieces[j], 4 * j, 4 * j) for j in (1, 2, 3)]
            (own,) = call(add_all_kernel, (), (pieces[0], *got), [(shape, BF)], limit=16, name="add_line")
            last = own[body // 16 :]
            own = own[: body // 16]
            got = [travel(own, 4 * j, 4 * j) for j in (1, 2, 3)]
            (mine,) = call(join_kernel, (line_place,), (own, *got), [((body // 4, lanes), BF)], limit=16, name="join_line")
            got = travel(mine, 2, 1)
            (mine,) = call(join_kernel, (second_bit,), (mine, got), [((body // 2, lanes), BF)], limit=16, name="join_two")
            other = travel(mine, 1, 2)
            index = first_bit
        return call(functools.partial(unpack_kernel, unpack), (index,), (mine, other), [(s, F32) for s in outs], limit=24, name="unpack"), last

    (g_ff_in, g_ff_out), _ = reduce_all(keep_a, send_a, [(width, inner // 2), (inner, half)], unpack_ff)
    (g_cross_out, g_cross_q, g_cross_kv), _ = reduce_all(keep_b, send_b, [(width, half), (width, half), (width, width)], unpack_columns)
    (g_qkv, g_self_out), last = reduce_all(keep_c, send_c, [(width, 3 * half), (width, half)], unpack_columns, tail=16)
    tot_s = last[:, :half].astype(F32)
    return (
        output,
        grad_input,
        grad_encoder,
        g_qkv,
        g_self_out,
        g_cross_q,
        g_cross_kv,
        g_cross_out,
        g_ff_in,
        g_ff_out,
        tot_s[0:3],
        tot_s[3:6],
        tot_s[8:16],
    )


def solution(mesh):
    acts = P(None, "dp", "seq", None)
    lens = P(None, "dp")
    cut = P(None, "seq")
    return jax.shard_map(
        local,
        mesh=mesh,
        in_specs=(acts, acts, acts, lens, lens) + (P(),) * 11,
        out_specs=(acts, acts, acts) + (cut,) * 10,
        check_vma=False,
    )
```

```python
import functools
import math

import jax
import jax.numpy as jnp
from jax import lax
from jax.experimental import pallas as pl
from jax.experimental.pallas import tpu as pltpu
from jax.sharding import PartitionSpec as P

HEADS = 8
NORM_EPS = 1e-05
NEG_FILL = -1e30
BF = jnp.bfloat16
F32 = jnp.float32
MIB = 1 << 20
ORDER = ('a', '', 'b', 'abcabcabcabcabcabcabcc')
ROUTES = (((1, 2), (2, 1), (4, 4), (8, 8)), ((1, 2), (2, 1), (4, 4), (8, 8)), ((1, 2), (2, 1), (4, 4), (8, 8)))
COST = {name: 100_000_000_000 for name in ("forward", "feed_keep", "cross", "cross_grads", "self", "self_grads")}
LANES = 1024


def mm(a, b):
    return lax.dot_general(a, b, (((1,), (0,)), ((), ())), preferred_element_type=F32)


def mm_bt(a, b):
    return lax.dot_general(a, b, (((1,), (1,)), ((), ())), preferred_element_type=F32)


def norm_forward(values, gain, bias):
    center = values - jnp.mean(values, -1, keepdims=True)
    rstd = lax.rsqrt(jnp.mean(center * center, -1, keepdims=True) + NORM_EPS)
    xhat = center * rstd
    return xhat, rstd, xhat * gain + bias


def norm_backward(xhat, rstd, gain, upstream):
    scaled = upstream * gain
    first = jnp.mean(scaled, -1, keepdims=True)
    second = jnp.mean(scaled * xhat, -1, keepdims=True)
    grad = rstd * (scaled - first - xhat * second)
    return grad, jnp.sum(upstream * xhat, 0, keepdims=True), jnp.sum(upstream, 0, keepdims=True)


def lane_half(shape, half):
    lane = lax.broadcasted_iota(jnp.int32, shape, 1)
    return (lane < 64) if half == 0 else (lane >= 64)


def weave(*lists):
    steps = [((i + 0.5) / len(some), k, step) for k, some in enumerate(lists) for i, step in enumerate(some)]
    for _, _, step in sorted(steps, key=lambda item: item[:2]):
        step()


def staged(count, *stages):
    held = {}

    def step(stage, item):
        def run():
            held[item] = stages[stage](item, held.get(item))

        return run

    return [
        step(k, t - k) for t in range(count + len(stages) - 1) for k in range(len(stages)) if 0 <= t - k < count
    ]


def attend_steps(sentence, length, q_ref, k_ref, v_ref, k_at, v_at, bias_ref, p_ref, rl_ref, out_ref, out_t):
    rows = pl.ds(sentence * length, length)

    def score(pair, _):
        queries = q_ref[rows, pair * 128 : pair * 128 + 128]
        keys = k_ref[rows, k_at + pair * 128 : k_at + pair * 128 + 128]
        zeros = jnp.zeros_like(queries)
        return [
            mm_bt(keys, jnp.where(lane_half(queries.shape, half), queries, zeros)) + bias_ref[sentence]
            for half in range(2)
        ]

    def soften(pair, scores):
        probs = []
        for half in range(2):
            top = jnp.max(scores[half], 0, keepdims=True)
            probs.append(jnp.exp(scores[half] - top).astype(BF))
            p_ref[sentence * HEADS + 2 * pair + half] = probs[half]
        return probs

    def mix(pair, probs):
        values_t = v_ref[rows, v_at + pair * 128 : v_at + pair * 128 + 128].T
        mixed = []
        for half in range(2):
            tall = jnp.concatenate([values_t[half * 64 : half * 64 + 64], jnp.ones((16, length), BF)], 0)
            both = mm(tall, probs[half])
            one_over = 1.0 / both[64:65]
            rl_ref[sentence * HEADS + 2 * pair + half] = one_over
            mixed.append(both[0:64] * one_over)
        joined = jnp.concatenate(mixed, 0).astype(BF)
        out_t[pair * 128 : pair * 128 + 128, rows] = joined
        out_ref[rows, pair * 128 : pair * 128 + 128] = joined.T

    return staged(HEADS // 2, score, soften, mix)


def attend_back_steps(
    sentence, length, q_ref, k_ref, v_ref, k_at, v_at, p_ref, rl_ref, out_t, go_t, gq_t, gk_t, gv_t, gk_at, gv_at
):
    rows = pl.ds(sentence * length, length)

    def start(pair, _):
        feats = slice(pair * 128, pair * 128 + 128)
        values = v_ref[rows, v_at + pair * 128 : v_at + pair * 128 + 128]
        mixed = out_t[feats, rows].astype(F32)
        grads = go_t[feats, rows].astype(F32)
        scaled, dots = [], []
        for half in range(2):
            part = slice(half * 64, half * 64 + 64)
            scaled.append((grads[part] * rl_ref[sentence * HEADS + 2 * pair + half]).astype(BF))
            dots.append(jnp.sum(mixed[part] * scaled[half].astype(F32), 0, keepdims=True))
        both = jnp.concatenate(scaled, 0)
        zeros = jnp.zeros_like(values)
        grad_probs = [mm(jnp.where(lane_half(values.shape, half), values, zeros), both) for half in range(2)]
        return scaled, dots, grad_probs

    def middle(pair, held):
        scaled, dots, grad_probs = held
        grad_scores = []
        for half in range(2):
            probs = p_ref[sentence * HEADS + 2 * pair + half].astype(F32)
            grad_scores.append((probs * (grad_probs[half] - dots[half])).astype(BF))
        return scaled, grad_scores

    def finish(pair, held):
        scaled, grad_scores = held
        queries_t = q_ref[rows, pair * 128 : pair * 128 + 128].T
        keys_t = k_ref[rows, k_at + pair * 128 : k_at + pair * 128 + 128].T
        gq, gk, gv = [], [], []
        for half in range(2):
            part = slice(half * 64, half * 64 + 64)
            gq.append(mm(keys_t[part], grad_scores[half]) * 0.125)
            gk.append(mm_bt(queries_t[part], grad_scores[half]))
            gv.append(mm_bt(scaled[half], p_ref[sentence * HEADS + 2 * pair + half]))
        for ref, at, grads in ((gq_t, 0, gq), (gk_t, gk_at, gk), (gv_t, gv_at, gv)):
            ref[at + pair * 128 : at + pair * 128 + 128, rows] = jnp.concatenate(grads, 0).astype(BF)

    return staged(HEADS // 2, start, middle, finish)


class Copies:
    def __init__(self, sems):
        self.sems, self.used, self.open = sems, 0, {}

    def start(self, name, source, target):
        copy = pltpu.make_async_copy(source, target, self.sems.at[self.used])
        self.used += 1
        copy.start()
        self.open.setdefault(name, []).append(copy)

    def wait(self, *names):
        for name in names or tuple(self.open):
            for copy in self.open.pop(name, ()):
                copy.wait()


def halves(place, length):
    half = length // 2
    return [
        [pl.ds(pl.multiple_of(sentence * length + which * half, half), half) for which in (place, 1 - place)]
        for sentence in range(2)
    ]


def feed_grads(which, ref, slow_t, ginner, gff_t, hidden):
    inner, width = hidden.shape[1], slow_t.shape[0]
    half_in, half_out = inner // 2, width // 2

    def give_in(index):
        def run():
            cols = pl.ds(pl.multiple_of(which * half_in + index * 256, 256), 256)
            ref[0:width, index * 256 : (index + 1) * 256] = mm(slow_t[...], ginner[:, cols]).astype(BF)

        return run

    def give_out(index):
        def run():
            feats = pl.ds(pl.multiple_of(which * half_out, half_out), half_out)
            low, at = width + (index // 2) * half_out, (index % 2) * 512
            ref[low : low + half_out, at : at + 512] = mm(
                gff_t[feats, :], hidden[:, index * 512 : (index + 1) * 512]
            ).astype(BF)

        return run

    return [give_out(i) for i in range(inner // 512)] + [give_in(i) for i in range(half_in // 256)]


def feed_keep_kernel(place_ref, gff_t, hidden, slow_t, ginner, keep_ref):
    weave(feed_grads(place_ref[0], keep_ref, slow_t, ginner, gff_t, hidden))


def forward_kernel(numbers_ref, *refs):
    (dec2_in, enc2_in, og2_in, dec_in, enc_in, og_in), refs = refs[:6], refs[6:]
    names = FORWARD_WEIGHTS
    weights_in, refs = refs[: len(names)], refs[len(names) :]
    kept = dict(zip(FORWARD_KEPT, refs))
    (out_own, out_oth, send_ref, gff_t, hidden, slow_t, ginner, gss, elow, qkv, p_self, rl_self, att_t, xhat1, rstd1,
     flow, encs, cq, ckv, p_cross, rl_cross, crossed_t, dnorm_ref) = refs[: len(FORWARD_KEPT) - len(PASSED_WEIGHTS)]
    refs = refs[len(FORWARD_KEPT) :]
    w = {name: kept["w_" + name] for name in PASSED_WEIGHTS}
    w.update(zip([name for name in names if name not in PASSED_WEIGHTS], refs))
    (dec_s, og_s, e_ref, bias_ref, att, fnorm, crossed, xhat2, rstd2, third, slow, slope, gff, outs, sems) = refs[
        len(names) - len(PASSED_WEIGHTS) :
    ]
    copies = Copies(sems)
    place = numbers_ref[0]
    tokens, width = e_ref.shape
    length = tokens // 2
    inner = ginner.shape[1]
    where = halves(place, length)
    for s in range(2):
        copies.start("dec", dec_in.at[place, s], dec_s.at[where[s][0]])
        copies.start("dec", dec2_in.at[place, s], dec_s.at[where[s][1]])
    for name, ref in zip(names[:4], weights_in[:4]):
        copies.start(name, ref, w[name])
    for s in range(2):
        copies.start("enc", enc_in.at[place, s], encs.at[where[s][0]])
        copies.start("enc", enc2_in.at[place, s], encs.at[where[s][1]])
    for name, ref in zip(names[4:], weights_in[4:]):
        copies.start(name, ref, w[name])
    for s in range(2):
        copies.start("og", og_in.at[place, s], og_s.at[where[s][0]])
        copies.start("og", og2_in.at[place, s], og_s.at[where[s][1]])

    rows = [slice(s * length, (s + 1) * length) for s in range(2)]
    keys_at = lax.broadcasted_iota(jnp.int32, (length, length), 0)
    query_at = lax.broadcasted_iota(jnp.int32, (length, length), 1)
    for s in range(2):
        bias_ref[s] = jnp.where((keys_at <= query_at) & (keys_at < numbers_ref[2 + s]), 0.0, NEG_FILL)
        bias_ref[2 + s] = jnp.where(keys_at < numbers_ref[4 + s], 0.0, NEG_FILL)

    def embed(s):
        def run():
            values = dec_s[rows[s]].astype(F32) + row
            e_ref[rows[s]] = values
            elow[rows[s]] = values.astype(BF)

        return run

    def pack(s, part):
        def run():
            cols = slice(part * width, (part + 1) * width)
            values = mm(elow[rows[s]], w["qkv"][:, cols])
            qkv[rows[s], cols] = (values * 0.125 if part == 0 else values).astype(BF)

        return run

    def pack_cross(s, part):
        def run():
            cols = slice(part * width, (part + 1) * width)
            ckv[rows[s], cols] = mm(encs[rows[s]], w["ckv"][:, cols]).astype(BF)

        return run

    held = {}

    def after_self(s):
        def project():
            held["first", s] = e_ref[rows[s]] + mm(att[rows[s]], w["so"][...])

        def norm():
            xhat, rstd, normed = norm_forward(held.pop(("first", s)), gain[0:1], nbias[0:1])
            xhat1[rows[s]] = xhat
            rstd1[rows[s]] = jnp.broadcast_to(rstd, (length, 128))
            fnorm[rows[s]] = normed
            flow[rows[s]] = normed.astype(BF)

        def query():
            cq[rows[s]] = (mm(flow[rows[s]], w["cq"][...]) * 0.125).astype(BF)

        return [project, norm, query]

    def after_cross(s):
        def project():
            held["second", s] = fnorm[rows[s]] + mm(crossed[rows[s]], w["co"][...])

        def norm():
            xhat, rstd, normed = norm_forward(held.pop(("second", s)), gain[1:2], nbias[1:2])
            xhat2[rows[s]] = xhat
            rstd2[rows[s]] = jnp.broadcast_to(rstd, (length, 128))
            third[rows[s]] = normed
            slow[rows[s]] = normed.astype(BF)

        def turn():
            slow_t[:, rows[s]] = slow[rows[s]].T

        return [project, norm, turn]

    step = 256

    def feed(s):
        def grow(index, _):
            return mm(slow[rows[s]], w["fi"][:, index * step : (index + 1) * step])

        def bend(index, v):
            cols = slice(index * step, (index + 1) * step)
            square = v * v
            bent = jnp.tanh(v * (0.7978845608028654 + (0.7978845608028654 * 0.044715) * square))
            half = 0.5 + 0.5 * bent
            hidden[rows[s], cols] = (v * half).astype(BF)
            rise = v * (0.7978845608028654 + (3 * 0.7978845608028654 * 0.044715) * square)
            slope[rows[s], cols] = (half + (0.5 - 0.5 * bent * bent) * rise).astype(BF)

        return staged(inner // step, grow, bend)

    gains = {}

    def after_feed(s):
        def shrink(part):
            def run():
                cols = slice(part * (width // 2), (part + 1) * (width // 2))
                third[rows[s], cols] += mm(hidden[rows[s]], w["fo"][:, cols])

            return run

        def norm():
            xhat, rstd, normed = norm_forward(third[rows[s]], gain[2:3], nbias[2:3])
            outs[rows[s]] = normed.astype(BF)
            grad, *gains[2, s] = norm_backward(xhat, rstd, gain[2:3], og_s[rows[s]].astype(F32))
            third[rows[s]] = grad
            gff[rows[s]] = grad.astype(BF)

        def turn():
            gff_t[:, rows[s]] = gff[rows[s]].T
            out_own[s] = outs[where[s][0], :]
            out_oth[s] = outs[where[s][1], :]

        return [shrink(0), shrink(1), norm, turn]

    def feed_back(s):
        def shrink(index, _):
            return mm_bt(gff[rows[s]], w["fo"][index * step : (index + 1) * step, :]).astype(BF)

        def bend(index, grad_hidden):
            cols = slice(index * step, (index + 1) * step)
            ginner[rows[s], cols] = (grad_hidden.astype(F32) * slope[rows[s], cols].astype(F32)).astype(BF)

        return staged(inner // step, shrink, bend)

    def after_feed_back(s):
        def shrink(part):
            def run():
                cols = slice(part * (width // 2), (part + 1) * (width // 2))
                third[rows[s], cols] += mm_bt(ginner[rows[s]], w["fi"][cols, :])

            return run

        def norm():
            gss[rows[s]], *gains[1, s] = norm_backward(xhat2[rows[s]], rstd2[rows[s], 0:1], gain[1:2], third[rows[s]])

        return [shrink(0), shrink(1), norm]

    copies.wait("table", "gain", "nbias", "dec", "qkv")
    gain = w["gain"][...].astype(F32)
    nbias = w["nbias"][...].astype(F32)
    picked = lax.broadcasted_iota(jnp.int32, w["table"].shape, 0) == numbers_ref[1]
    row = jnp.sum(jnp.where(picked, w["table"][...].astype(F32), 0.0), 0, keepdims=True)
    weave([embed(0)])
    weave([pack(0, part) for part in range(3)], [embed(1)])
    copies.wait("enc", "ckv")
    weave(
        attend_steps(0, length, qkv, qkv, qkv, width, 2 * width, bias_ref, p_self, rl_self, att, att_t),
        [pack(1, part) for part in range(3)] + [pack_cross(0, 0), pack_cross(0, 1)],
    )
    copies.wait("so", "cq", "co")
    weave(
        attend_steps(1, length, qkv, qkv, qkv, width, 2 * width, bias_ref, p_self, rl_self, att, att_t),
        after_self(0) + [pack_cross(1, 0), pack_cross(1, 1)],
    )
    cross_bias = bias_ref.at[2:4]
    weave(
        attend_steps(0, length, cq, ckv, ckv, 0, width, cross_bias, p_cross, rl_cross, crossed, crossed_t),
        after_self(1),
    )
    copies.wait("fi", "fo", "og")
    weave(
        attend_steps(1, length, cq, ckv, ckv, 0, width, cross_bias, p_cross, rl_cross, crossed, crossed_t),
        after_cross(0),
    )
    weave(feed(0), after_cross(1))
    weave(feed(1), after_feed(0))
    weave(feed_back(0), after_feed(1))
    weave(feed_back(1), after_feed_back(0))
    weave(feed_grads(1 - place, send_ref, slow_t, ginner, gff_t, hidden), after_feed_back(1))
    dnorm_ref[...] = jnp.zeros(dnorm_ref.shape, F32)
    for k in (1, 2):
        dnorm_ref[k : k + 1, :] = gains[k, 0][0] + gains[k, 1][0]
        dnorm_ref[3 + k : 4 + k, :] = gains[k, 0][1] + gains[k, 1][1]
    copies.wait()


FORWARD_WEIGHTS = ("table", "qkv", "gain", "nbias", "ckv", "so", "cq", "co", "fi", "fo")
PASSED_WEIGHTS = ("qkv", "gain", "ckv", "so", "cq", "co")
FORWARD_KEPT = (
    "out_own", "out_oth", "send_a", "gff_t", "hidden", "slow_t", "ginner", "gss", "elow", "qkv", "p_self", "rl_self",
    "att_t", "xhat1", "rstd1", "flow", "encs", "cq", "ckv", "p_cross", "rl_cross", "crossed_t", "dnorm",
) + tuple("w_" + name for name in PASSED_WEIGHTS)


def cross_kernel(
    gss, dnorm_in, w_gain, w_co, w_cq, ckv, cq, p_cross, rl_cross, crossed_t, xhat1, rstd1,
    branch, gq_t, gkv_t, gfs, dnorm_ref,
    go_t,
):
    tokens, width = gss.shape
    length = tokens // 2
    rows = [slice(s * length, (s + 1) * length) for s in range(2)]
    gain = w_gain[...].astype(F32)
    gains = {}

    def begin(s):
        def run():
            low = gss[rows[s]].astype(BF)
            branch[rows[s]] = low
            go_t[:, rows[s]] = mm_bt(w_co[...], low).astype(BF)

        return run

    def after(s):
        held = {}

        def query():
            held["first"] = gss[rows[s]] + mm_bt(gq_t[:, rows[s]].T, w_cq[...])

        def norm():
            gfs[rows[s]], *gains[s] = norm_backward(xhat1[rows[s]], rstd1[rows[s], 0:1], gain[0:1], held["first"])

        return [query, norm]

    def attention(s):
        return attend_back_steps(
            s, length, cq, ckv, ckv, 0, width, p_cross, rl_cross, crossed_t, go_t, gq_t, gkv_t, gkv_t, 0, width
        )

    begin(0)()
    weave(attention(0), [begin(1)])
    weave(attention(1), after(0))
    weave(after(1))
    dnorm_ref[...] = dnorm_in[...]
    dnorm_ref[0:1, :] = gains[0][0] + gains[1][0]
    dnorm_ref[3:4, :] = gains[0][1] + gains[1][1]


def give_tall(which, ref, mixed_t, branch):
    width = branch.shape[1]
    half = width // 2
    cols = pl.ds(pl.multiple_of(which * half, half), half)
    grads = mm(mixed_t[...], branch[:, cols]).astype(BF)
    ref[half:width, width : width + half] = grads[0:half]
    ref[half:width, width + half :] = grads[half:]


def cross_grads_kernel(
    place_ref, branch, gq_t, gkv_t, crossed_t, flow, encs, w_ckv, send_ref, keep_ref, genc_own, genc_oth, genc
):
    place = place_ref[0]
    tokens, width = branch.shape
    length = tokens // 2
    half = width // 2
    where = halves(place, length)

    def give(which, ref):
        def out():
            give_tall(which, ref, crossed_t, branch)

        def query():
            feats = pl.ds(pl.multiple_of(which * half, half), half)
            ref[0:half, width:] = mm(gq_t[feats, :], flow[...]).astype(BF)

        def pair():
            feats = pl.ds(pl.multiple_of(which * width, half), width)
            ref[:, 0:width] = mm(gkv_t[feats, :], encs[...]).astype(BF)

        return [out, query, pair]

    def encoder(s):
        def run():
            rows = slice(s * length, (s + 1) * length)
            genc[rows] = mm(w_ckv[...], gkv_t[:, rows]).astype(BF).T
            genc_own[s] = genc[where[s][0], :]
            genc_oth[s] = genc[where[s][1], :]

        return run

    weave(give(1 - place, send_ref) + give(place, keep_ref), [encoder(0), encoder(1)])


def self_kernel(gfs, w_so, qkv, p_self, rl_self, att_t, branch, gqkv_t, go_t):
    tokens, width = gfs.shape
    length = tokens // 2
    rows = [slice(s * length, (s + 1) * length) for s in range(2)]

    def begin(s):
        def run():
            low = gfs[rows[s]].astype(BF)
            branch[rows[s]] = low
            go_t[:, rows[s]] = mm_bt(w_so[...], low).astype(BF)

        return run

    def attention(s):
        return attend_back_steps(
            s, length, qkv, qkv, qkv, width, 2 * width, p_self, rl_self, att_t, go_t, gqkv_t, gqkv_t, gqkv_t,
            width, 2 * width,
        )

    begin(0)()
    weave(attention(0), [begin(1)])
    weave(attention(1))


def self_grads_kernel(
    numbers_ref, gfs, dnorm_in, branch, gqkv_t, att_t, elow, w_qkv,
    send_ref, keep_ref, gin_own, gin_oth,
    gin, small,
):
    place = numbers_ref[0]
    tokens, width = gfs.shape
    length = tokens // 2
    half = width // 2
    where = halves(place, length)
    sums, held = {}, {}

    def give(which, ref):
        def out():
            give_tall(which, ref, att_t, branch)

        def part(index):
            def run():
                feats = pl.ds(pl.multiple_of(which * 3 * half + index * half, half), half)
                low, at = ((0, 0), (half, 0), (0, width))[index]
                ref[low : low + half, at : at + width] = mm(gqkv_t[feats, :], elow[...]).astype(BF)

            return run

        return [out, part(0), part(1), part(2)]

    def back(s):
        rows = slice(s * length, (s + 1) * length)

        def start():
            held[s] = mm(w_qkv[...], gqkv_t[:, rows])

        def finish():
            total = gfs[rows] + held.pop(s).T
            gin[rows] = total.astype(BF)
            sums[s] = jnp.sum(total, 0, keepdims=True)
            gin_own[s] = gin[where[s][0], :]
            gin_oth[s] = gin[where[s][1], :]

        return [start, finish]

    weave(give(1 - place, send_ref) + give(place, keep_ref), back(0) + back(1))
    small[0:8, :] = dnorm_in[...]
    picked = lax.broadcasted_iota(jnp.int32, (8, width), 0) == numbers_ref[1]
    small[8:16, :] = jnp.where(picked, jnp.broadcast_to(sums[0] + sums[1], (8, width)), 0.0)
    for which, ref in ((1 - place, send_ref), (place, keep_ref)):
        ref[width : width + 16, :] = jnp.zeros((16, ref.shape[1]), BF)
        ref[width : width + 16, 0:half] = small[:, pl.ds(pl.multiple_of(which * half, half), half)].astype(BF)


def add_split_kernel(tail, bit_ref, a_ref, b_ref, send_ref, keep_ref):
    half = send_ref.shape[0] - tail
    bit = bit_ref[0]
    for which, ref in ((1 - bit, send_ref), (bit, keep_ref)):
        rows = pl.ds(pl.multiple_of(which * half, 16), half)
        ref[0:half, :] = (a_ref[rows, :].astype(F32) + b_ref[rows, :].astype(F32)).astype(BF)
        if tail:
            last = pl.ds(2 * half, tail)
            ref[half : half + tail, :] = (a_ref[last, :].astype(F32) + b_ref[last, :].astype(F32)).astype(BF)


def add_all_kernel(*refs):
    total = refs[0][...].astype(F32)
    for ref in refs[1:-1]:
        total = total + ref[...].astype(F32)
    refs[-1][...] = total.astype(BF)


def join_kernel(index_ref, *refs):
    out = refs[-1]
    rows = refs[0].shape[0]
    for j, ref in enumerate(refs[:-1]):
        out[pl.ds(pl.multiple_of((index_ref[0] ^ j) * rows, 16), rows), :] = ref[...]


def unpack_kernel(unpack, index_ref, mine_ref, got_ref, *outs):
    @pl.when(index_ref[0] == 0)
    def _():
        unpack(mine_ref, got_ref, *outs)

    @pl.when(index_ref[0] != 0)
    def _():
        unpack(got_ref, mine_ref, *outs)


def unpack_ff(low_ref, high_ref, in_ref, out_ref):
    in_ref[...] = low_ref[...].astype(F32)
    half = out_ref.shape[1]
    for j in range(2):
        tall = low_ref.shape[1]
        out_ref[j * tall : (j + 1) * tall, :] = high_ref[j * half : (j + 1) * half, :].T.astype(F32)


def unpack_tall(low_ref, high_ref, out_ref):
    half = out_ref.shape[1]
    width = 2 * half
    out_ref[0:half, :] = high_ref[:, width : width + half].astype(F32)
    out_ref[half:width, :] = high_ref[:, width + half :].astype(F32)


def unpack_cross(low_ref, high_ref, kv_ref, query_ref, out_ref):
    half, width = low_ref.shape[0], query_ref.shape[0]
    kv_ref[:, 0:half] = low_ref[:, 0:width].T.astype(F32)
    kv_ref[:, half:] = high_ref[:, 0:width].T.astype(F32)
    query_ref[...] = low_ref[:, width:].T.astype(F32)
    unpack_tall(low_ref, high_ref, out_ref)


def unpack_self(low_ref, high_ref, qkv_ref, out_ref):
    half, width = low_ref.shape[0], qkv_ref.shape[0]
    qkv_ref[:, 0:half] = low_ref[:, 0:width].T.astype(F32)
    qkv_ref[:, half:width] = high_ref[:, 0:width].T.astype(F32)
    qkv_ref[:, width:] = low_ref[:, width:].T.astype(F32)
    unpack_tall(low_ref, high_ref, out_ref)


def smem():
    return pl.BlockSpec(memory_space=pltpu.SMEM)


def vmem():
    return pl.BlockSpec(memory_space=pltpu.VMEM)


def call(kernel, scalars, arrays, outs, scratch=(), name=None, far=(), results=(), sems=0, after=()):
    held = [*results, *scratch]
    limit = sum(math.prod(s[:-2]) * -(-s[-2] // 16) * 16 * s[-1] * jnp.dtype(d).itemsize for s, d in held) + 4 * MIB
    taken = len(scalars) + len(arrays) + len(far)
    anywhere = pl.BlockSpec(memory_space=pl.ANY)

    def body(*refs):
        kernel(*refs[:taken], *refs[taken + len(after) :])

    return pl.pallas_call(
        body,
        out_shape=tuple(pltpu.VMEM(s, d) for s, d in outs) + tuple(jax.ShapeDtypeStruct(s, d) for s, d in results),
        in_specs=[smem() for _ in scalars]
        + [vmem() for _ in arrays]
        + [pl.BlockSpec(memory_space=pltpu.HBM) for _ in far]
        + [anywhere for _ in after],
        out_specs=tuple(vmem() for _ in (*outs, *results)),
        scratch_shapes=[pltpu.VMEM(s, d) for s, d in scratch] + ([pltpu.SemaphoreType.DMA((sems,))] if sems else []),
        compiler_params=pltpu.CompilerParams(vmem_limit_bytes=limit),
        cost_estimate=pl.CostEstimate(flops=COST.get(name, 1000), bytes_accessed=1000, transcendentals=0),
        name=name,
    )(
        *scalars,
        *(pltpu.with_memory_space_constraint(a, pltpu.VMEM) for a in arrays),
        *(pltpu.with_memory_space_constraint(a, pltpu.HBM) for a in far),
        *after,
    )


def local(
    dec_in, enc_out, out_grad, tgt_len, src_len, pair_id,
    self_qkv, self_out, cross_q, cross_kv, cross_out, ff_in, ff_out, norm_gain, norm_bias, lang_table,
):
    micro_count, sent_count, local_len, width = dec_in.shape
    seq_count = lax.axis_size("seq")
    dp_count = lax.axis_size("dp")
    place = lax.axis_index("seq")
    dp_place = lax.axis_index("dp")
    inner = ff_in.shape[1]
    length = local_len * seq_count
    tokens = sent_count * length
    half = width // 2
    mine = jnp.arange(micro_count) == place
    numbers = jnp.concatenate(
        [
            place.reshape(1),
            jnp.sum(jnp.where(mine, pair_id, 0)).reshape(1),
            jnp.sum(jnp.where(mine[:, None], tgt_len, 0), 0),
            jnp.sum(jnp.where(mine[:, None], src_len, 0), 0),
        ]
    ).astype(jnp.int32)
    swap = [(0, 1), (1, 0)]

    dec2 = lax.ppermute(dec_in, "seq", swap)
    enc2 = lax.ppermute(enc_out, "seq", swap)
    og2 = lax.ppermute(out_grad, "seq", swap)

    rows = (sent_count, local_len, width)
    whole = (tokens, width)
    probs = (sent_count * HEADS, length, length)
    sums = (sent_count * HEADS, 1, length)
    turned = (width, tokens)
    kinds = {
        "out_own": (rows, BF), "out_oth": (rows, BF), "send_a": ((2 * width, LANES), BF), "gff_t": (turned, BF),
        "hidden": ((tokens, inner), BF), "slow_t": (turned, BF), "ginner": ((tokens, inner), BF), "gss": (whole, F32),
        "elow": (whole, BF), "qkv": ((tokens, 3 * width), BF), "p_self": (probs, BF), "rl_self": (sums, F32),
        "att_t": (turned, BF), "xhat1": (whole, F32), "rstd1": ((tokens, 128), F32), "flow": (whole, BF),
        "encs": (whole, BF), "cq": (whole, BF), "ckv": ((tokens, 2 * width), BF), "p_cross": (probs, BF),
        "rl_cross": (sums, F32), "crossed_t": (turned, BF), "dnorm": ((8, width), F32),
    }
    params = {
        "qkv": self_qkv, "so": self_out, "cq": cross_q, "ckv": cross_kv, "co": cross_out, "fi": ff_in, "fo": ff_out,
        "gain": norm_gain, "nbias": norm_bias, "table": lang_table,
    }
    kinds.update({"w_" + name: (weight.shape, weight.dtype) for name, weight in params.items()})
    kept = call(
        forward_kernel,
        (numbers,),
        (dec2, enc2, og2),
        [kinds[name] for name in FORWARD_KEPT],
        [kinds["w_" + name] for name in FORWARD_WEIGHTS if name not in PASSED_WEIGHTS]
        + [
            (whole, BF), (whole, BF), (whole, F32), ((4, length, length), F32), (whole, BF), (whole, F32), (whole, BF),
            (whole, F32), ((tokens, 128), F32), (whole, F32), (whole, BF), ((tokens, inner), BF), (whole, BF), (whole, BF),
        ],
        name="forward",
        far=(dec_in, enc_out, out_grad, *(params[name] for name in FORWARD_WEIGHTS)),
        sems=32,
    )
    held = dict(zip(FORWARD_KEPT, kept))

    def of(*names):
        return [held[name] for name in names]

    def flips(core_zero, core_one):
        return [(2 * d, 2 * (d ^ core_zero)) for d in range(dp_count)] + [
            (2 * d + 1, 2 * (d ^ core_one) + 1) for d in range(dp_count)
        ]

    def travel(array, core_zero, core_one):
        return lax.ppermute(array, ("dp", "seq"), flips(core_zero, core_one))

    last = []

    def go_on(*groups):
        result = None
        for group in groups:
            result = next(group)
        return result

    def reduce_all(keep, send, outs, unpack, route, tail=0):
        def run(kernel, scalars, arrays, outs, name, results=()):
            got = call(kernel, scalars, arrays, outs, name=name, results=results, after=tuple(last))
            last[:] = [got[0]]
            return got

        rows, lanes = keep.shape
        body = rows - tail
        got = lax.ppermute(send, "seq", swap)
        if dp_count != 16:
            (total,) = run(add_all_kernel, (), (keep, got), [((rows, lanes), BF)], "add_core")
            total = lax.psum(total, "dp")
            mine, other, rest = total[: body // 2], total[body // 2 : body], total[body:]
            bit = jnp.zeros((1,), jnp.int32)
            for _ in range(2 * len(route)):
                yield
        else:
            bits = [
                (jnp.where(place == 0, dp_place & zero, dp_place & one) != 0).astype(jnp.int32).reshape(1)
                for zero, one in route
            ]
            held = body
            for bit, flip in zip(bits, route):
                held //= 2
                shape = (held + tail, lanes)
                send, keep = run(functools.partial(add_split_kernel, tail), (bit,), (keep, got), [(shape, BF)] * 2, "add_split")
                got = travel(send, *flip)
                yield
            (mine,) = run(add_all_kernel, (), (keep, got), [(shape, BF)], "add_last")
            mine, rest = mine[:held], mine[held:]
            for bit, flip in zip(bits[:0:-1], route[:0:-1]):
                other = travel(mine, *flip)
                yield
                held *= 2
                (mine,) = run(join_kernel, (bit,), (mine, other), [((held, lanes), BF)], "join")
            other = travel(mine, *route[0])
            bit = bits[0]
            yield
        unpacked = run(
            functools.partial(unpack_kernel, unpack), (bit,), (mine, other), [], "unpack", [(s, F32) for s in outs]
        )
        yield unpacked, rest

    groups = {}

    def go_through(letters):
        go_on(*(groups[letter] for letter in letters))

    (keep_a,) = call(
        feed_keep_kernel,
        (numbers,),
        of("gff_t", "hidden", "slow_t", "ginner"),
        [((2 * width, LANES), BF)],
        name="feed_keep",
    )
    groups["a"] = reduce_all(keep_a, held["send_a"], [(width, inner // 2), (inner, half)], unpack_ff, ROUTES[0])
    branch, gq_t, gkv_t, gfs, dnorm = call(
        cross_kernel,
        (),
        of("gss", "dnorm", "w_gain", "w_co", "w_cq", "ckv", "cq", "p_cross", "rl_cross", "crossed_t", "xhat1", "rstd1"),
        [(whole, BF), (turned, BF), ((2 * width, tokens), BF), (whole, F32), ((8, width), F32)],
        [(turned, BF)],
        name="cross",
        after=[keep_a],
    )
    go_through(ORDER[0])
    buffer = ((width, LANES), BF)
    send_b, keep_b, genc_own, genc_oth = call(
        cross_grads_kernel,
        (numbers,),
        [branch, gq_t, gkv_t, *of("crossed_t", "flow", "encs", "w_ckv")],
        [buffer, buffer, (rows, BF), (rows, BF)],
        [(whole, BF)],
        name="cross_grads",
        after=last,
    )
    groups["b"] = reduce_all(
        keep_b, send_b, [(width, width), (width, half), (width, half)], unpack_cross, ROUTES[1]
    )
    go_through(ORDER[1])
    branch, gqkv_t = call(
        self_kernel,
        (),
        [gfs, *of("w_so", "qkv", "p_self", "rl_self", "att_t")],
        [(whole, BF), ((3 * width, tokens), BF)],
        [(turned, BF)],
        name="self",
        after=last,
    )
    go_through(ORDER[2])
    buffer = ((width + 16, LANES), BF)
    send_c, keep_c, gin_own, gin_oth = call(
        self_grads_kernel,
        (numbers,),
        [gfs, dnorm, branch, gqkv_t, *of("att_t", "elow", "w_qkv")],
        [buffer, buffer, (rows, BF), (rows, BF)],
        [(whole, BF), ((16, width), F32)],
        name="self_grads",
        after=last,
    )
    groups["c"] = reduce_all(
        keep_c, send_c, [(width, 3 * half), (width, half)], unpack_self, ROUTES[2], tail=16
    )
    last[:] = [send_c]
    go_through(ORDER[3])
    (g_ff_in, g_ff_out), _ = go_on(groups["a"])
    (g_cross_kv, g_cross_q, g_cross_out), _ = go_on(groups["b"])
    (g_qkv, g_self_out), tot_s = go_on(groups["c"])
    tot_s = tot_s[:, :half].astype(F32)
    def both(own, other):
        got = lax.ppermute(other, "seq", swap)
        return jnp.where(place == 0, jnp.stack([own, got]), jnp.stack([got, own]))

    output = both(*of("out_own", "out_oth"))
    grad_encoder = both(genc_own, genc_oth)
    grad_input = both(gin_own, gin_oth)

    return (
        output,
        grad_input,
        grad_encoder,
        g_qkv,
        g_self_out,
        g_cross_q,
        g_cross_kv,
        g_cross_out,
        g_ff_in,
        g_ff_out,
        tot_s[0:3],
        tot_s[3:6],
        tot_s[8:16],
    )


def solution(mesh):
    acts = P(None, "dp", "seq", None)
    lens = P(None, "dp")
    cut = P(None, "seq")
    return jax.shard_map(
        local,
        mesh=mesh,
        in_specs=(acts, acts, acts, lens, lens) + (P(),) * 11,
        out_specs=(acts, acts, acts) + (cut,) * 10,
        check_vma=False,
    )
```

```python
import functools
import math

import jax
import jax.numpy as jnp
from jax import lax
from jax.experimental import pallas as pl
from jax.experimental.pallas import tpu as pltpu
from jax.sharding import PartitionSpec as P

HEADS = 8
NORM_EPS = 1e-05
NEG_FILL = -1e30
BF = jnp.bfloat16
F32 = jnp.float32
MIB = 1 << 20
ORDER = "XFfGSFxTfFsxFfsPxFsfxsFfxsFfxsFxfsxfFsxsf"
PLANE_FIRST = ((1, 2), (2, 1), (4, 4), (8, 8))
BETWEEN = ((1, 2), (4, 4), (2, 1), (8, 8))
LINE_FIRST = ((4, 4), (1, 2), (2, 1), (8, 8))
ROUTES = {"f": ((4, 4), (1, 2), (8, 8), (2, 1)), "F": PLANE_FIRST, "x": BETWEEN, "s": PLANE_FIRST}
SMALL_COST = {"flops": 20_000_000_000, "bytes_accessed": 400_000_000}
COST = {
    name: {"flops": 100_000_000_000, "bytes_accessed": 1000}
    for name in ("forward", "feed_keep", "cross", "cross_grads", "self", "self_grads")
}
LANES = 1024


def mm(a, b):
    return lax.dot_general(a, b, (((1,), (0,)), ((), ())), preferred_element_type=F32)


def mm_bt(a, b):
    return lax.dot_general(a, b, (((1,), (1,)), ((), ())), preferred_element_type=F32)


def norm_forward(values, gain, bias):
    center = values - jnp.mean(values, -1, keepdims=True)
    rstd = lax.rsqrt(jnp.mean(center * center, -1, keepdims=True) + NORM_EPS)
    xhat = center * rstd
    return xhat, rstd, xhat * gain + bias


def norm_backward(xhat, rstd, gain, upstream):
    scaled = upstream * gain
    first = jnp.mean(scaled, -1, keepdims=True)
    second = jnp.mean(scaled * xhat, -1, keepdims=True)
    grad = rstd * (scaled - first - xhat * second)
    return grad, jnp.sum(upstream * xhat, 0, keepdims=True), jnp.sum(upstream, 0, keepdims=True)


def lane_half(shape, half):
    lane = lax.broadcasted_iota(jnp.int32, shape, 1)
    return (lane < 64) if half == 0 else (lane >= 64)


def weave(*lists):
    steps = [((i + 0.5) / len(some), k, step) for k, some in enumerate(lists) for i, step in enumerate(some)]
    for _, _, step in sorted(steps, key=lambda item: item[:2]):
        step()


def staged(count, *stages):
    held = {}

    def step(stage, item):
        def run():
            held[item] = stages[stage](item, held.get(item))

        return run

    return [
        step(k, t - k) for t in range(count + len(stages) - 1) for k in range(len(stages)) if 0 <= t - k < count
    ]


def attend_steps(sentence, length, q_ref, k_ref, v_ref, k_at, v_at, bias_ref, p_ref, rl_ref, out_ref, out_t):
    rows = pl.ds(sentence * length, length)

    def score(pair, _):
        queries = q_ref[rows, pair * 128 : pair * 128 + 128]
        keys = k_ref[rows, k_at + pair * 128 : k_at + pair * 128 + 128]
        zeros = jnp.zeros_like(queries)
        return [
            mm_bt(keys, jnp.where(lane_half(queries.shape, half), queries, zeros)) + bias_ref[sentence]
            for half in range(2)
        ]

    def soften(pair, scores):
        probs = []
        for half in range(2):
            top = jnp.max(scores[half], 0, keepdims=True)
            probs.append(jnp.exp(scores[half] - top).astype(BF))
            p_ref[sentence * HEADS + 2 * pair + half] = probs[half]
        return probs

    def mix(pair, probs):
        values_t = v_ref[rows, v_at + pair * 128 : v_at + pair * 128 + 128].T
        mixed = []
        for half in range(2):
            tall = jnp.concatenate([values_t[half * 64 : half * 64 + 64], jnp.ones((16, length), BF)], 0)
            both = mm(tall, probs[half])
            one_over = 1.0 / both[64:65]
            rl_ref[sentence * HEADS + 2 * pair + half] = one_over
            mixed.append(both[0:64] * one_over)
        joined = jnp.concatenate(mixed, 0).astype(BF)
        out_t[pair * 128 : pair * 128 + 128, rows] = joined
        out_ref[rows, pair * 128 : pair * 128 + 128] = joined.T

    return staged(HEADS // 2, score, soften, mix)


def attend_back_steps(
    sentence, length, q_ref, k_ref, v_ref, k_at, v_at, p_ref, rl_ref, out_t, go_t, gq_t, gk_t, gv_t, gk_at, gv_at
):
    rows = pl.ds(sentence * length, length)

    def start(pair, _):
        feats = slice(pair * 128, pair * 128 + 128)
        values = v_ref[rows, v_at + pair * 128 : v_at + pair * 128 + 128]
        mixed = out_t[feats, rows].astype(F32)
        grads = go_t[feats, rows].astype(F32)
        scaled, dots = [], []
        for half in range(2):
            part = slice(half * 64, half * 64 + 64)
            scaled.append((grads[part] * rl_ref[sentence * HEADS + 2 * pair + half]).astype(BF))
            dots.append(jnp.sum(mixed[part] * scaled[half].astype(F32), 0, keepdims=True))
        both = jnp.concatenate(scaled, 0)
        zeros = jnp.zeros_like(values)
        grad_probs = [mm(jnp.where(lane_half(values.shape, half), values, zeros), both) for half in range(2)]
        return scaled, dots, grad_probs

    def middle(pair, held):
        scaled, dots, grad_probs = held
        grad_scores = []
        for half in range(2):
            probs = p_ref[sentence * HEADS + 2 * pair + half].astype(F32)
            grad_scores.append((probs * (grad_probs[half] - dots[half])).astype(BF))
        return scaled, grad_scores

    def finish(pair, held):
        scaled, grad_scores = held
        queries_t = q_ref[rows, pair * 128 : pair * 128 + 128].T
        keys_t = k_ref[rows, k_at + pair * 128 : k_at + pair * 128 + 128].T
        gq, gk, gv = [], [], []
        for half in range(2):
            part = slice(half * 64, half * 64 + 64)
            gq.append(mm(keys_t[part], grad_scores[half]) * 0.125)
            gk.append(mm_bt(queries_t[part], grad_scores[half]))
            gv.append(mm_bt(scaled[half], p_ref[sentence * HEADS + 2 * pair + half]))
        for ref, at, grads in ((gq_t, 0, gq), (gk_t, gk_at, gk), (gv_t, gv_at, gv)):
            ref[at + pair * 128 : at + pair * 128 + 128, rows] = jnp.concatenate(grads, 0).astype(BF)

    return staged(HEADS // 2, start, middle, finish)


class Copies:
    def __init__(self, sems):
        self.sems, self.used, self.open = sems, 0, {}

    def start(self, name, source, target):
        copy = pltpu.make_async_copy(source, target, self.sems.at[self.used])
        self.used += 1
        copy.start()
        self.open.setdefault(name, []).append(copy)

    def wait(self, *names):
        for name in names or tuple(self.open):
            for copy in self.open.pop(name, ()):
                copy.wait()


def halves(place, length):
    half = length // 2
    return [
        [pl.ds(pl.multiple_of(sentence * length + which * half, half), half) for which in (place, 1 - place)]
        for sentence in range(2)
    ]


def feed_grads(which, in_ref, out_ref, slow_t, ginner, gff_t, hidden):
    inner, width = hidden.shape[1], slow_t.shape[0]
    half_in, half_out = inner // 2, width // 2

    def give_in(index):
        def run():
            cols = pl.ds(pl.multiple_of(which * half_in + index * 256, 256), 256)
            in_ref[:, index * 256 : (index + 1) * 256] = mm(slow_t[...], ginner[:, cols]).astype(BF)

        return run

    def give_out(index):
        def run():
            feats = pl.ds(pl.multiple_of(which * half_out, half_out), half_out)
            low, at = (index // 2) * half_out, (index % 2) * 512
            out_ref[low : low + half_out, at : at + 512] = mm(
                gff_t[feats, :], hidden[:, index * 512 : (index + 1) * 512]
            ).astype(BF)

        return run

    return [give_out(i) for i in range(inner // 512)] + [give_in(i) for i in range(half_in // 256)]


def feed_keep_kernel(numbers_ref, gff_t, hidden, slow_t, ginner, in_ref, out_ref):
    weave(feed_grads(numbers_ref[0], in_ref, out_ref, slow_t, ginner, gff_t, hidden))


def forward_kernel(numbers_ref, *refs):
    (dec2_in, enc2_in, og2_in, dec_in, enc_in, og_in), refs = refs[:6], refs[6:]
    names = FORWARD_WEIGHTS
    weights_in, refs = refs[: len(names)], refs[len(names) :]
    kept = dict(zip(FORWARD_KEPT, refs))
    (out_own, out_oth, send_in, send_out, gff_t, hidden, slow_t, ginner, gss, elow, qkv, p_self, rl_self, att_t, xhat1, rstd1,
     flow, encs, cq, ckv, p_cross, rl_cross, crossed_t, dnorm_ref) = refs[: len(FORWARD_KEPT) - len(PASSED_WEIGHTS)]
    refs = refs[len(FORWARD_KEPT) :]
    w = {name: kept["w_" + name] for name in PASSED_WEIGHTS}
    w.update(zip([name for name in names if name not in PASSED_WEIGHTS], refs))
    (dec_s, og_s, e_ref, bias_ref, att, fnorm, crossed, xhat2, rstd2, third, slow, slope, gff, outs, sems) = refs[
        len(names) - len(PASSED_WEIGHTS) :
    ]
    copies = Copies(sems)
    place = numbers_ref[0]
    tokens, width = e_ref.shape
    length = tokens // 2
    inner = ginner.shape[1]
    where = halves(place, length)
    for s in range(2):
        copies.start("dec", dec_in.at[place, s], dec_s.at[where[s][0]])
        copies.start("dec", dec2_in.at[place, s], dec_s.at[where[s][1]])
    for name, ref in zip(names[:4], weights_in[:4]):
        copies.start(name, ref, w[name])
    for s in range(2):
        copies.start("enc", enc_in.at[place, s], encs.at[where[s][0]])
        copies.start("enc", enc2_in.at[place, s], encs.at[where[s][1]])
    for name, ref in zip(names[4:], weights_in[4:]):
        copies.start(name, ref, w[name])
    for s in range(2):
        copies.start("og", og_in.at[place, s], og_s.at[where[s][0]])
        copies.start("og", og2_in.at[place, s], og_s.at[where[s][1]])

    rows = [slice(s * length, (s + 1) * length) for s in range(2)]
    keys_at = lax.broadcasted_iota(jnp.int32, (length, length), 0)
    query_at = lax.broadcasted_iota(jnp.int32, (length, length), 1)
    for s in range(2):
        bias_ref[s] = jnp.where((keys_at <= query_at) & (keys_at < numbers_ref[2 + s]), 0.0, NEG_FILL)
        bias_ref[2 + s] = jnp.where(keys_at < numbers_ref[4 + s], 0.0, NEG_FILL)

    def embed(s):
        def run():
            values = dec_s[rows[s]].astype(F32) + row
            e_ref[rows[s]] = values
            elow[rows[s]] = values.astype(BF)

        return run

    def pack(s, part):
        def run():
            cols = slice(part * width, (part + 1) * width)
            values = mm(elow[rows[s]], w["qkv"][:, cols])
            qkv[rows[s], cols] = (values * 0.125 if part == 0 else values).astype(BF)

        return run

    def pack_cross(s, part):
        def run():
            cols = slice(part * width, (part + 1) * width)
            ckv[rows[s], cols] = mm(encs[rows[s]], w["ckv"][:, cols]).astype(BF)

        return run

    held = {}

    def after_self(s):
        def project():
            held["first", s] = e_ref[rows[s]] + mm(att[rows[s]], w["so"][...])

        def norm():
            xhat, rstd, normed = norm_forward(held.pop(("first", s)), gain[0:1], nbias[0:1])
            xhat1[rows[s]] = xhat
            rstd1[rows[s]] = jnp.broadcast_to(rstd, (length, 128))
            fnorm[rows[s]] = normed
            flow[rows[s]] = normed.astype(BF)

        def query():
            cq[rows[s]] = (mm(flow[rows[s]], w["cq"][...]) * 0.125).astype(BF)

        return [project, norm, query]

    def after_cross(s):
        def project():
            held["second", s] = fnorm[rows[s]] + mm(crossed[rows[s]], w["co"][...])

        def norm():
            xhat, rstd, normed = norm_forward(held.pop(("second", s)), gain[1:2], nbias[1:2])
            xhat2[rows[s]] = xhat
            rstd2[rows[s]] = jnp.broadcast_to(rstd, (length, 128))
            third[rows[s]] = normed
            slow[rows[s]] = normed.astype(BF)

        def turn():
            slow_t[:, rows[s]] = slow[rows[s]].T

        return [project, norm, turn]

    step = 256

    def feed(s):
        def grow(index, _):
            return mm(slow[rows[s]], w["fi"][:, index * step : (index + 1) * step])

        def bend(index, v):
            cols = slice(index * step, (index + 1) * step)
            square = v * v
            bent = jnp.tanh(v * (0.7978845608028654 + (0.7978845608028654 * 0.044715) * square))
            half = 0.5 + 0.5 * bent
            hidden[rows[s], cols] = (v * half).astype(BF)
            rise = v * (0.7978845608028654 + (3 * 0.7978845608028654 * 0.044715) * square)
            slope[rows[s], cols] = (half + (0.5 - 0.5 * bent * bent) * rise).astype(BF)

        return staged(inner // step, grow, bend)

    gains = {}

    def after_feed(s):
        def shrink(part):
            def run():
                cols = slice(part * (width // 2), (part + 1) * (width // 2))
                third[rows[s], cols] += mm(hidden[rows[s]], w["fo"][:, cols])

            return run

        def norm():
            xhat, rstd, normed = norm_forward(third[rows[s]], gain[2:3], nbias[2:3])
            outs[rows[s]] = normed.astype(BF)
            grad, *gains[2, s] = norm_backward(xhat, rstd, gain[2:3], og_s[rows[s]].astype(F32))
            third[rows[s]] = grad
            gff[rows[s]] = grad.astype(BF)

        def turn():
            gff_t[:, rows[s]] = gff[rows[s]].T
            out_own[s] = outs[where[s][0], :]
            out_oth[:, s * width : (s + 1) * width] = outs[where[s][1], :]

        return [shrink(0), shrink(1), norm, turn]

    def feed_back(s):
        def shrink(index, _):
            return mm_bt(gff[rows[s]], w["fo"][index * step : (index + 1) * step, :]).astype(BF)

        def bend(index, grad_hidden):
            cols = slice(index * step, (index + 1) * step)
            ginner[rows[s], cols] = (grad_hidden.astype(F32) * slope[rows[s], cols].astype(F32)).astype(BF)

        return staged(inner // step, shrink, bend)

    def after_feed_back(s):
        def shrink(part):
            def run():
                cols = slice(part * (width // 2), (part + 1) * (width // 2))
                third[rows[s], cols] += mm_bt(ginner[rows[s]], w["fi"][cols, :])

            return run

        def norm():
            gss[rows[s]], *gains[1, s] = norm_backward(xhat2[rows[s]], rstd2[rows[s], 0:1], gain[1:2], third[rows[s]])

        return [shrink(0), shrink(1), norm]

    copies.wait("table", "gain", "nbias", "dec", "qkv")
    gain = w["gain"][...].astype(F32)
    nbias = w["nbias"][...].astype(F32)
    picked = lax.broadcasted_iota(jnp.int32, w["table"].shape, 0) == numbers_ref[1]
    row = jnp.sum(jnp.where(picked, w["table"][...].astype(F32), 0.0), 0, keepdims=True)
    weave([embed(0)])
    weave([pack(0, part) for part in range(3)], [embed(1)])
    copies.wait("enc", "ckv")
    weave(
        attend_steps(0, length, qkv, qkv, qkv, width, 2 * width, bias_ref, p_self, rl_self, att, att_t),
        [pack(1, part) for part in range(3)] + [pack_cross(0, 0), pack_cross(0, 1)],
    )
    copies.wait("so", "cq", "co")
    weave(
        attend_steps(1, length, qkv, qkv, qkv, width, 2 * width, bias_ref, p_self, rl_self, att, att_t),
        after_self(0) + [pack_cross(1, 0), pack_cross(1, 1)],
    )
    cross_bias = bias_ref.at[2:4]
    weave(
        attend_steps(0, length, cq, ckv, ckv, 0, width, cross_bias, p_cross, rl_cross, crossed, crossed_t),
        after_self(1),
    )
    copies.wait("fi", "fo", "og")
    weave(
        attend_steps(1, length, cq, ckv, ckv, 0, width, cross_bias, p_cross, rl_cross, crossed, crossed_t),
        after_cross(0),
    )
    weave(feed(0), after_cross(1))
    weave(feed(1), after_feed(0))
    weave(feed_back(0), after_feed(1))
    weave(feed_back(1), after_feed_back(0))
    weave(feed_grads(1 - place, send_in, send_out, slow_t, ginner, gff_t, hidden), after_feed_back(1))
    dnorm_ref[...] = jnp.zeros(dnorm_ref.shape, F32)
    for k in (1, 2):
        dnorm_ref[k : k + 1, :] = gains[k, 0][0] + gains[k, 1][0]
        dnorm_ref[3 + k : 4 + k, :] = gains[k, 0][1] + gains[k, 1][1]
    copies.wait()


FORWARD_WEIGHTS = ("table", "qkv", "gain", "nbias", "ckv", "so", "cq", "co", "fi", "fo")
PASSED_WEIGHTS = ("qkv", "gain", "ckv", "so", "cq", "co")
FORWARD_KEPT = (
    "out_own", "out_oth", "send_in", "send_out", "gff_t", "hidden", "slow_t", "ginner", "gss", "elow", "qkv", "p_self", "rl_self",
    "att_t", "xhat1", "rstd1", "flow", "encs", "cq", "ckv", "p_cross", "rl_cross", "crossed_t", "dnorm",
) + tuple("w_" + name for name in PASSED_WEIGHTS)


def cross_kernel(
    gss, dnorm_in, w_gain, w_co, w_cq, ckv, cq, p_cross, rl_cross, crossed_t, xhat1, rstd1,
    branch, gq_t, gkv_t, gfs, dnorm_ref,
    go_t,
):
    tokens, width = gss.shape
    length = tokens // 2
    rows = [slice(s * length, (s + 1) * length) for s in range(2)]
    gain = w_gain[...].astype(F32)
    gains = {}

    def begin(s):
        def run():
            low = gss[rows[s]].astype(BF)
            branch[rows[s]] = low
            go_t[:, rows[s]] = mm_bt(w_co[...], low).astype(BF)

        return run

    def after(s):
        held = {}

        def query():
            held["first"] = gss[rows[s]] + mm_bt(gq_t[:, rows[s]].T, w_cq[...])

        def norm():
            gfs[rows[s]], *gains[s] = norm_backward(xhat1[rows[s]], rstd1[rows[s], 0:1], gain[0:1], held["first"])

        return [query, norm]

    def attention(s):
        return attend_back_steps(
            s, length, cq, ckv, ckv, 0, width, p_cross, rl_cross, crossed_t, go_t, gq_t, gkv_t, gkv_t, 0, width
        )

    begin(0)()
    weave(attention(0), [begin(1)])
    weave(attention(1), after(0))
    weave(after(1))
    dnorm_ref[...] = dnorm_in[...]
    dnorm_ref[0:1, :] = gains[0][0] + gains[1][0]
    dnorm_ref[3:4, :] = gains[0][1] + gains[1][1]


def give_tall(which, ref, mixed_t, branch):
    width = branch.shape[1]
    half = width // 2
    cols = pl.ds(pl.multiple_of(which * half, half), half)
    grads = mm(mixed_t[...], branch[:, cols]).astype(BF)
    ref[half:width, width : width + half] = grads[0:half]
    ref[half:width, width + half :] = grads[half:]


def cross_grads_kernel(
    numbers_ref, branch, gq_t, gkv_t, crossed_t, flow, encs, w_ckv, out_oth, send_ref, keep_ref, genc_own, genc
):
    place = numbers_ref[0]
    tokens, width = branch.shape
    length = tokens // 2
    half = width // 2
    where = halves(place, length)

    def give(which, ref):
        def out():
            give_tall(which, ref, crossed_t, branch)

        def query():
            feats = pl.ds(pl.multiple_of(which * half, half), half)
            ref[0:half, width:] = mm(gq_t[feats, :], flow[...]).astype(BF)

        def pair():
            feats = pl.ds(pl.multiple_of(which * width, half), width)
            ref[0:width, 0:width] = mm(gkv_t[feats, :], encs[...]).astype(BF)

        return [out, query, pair]

    def encoder(s):
        def run():
            rows = slice(s * length, (s + 1) * length)
            genc[rows] = mm(w_ckv[...], gkv_t[:, rows]).astype(BF).T
            genc_own[s] = genc[where[s][0], :]
            send_ref[width : width + length // 2, s * width : (s + 1) * width] = genc[where[s][1], :]

        return run

    weave(give(1 - place, send_ref) + give(place, keep_ref), [encoder(0), encoder(1)])
    send_ref[width + length // 2 :, :] = out_oth[...]


def self_kernel(gfs, w_so, qkv, p_self, rl_self, att_t, branch, gqkv_t, go_t):
    tokens, width = gfs.shape
    length = tokens // 2
    rows = [slice(s * length, (s + 1) * length) for s in range(2)]

    def begin(s):
        def run():
            low = gfs[rows[s]].astype(BF)
            branch[rows[s]] = low
            go_t[:, rows[s]] = mm_bt(w_so[...], low).astype(BF)

        return run

    def attention(s):
        return attend_back_steps(
            s, length, qkv, qkv, qkv, width, 2 * width, p_self, rl_self, att_t, go_t, gqkv_t, gqkv_t, gqkv_t,
            width, 2 * width,
        )

    begin(0)()
    weave(attention(0), [begin(1)])
    weave(attention(1))


def self_grads_kernel(
    numbers_ref, gfs, dnorm_in, branch, gqkv_t, att_t, elow, w_qkv,
    send_ref, keep_ref, gin_own,
    gin, small,
):
    place = numbers_ref[0]
    tokens, width = gfs.shape
    length = tokens // 2
    half = width // 2
    where = halves(place, length)
    sums, held = {}, {}

    def give(which, ref):
        def out():
            give_tall(which, ref, att_t, branch)

        def part(index):
            def run():
                feats = pl.ds(pl.multiple_of(which * 3 * half + index * half, half), half)
                low, at = ((0, 0), (half, 0), (0, width))[index]
                ref[low : low + half, at : at + width] = mm(gqkv_t[feats, :], elow[...]).astype(BF)

            return run

        return [out, part(0), part(1), part(2)]

    def back(s):
        rows = slice(s * length, (s + 1) * length)

        def start():
            held[s] = mm(w_qkv[...], gqkv_t[:, rows])

        def finish():
            total = gfs[rows] + held.pop(s).T
            gin[rows] = total.astype(BF)
            sums[s] = jnp.sum(total, 0, keepdims=True)
            gin_own[s] = gin[where[s][0], :]
            send_ref[width + 16 :, s * width : (s + 1) * width] = gin[where[s][1], :]

        return [start, finish]

    weave(give(1 - place, send_ref) + give(place, keep_ref), back(0) + back(1))
    small[0:8, :] = dnorm_in[...]
    picked = lax.broadcasted_iota(jnp.int32, (8, width), 0) == numbers_ref[1]
    small[8:16, :] = jnp.where(picked, jnp.broadcast_to(sums[0] + sums[1], (8, width)), 0.0)
    for which, ref in ((1 - place, send_ref), (place, keep_ref)):
        ref[width : width + 16, :] = jnp.zeros((16, ref.shape[1]), BF)
        ref[width : width + 16, 0:half] = small[:, pl.ds(pl.multiple_of(which * half, half), half)].astype(BF)


def add_split_kernel(tail, bit_ref, a_ref, b_ref, send_ref, keep_ref):
    half = send_ref.shape[0] - tail
    bit = bit_ref[0]
    for which, ref in ((1 - bit, send_ref), (bit, keep_ref)):
        rows = pl.ds(pl.multiple_of(which * half, 16), half)
        ref[0:half, :] = (a_ref[rows, :].astype(F32) + b_ref[rows, :].astype(F32)).astype(BF)
        if tail:
            last = pl.ds(2 * half, tail)
            ref[half : half + tail, :] = (a_ref[last, :].astype(F32) + b_ref[last, :].astype(F32)).astype(BF)


def add_kernel(tail, a_ref, b_ref, out_ref, *tail_refs):
    rows = out_ref.shape[0]
    out_ref[...] = (a_ref[0:rows, :].astype(F32) + b_ref[0:rows, :].astype(F32)).astype(BF)
    if tail:
        last = slice(rows, rows + tail)
        tail_refs[0][...] = (a_ref[last, :].astype(F32) + b_ref[last, :].astype(F32)).astype(BF)


def join_kernel(index_ref, *refs):
    out = refs[-1]
    rows = refs[0].shape[0]
    for j, ref in enumerate(refs[:-1]):
        out[pl.ds(pl.multiple_of((index_ref[0] ^ j) * rows, 16), rows), :] = ref[...]


def unpack_kernel(unpack, count, index_ref, mine_ref, got_ref, *refs):
    rest = refs[: len(refs) - count - 1]
    mark_ref, *outs = refs[len(rest) :]
    mark_ref[...] = jnp.zeros(mark_ref.shape, F32)

    @pl.when(index_ref[0] == 0)
    def _():
        unpack(mine_ref, got_ref, *rest, *outs)

    @pl.when(index_ref[0] != 0)
    def _():
        unpack(got_ref, mine_ref, *rest, *outs)


def unpack_in(low_ref, high_ref, in_ref):
    half = low_ref.shape[0]
    in_ref[0:half, :] = low_ref[...].astype(F32)
    in_ref[half:, :] = high_ref[...].astype(F32)


def unpack_out(low_ref, high_ref, out_ref):
    tall = low_ref.shape[1]
    out_ref[0:tall, :] = low_ref[...].T.astype(F32)
    out_ref[tall:, :] = high_ref[...].T.astype(F32)


def unpack_tall(low_ref, high_ref, out_ref):
    half = out_ref.shape[1]
    width = 2 * half
    out_ref[0:half, :] = high_ref[:, width : width + half].astype(F32)
    out_ref[half:width, :] = high_ref[:, width + half :].astype(F32)


def unpack_cross(low_ref, high_ref, kv_ref, query_ref, out_ref):
    half, width = low_ref.shape[0], query_ref.shape[0]
    kv_ref[:, 0:half] = low_ref[:, 0:width].T.astype(F32)
    kv_ref[:, half:] = high_ref[:, 0:width].T.astype(F32)
    query_ref[...] = low_ref[:, width:].T.astype(F32)
    unpack_tall(low_ref, high_ref, out_ref)


def unpack_self(low_ref, high_ref, small_ref, qkv_ref, out_ref, gain_ref, bias_ref, table_ref):
    half, width = low_ref.shape[0], qkv_ref.shape[0]
    qkv_ref[:, 0:half] = low_ref[:, 0:width].T.astype(F32)
    qkv_ref[:, half:width] = high_ref[:, 0:width].T.astype(F32)
    qkv_ref[:, width:] = low_ref[:, width:].T.astype(F32)
    unpack_tall(low_ref, high_ref, out_ref)
    small = small_ref[:, 0 : gain_ref.shape[1]].astype(F32)
    gain_ref[...] = small[0:3]
    bias_ref[...] = small[3:6]
    table_ref[...] = small[8:16]


def place_kernel(numbers_ref, out_own, genc_own, gin_own, got_cross, got_self, *outs):
    place = numbers_ref[0]
    half, width = out_own.shape[1:]
    first = width + 16
    others = (got_cross, width + half), (got_cross, width), (got_self, first)
    for own_ref, (got_ref, at), out_ref in zip((out_own, genc_own, gin_own), others, outs):
        out_ref[place] = own_ref[...]
        for sentence in range(2):
            out_ref[1 - place, sentence] = got_ref[at : at + half, sentence * width : (sentence + 1) * width]


def smem():
    return pl.BlockSpec(memory_space=pltpu.SMEM)


def vmem():
    return pl.BlockSpec(memory_space=pltpu.VMEM)


def call(kernel, scalars, arrays, outs, scratch=(), name=None, far=(), results=(), sems=0, after=()):
    held = [*results, *scratch]
    limit = sum(math.prod(s[:-2]) * -(-s[-2] // 16) * 16 * s[-1] * jnp.dtype(d).itemsize for s, d in held) + 4 * MIB
    taken = len(scalars) + len(arrays) + len(far)
    anywhere = pl.BlockSpec(memory_space=pl.ANY)

    def body(*refs):
        kernel(*refs[:taken], *refs[taken + len(after) :])

    return pl.pallas_call(
        body,
        out_shape=tuple(pltpu.VMEM(s, d) for s, d in outs) + tuple(jax.ShapeDtypeStruct(s, d) for s, d in results),
        in_specs=[smem() for _ in scalars]
        + [vmem() for _ in arrays]
        + [pl.BlockSpec(memory_space=pltpu.HBM) for _ in far]
        + [anywhere for _ in after],
        out_specs=tuple(vmem() for _ in (*outs, *results)),
        scratch_shapes=[pltpu.VMEM(s, d) for s, d in scratch] + ([pltpu.SemaphoreType.DMA((sems,))] if sems else []),
        compiler_params=pltpu.CompilerParams(vmem_limit_bytes=limit),
        cost_estimate=pl.CostEstimate(**COST.get(name, SMALL_COST), transcendentals=0),
        name=name,
    )(
        *scalars,
        *(pltpu.with_memory_space_constraint(a, pltpu.VMEM) for a in arrays),
        *(pltpu.with_memory_space_constraint(a, pltpu.HBM) for a in far),
        *after,
    )


def local(
    dec_in, enc_out, out_grad, tgt_len, src_len, pair_id,
    self_qkv, self_out, cross_q, cross_kv, cross_out, ff_in, ff_out, norm_gain, norm_bias, lang_table,
):
    micro_count, sent_count, local_len, width = dec_in.shape
    seq_count = lax.axis_size("seq")
    dp_count = lax.axis_size("dp")
    place = lax.axis_index("seq")
    dp_place = lax.axis_index("dp")
    inner = ff_in.shape[1]
    length = local_len * seq_count
    tokens = sent_count * length
    half = width // 2
    mine = jnp.arange(micro_count) == place
    numbers = jnp.concatenate(
        [
            place.reshape(1),
            jnp.sum(jnp.where(mine, pair_id, 0)).reshape(1),
            jnp.sum(jnp.where(mine[:, None], tgt_len, 0), 0),
            jnp.sum(jnp.where(mine[:, None], src_len, 0), 0),
        ]
    ).astype(jnp.int32)
    swap = [(0, 1), (1, 0)]

    dec2 = lax.ppermute(dec_in, "seq", swap)
    enc2 = lax.ppermute(enc_out, "seq", swap)
    og2 = lax.ppermute(out_grad, "seq", swap)

    rows = (sent_count, local_len, width)
    whole = (tokens, width)
    probs = (sent_count * HEADS, length, length)
    sums = (sent_count * HEADS, 1, length)
    turned = (width, tokens)
    buffer = (width, LANES)
    kinds = {
        "out_own": (rows, BF), "out_oth": ((local_len, LANES), BF), "send_in": (buffer, BF),
        "send_out": (buffer, BF), "gff_t": (turned, BF),
        "hidden": ((tokens, inner), BF), "slow_t": (turned, BF), "ginner": ((tokens, inner), BF), "gss": (whole, F32),
        "elow": (whole, BF), "qkv": ((tokens, 3 * width), BF), "p_self": (probs, BF), "rl_self": (sums, F32),
        "att_t": (turned, BF), "xhat1": (whole, F32), "rstd1": ((tokens, 128), F32), "flow": (whole, BF),
        "encs": (whole, BF), "cq": (whole, BF), "ckv": ((tokens, 2 * width), BF), "p_cross": (probs, BF),
        "rl_cross": (sums, F32), "crossed_t": (turned, BF), "dnorm": ((8, width), F32),
    }
    params = {
        "qkv": self_qkv, "so": self_out, "cq": cross_q, "ckv": cross_kv, "co": cross_out, "fi": ff_in, "fo": ff_out,
        "gain": norm_gain, "nbias": norm_bias, "table": lang_table,
    }
    kinds.update({"w_" + name: (weight.shape, weight.dtype) for name, weight in params.items()})
    kept = call(
        forward_kernel,
        (numbers,),
        (dec2, enc2, og2),
        [kinds[name] for name in FORWARD_KEPT],
        [kinds["w_" + name] for name in FORWARD_WEIGHTS if name not in PASSED_WEIGHTS]
        + [
            (whole, BF), (whole, BF), (whole, F32), ((4, length, length), F32), (whole, BF), (whole, F32), (whole, BF),
            (whole, F32), ((tokens, 128), F32), (whole, F32), (whole, BF), ((tokens, inner), BF), (whole, BF), (whole, BF),
        ],
        name="forward",
        far=(dec_in, enc_out, out_grad, *(params[name] for name in FORWARD_WEIGHTS)),
        sems=32,
    )
    held = dict(zip(FORWARD_KEPT, kept))

    def of(*names):
        return [held[name] for name in names]

    def flips(core_zero, core_one):
        return [(2 * d, 2 * (d ^ core_zero)) for d in range(dp_count)] + [
            (2 * d + 1, 2 * (d ^ core_one) + 1) for d in range(dp_count)
        ]

    def travel(array, core_zero, core_one):
        return lax.ppermute(array, ("dp", "seq"), flips(core_zero, core_one))

    last = []

    def reduce_all(keep, got, outs, unpack, route, tail=0):
        def run(kernel, scalars, arrays, outs, name, results=()):
            got = call(kernel, scalars, arrays, outs, name=name, results=results, after=tuple(last))
            last[:] = [got[0]]
            return got

        rows, lanes = keep.shape
        body = rows - tail
        if dp_count != 16:
            (total,) = run(functools.partial(add_kernel, 0), (), (keep, got), [((rows, lanes), BF)], "add_core")
            total = lax.psum(total, "dp")
            mine, other = total[: body // 2], total[body // 2 : body]
            rest = (total[body:],) if tail else ()
            bit = jnp.zeros((1,), jnp.int32)
            for _ in range(2 * len(route)):
                yield
        else:
            bits = [
                (jnp.where(place == 0, dp_place & zero, dp_place & one) != 0).astype(jnp.int32).reshape(1)
                for zero, one in route
            ]
            held = body
            for bit, flip in zip(bits, route):
                held //= 2
                shape = (held + tail, lanes)
                send, keep = run(functools.partial(add_split_kernel, tail), (bit,), (keep, got), [(shape, BF)] * 2, "add_split")
                got = travel(send, *flip)
                yield
            pieces = [((held, lanes), BF)] + ([((tail, lanes), BF)] if tail else [])
            mine, *rest = run(functools.partial(add_kernel, tail), (), (keep, got), pieces, "add_last")
            for bit, flip in zip(bits[:0:-1], route[:0:-1]):
                other = travel(mine, *flip)
                yield
                held *= 2
                (mine,) = run(join_kernel, (bit,), (mine, other), [((held, lanes), BF)], "join")
            other = travel(mine, *route[0])
            bit = bits[0]
            yield
        _, *unpacked = run(
            functools.partial(unpack_kernel, unpack, len(outs)),
            (bit,),
            (mine, other, *rest),
            [((8, 128), F32)],
            "unpack",
            [(s, F32) for s in outs],
        )
        yield unpacked

    held["keep_in"], held["keep_out"] = call(
        feed_keep_kernel,
        (numbers,),
        of("gff_t", "hidden", "slow_t", "ginner"),
        [(buffer, BF), (buffer, BF)],
        name="feed_keep",
    )
    last[:] = of("keep_in")

    def store(names, arrays):
        held.update(zip(names, arrays))
        last[:] = [arrays[0]]

    def cross_back():
        store(
            ("cross_branch", "gq_t", "gkv_t", "gfs", "dnorm"),
            call(
                cross_kernel,
                (),
                of("gss", "dnorm", "w_gain", "w_co", "w_cq", "ckv", "cq", "p_cross", "rl_cross", "crossed_t", "xhat1", "rstd1"),
                [(whole, BF), (turned, BF), ((2 * width, tokens), BF), (whole, F32), ((8, width), F32)],
                [(turned, BF)],
                name="cross",
                after=last,
            ),
        )

    def cross_grads():
        longer = (width + 2 * local_len, LANES)
        send, keep, held["genc_own"] = call(
            cross_grads_kernel,
            (numbers,),
            of("cross_branch", "gq_t", "gkv_t", "crossed_t", "flow", "encs", "w_ckv", "out_oth"),
            [(longer, BF), (buffer, BF), (rows, BF)],
            [(whole, BF)],
            name="cross_grads",
            after=last,
        )
        last[:] = [send]
        held["got_cross"] = lax.ppermute(send, "seq", swap)
        groups["x"] = reduce_all(
            keep, held["got_cross"], [(width, width), (width, half), (width, half)], unpack_cross, ROUTES["x"]
        )

    def self_back():
        store(
            ("self_branch", "gqkv_t"),
            call(
                self_kernel,
                (),
                of("gfs", "w_so", "qkv", "p_self", "rl_self", "att_t"),
                [(whole, BF), ((3 * width, tokens), BF)],
                [(turned, BF)],
                name="self",
                after=last,
            ),
        )

    def self_grads():
        longer = (width + 16 + local_len, LANES)
        send, keep, held["gin_own"] = call(
            self_grads_kernel,
            (numbers,),
            of("gfs", "dnorm", "self_branch", "gqkv_t", "att_t", "elow", "w_qkv"),
            [(longer, BF), ((width + 16, LANES), BF), (rows, BF)],
            [(whole, BF), ((16, width), F32)],
            name="self_grads",
            after=last,
        )
        last[:] = [send]
        held["got_self"] = lax.ppermute(send, "seq", swap)
        results = [(width, 3 * half), (width, half), (3, half), (3, half), (8, half)]
        groups["s"] = reduce_all(keep, held["got_self"], results, unpack_self, ROUTES["s"], tail=16)

    def place_all():
        held["placed"] = call(
            place_kernel,
            (numbers,),
            of("out_own", "genc_own", "gin_own", "got_cross", "got_self"),
            [],
            name="place",
            results=[(dec_in.shape, BF)] * 3,
            after=last,
        )

    groups = {
        "f": reduce_all(held["keep_in"], lax.ppermute(held["send_in"], "seq", swap), [(width, inner // 2)], unpack_in, ROUTES["f"]),
        "F": reduce_all(held["keep_out"], lax.ppermute(held["send_out"], "seq", swap), [(inner, half)], unpack_out, ROUTES["F"]),
    }
    kernels = {"X": cross_back, "G": cross_grads, "S": self_back, "T": self_grads, "P": place_all}
    sums = {}
    for letter in ORDER:
        if letter in kernels:
            kernels[letter]()
        else:
            sums[letter] = next(groups[letter])
    (g_ff_in,), (g_ff_out,) = sums["f"], sums["F"]
    g_cross_kv, g_cross_q, g_cross_out = sums["x"]
    g_qkv, g_self_out, g_gain, g_bias, g_table = sums["s"]
    output, grad_encoder, grad_input = held["placed"]
    return (
        output,
        grad_input,
        grad_encoder,
        g_qkv,
        g_self_out,
        g_cross_q,
        g_cross_kv,
        g_cross_out,
        g_ff_in,
        g_ff_out,
        g_gain,
        g_bias,
        g_table,
    )


def solution(mesh):
    acts = P(None, "dp", "seq", None)
    lens = P(None, "dp")
    cut = P(None, "seq")
    return jax.shard_map(
        local,
        mesh=mesh,
        in_specs=(acts, acts, acts, lens, lens) + (P(),) * 11,
        out_specs=(acts, acts, acts) + (cut,) * 10,
        check_vma=False,
    )
```

```python
import functools
import math
from types import SimpleNamespace
from typing import Any, NamedTuple

import jax
import jax.numpy as jnp
from jax import lax
from jax.experimental import pallas as pl
from jax.experimental.pallas import tpu as pltpu
from jax.sharding import PartitionSpec as P

HEADS = 8
NORM_EPS = 1e-05
NEG_FILL = -1e30
BF = jnp.bfloat16
F32 = jnp.float32
MIB = 1 << 20
ORDER = "XfFGSfxTFfsxfFsFxsxfFsFfPxsxfsFxsfxFs"
PLANE_FIRST = ((1, 2), (2, 1), (4, 4), (8, 8))
BETWEEN = ((1, 2), (4, 4), (2, 1), (8, 8))
LINE_FIRST = ((4, 4), (1, 2), (2, 1), (8, 8))
ROUTES = {"f": PLANE_FIRST, "F": LINE_FIRST, "x": BETWEEN, "s": PLANE_FIRST}
SMALL_COST = {"flops": 20_000_000_000, "bytes_accessed": 400_000_000}
COST = {
    name: {"flops": 100_000_000_000, "bytes_accessed": 1000}
    for name in ("forward", "feed_keep", "cross", "cross_grads", "self", "self_grads")
}
LANES = 1024


def mm(a, b):
    return lax.dot_general(a, b, (((1,), (0,)), ((), ())), preferred_element_type=F32)


def mm_bt(a, b):
    return lax.dot_general(a, b, (((1,), (1,)), ((), ())), preferred_element_type=F32)


def norm_forward(values, gain, bias):
    center = values - jnp.mean(values, -1, keepdims=True)
    rstd = lax.rsqrt(jnp.mean(center * center, -1, keepdims=True) + NORM_EPS)
    xhat = center * rstd
    return xhat, rstd, xhat * gain + bias


def norm_backward(xhat, rstd, gain, upstream):
    scaled = upstream * gain
    first = jnp.mean(scaled, -1, keepdims=True)
    second = jnp.mean(scaled * xhat, -1, keepdims=True)
    grad = rstd * (scaled - first - xhat * second)
    return grad, jnp.sum(upstream * xhat, 0, keepdims=True), jnp.sum(upstream, 0, keepdims=True)


def lane_half(shape, half):
    lane = lax.broadcasted_iota(jnp.int32, shape, 1)
    return (lane < 64) if half == 0 else (lane >= 64)


def weave(*lists):
    steps = [((i + 0.5) / len(some), k, step) for k, some in enumerate(lists) for i, step in enumerate(some)]
    for _, _, step in sorted(steps, key=lambda item: item[:2]):
        step()


def staged(count, *stages):
    held = {}

    def step(stage, item):
        def run():
            held[item] = stages[stage](item, held.get(item))

        return run

    return [
        step(k, t - k) for t in range(count + len(stages) - 1) for k in range(len(stages)) if 0 <= t - k < count
    ]


def attend_steps(sentence, length, q_ref, k_ref, v_ref, k_at, v_at, bias_ref, p_ref, rl_ref, out_ref, out_t):
    rows = pl.ds(sentence * length, length)

    def score(pair, _):
        queries = q_ref[rows, pair * 128 : pair * 128 + 128]
        keys = k_ref[rows, k_at + pair * 128 : k_at + pair * 128 + 128]
        zeros = jnp.zeros_like(queries)
        return [
            mm_bt(keys, jnp.where(lane_half(queries.shape, half), queries, zeros)) + bias_ref[sentence]
            for half in range(2)
        ]

    def soften(pair, scores):
        probs = []
        for half in range(2):
            top = jnp.max(scores[half], 0, keepdims=True)
            probs.append(jnp.exp(scores[half] - top).astype(BF))
            p_ref[sentence * HEADS + 2 * pair + half] = probs[half]
        return probs

    def mix(pair, probs):
        values_t = v_ref[rows, v_at + pair * 128 : v_at + pair * 128 + 128].T
        mixed = []
        for half in range(2):
            tall = jnp.concatenate([values_t[half * 64 : half * 64 + 64], jnp.ones((16, length), BF)], 0)
            both = mm(tall, probs[half])
            one_over = 1.0 / both[64:65]
            rl_ref[sentence * HEADS + 2 * pair + half] = one_over
            mixed.append(both[0:64] * one_over)
        joined = jnp.concatenate(mixed, 0).astype(BF)
        out_t[pair * 128 : pair * 128 + 128, rows] = joined
        out_ref[rows, pair * 128 : pair * 128 + 128] = joined.T

    return staged(HEADS // 2, score, soften, mix)


def attend_back_steps(
    sentence, length, q_ref, k_ref, v_ref, k_at, v_at, p_ref, rl_ref, out_t, go_t, gq_t, gk_t, gv_t, gk_at, gv_at
):
    rows = pl.ds(sentence * length, length)

    def start(pair, _):
        feats = slice(pair * 128, pair * 128 + 128)
        values = v_ref[rows, v_at + pair * 128 : v_at + pair * 128 + 128]
        mixed = out_t[feats, rows].astype(F32)
        grads = go_t[feats, rows].astype(F32)
        scaled, dots = [], []
        for half in range(2):
            part = slice(half * 64, half * 64 + 64)
            scaled.append((grads[part] * rl_ref[sentence * HEADS + 2 * pair + half]).astype(BF))
            dots.append(jnp.sum(mixed[part] * scaled[half].astype(F32), 0, keepdims=True))
        both = jnp.concatenate(scaled, 0)
        zeros = jnp.zeros_like(values)
        grad_probs = [mm(jnp.where(lane_half(values.shape, half), values, zeros), both) for half in range(2)]
        return scaled, dots, grad_probs

    def middle(pair, held):
        scaled, dots, grad_probs = held
        grad_scores = []
        for half in range(2):
            probs = p_ref[sentence * HEADS + 2 * pair + half].astype(F32)
            grad_scores.append((probs * (grad_probs[half] - dots[half])).astype(BF))
        return scaled, grad_scores

    def finish(pair, held):
        scaled, grad_scores = held
        queries_t = q_ref[rows, pair * 128 : pair * 128 + 128].T
        keys_t = k_ref[rows, k_at + pair * 128 : k_at + pair * 128 + 128].T
        gq, gk, gv = [], [], []
        for half in range(2):
            part = slice(half * 64, half * 64 + 64)
            gq.append(mm(keys_t[part], grad_scores[half]) * 0.125)
            gk.append(mm_bt(queries_t[part], grad_scores[half]))
            gv.append(mm_bt(scaled[half], p_ref[sentence * HEADS + 2 * pair + half]))
        for ref, at, grads in ((gq_t, 0, gq), (gk_t, gk_at, gk), (gv_t, gv_at, gv)):
            ref[at + pair * 128 : at + pair * 128 + 128, rows] = jnp.concatenate(grads, 0).astype(BF)

    return staged(HEADS // 2, start, middle, finish)


class Copies:
    def __init__(self, sems):
        self.sems, self.used, self.open = sems, 0, {}

    def start(self, name, source, target):
        copy = pltpu.make_async_copy(source, target, self.sems.at[self.used])
        self.used += 1
        copy.start()
        self.open.setdefault(name, []).append(copy)

    def wait(self, *names):
        for name in names or tuple(self.open):
            for copy in self.open.pop(name, ()):
                copy.wait()


def halves(place, length):
    half = length // 2
    return [
        [pl.ds(pl.multiple_of(sentence * length + which * half, half), half) for which in (place, 1 - place)]
        for sentence in range(2)
    ]


def feed_grads(which, in_ref, out_ref, slow_t, ginner, gff_t, hidden):
    inner, width = hidden.shape[1], slow_t.shape[0]
    half_in, half_out = inner // 2, width // 2

    def give_in(index):
        def run():
            cols = pl.ds(pl.multiple_of(which * half_in + index * 256, 256), 256)
            in_ref[:, index * 256 : (index + 1) * 256] = mm(slow_t[...], ginner[:, cols]).astype(BF)

        return run

    def give_out(index):
        def run():
            feats = pl.ds(pl.multiple_of(which * half_out, half_out), half_out)
            low, at = (index // 2) * half_out, (index % 2) * 512
            out_ref[low : low + half_out, at : at + 512] = mm(
                gff_t[feats, :], hidden[:, index * 512 : (index + 1) * 512]
            ).astype(BF)

        return run

    return [give_out(i) for i in range(inner // 512)] + [give_in(i) for i in range(half_in // 256)]


def feed_keep_kernel(numbers_ref, gff_t, hidden, slow_t, ginner, in_ref, out_ref):
    weave(feed_grads(numbers_ref[0], in_ref, out_ref, slow_t, ginner, gff_t, hidden))


class Weights(NamedTuple):
    table: Any
    qkv: Any
    gain: Any
    nbias: Any
    ckv: Any
    so: Any
    cq: Any
    co: Any
    fi: Any
    fo: Any


class Kept(NamedTuple):
    out_own: Any
    out_oth: Any
    send_in: Any
    send_out: Any
    gff_t: Any
    hidden: Any
    slow_t: Any
    ginner: Any
    gss: Any
    elow: Any
    qkv: Any
    p_self: Any
    rl_self: Any
    att_t: Any
    xhat1: Any
    rstd1: Any
    flow: Any
    encs: Any
    cq: Any
    ckv: Any
    p_cross: Any
    rl_cross: Any
    crossed_t: Any
    dnorm: Any
    w_qkv: Any
    w_gain: Any
    w_ckv: Any
    w_so: Any
    w_cq: Any
    w_co: Any


def forward_kernel(numbers_ref, *refs):
    (dec2_in, enc2_in, og2_in, dec_in, enc_in, og_in), refs = refs[:6], refs[6:]
    weights_in, refs = Weights(*refs[: len(Weights._fields)]), refs[len(Weights._fields) :]
    kept, refs = Kept(*refs[: len(Kept._fields)]), refs[len(Kept._fields) :]
    (out_own, out_oth, send_in, send_out, gff_t, hidden, slow_t, ginner, gss, elow, qkv, p_self, rl_self, att_t, xhat1,
     rstd1, flow, encs, cq, ckv, p_cross, rl_cross, crossed_t, dnorm_ref) = kept[:24]
    w = Weights(*refs[:1], kept.w_qkv, kept.w_gain, refs[1], kept.w_ckv, kept.w_so, kept.w_cq, kept.w_co, *refs[2:4])
    (dec_s, og_s, bias_ref, att, xhat2, rstd2, third, slow, slope, gff, outs, sems) = refs[4:]
    crossed = att
    at = Weights(*range(len(Weights._fields)))
    dec, enc, og = (-1, -2, -3)
    copies = Copies(sems)
    place = numbers_ref[0]
    tokens, width = dec_s.shape
    length = tokens // 2
    inner = ginner.shape[1]
    where = halves(place, length)
    for s in range(2):
        copies.start(dec, dec_in.at[place, s], dec_s.at[where[s][0]])
        copies.start(dec, dec2_in.at[place, s], dec_s.at[where[s][1]])
    for key in at[:4]:
        copies.start(key, weights_in[key], w[key])
    for s in range(2):
        copies.start(enc, enc_in.at[place, s], encs.at[where[s][0]])
        copies.start(enc, enc2_in.at[place, s], encs.at[where[s][1]])
    for key in at[4:]:
        copies.start(key, weights_in[key], w[key])
    for s in range(2):
        copies.start(og, og_in.at[place, s], og_s.at[where[s][0]])
        copies.start(og, og2_in.at[place, s], og_s.at[where[s][1]])

    rows = [slice(s * length, (s + 1) * length) for s in range(2)]
    keys_at = lax.broadcasted_iota(jnp.int32, (length, length), 0)
    query_at = lax.broadcasted_iota(jnp.int32, (length, length), 1)
    for s in range(2):
        bias_ref[s] = jnp.where((keys_at <= query_at) & (keys_at < numbers_ref[2 + s]), 0.0, NEG_FILL)
        bias_ref[2 + s] = jnp.where(keys_at < numbers_ref[4 + s], 0.0, NEG_FILL)

    def embed(s):
        def run():
            elow[rows[s]] = (dec_s[rows[s]].astype(F32) + row).astype(BF)

        return run

    def pack(s, part):
        def run():
            cols = slice(part * width, (part + 1) * width)
            values = mm(elow[rows[s]], w.qkv[:, cols])
            qkv[rows[s], cols] = (values * 0.125 if part == 0 else values).astype(BF)

        return run

    def pack_cross(s, part):
        def run():
            cols = slice(part * width, (part + 1) * width)
            ckv[rows[s], cols] = mm(encs[rows[s]], w.ckv[:, cols]).astype(BF)

        return run

    held = {}

    def after_self(s):
        def project():
            held[0, s] = dec_s[rows[s]].astype(F32) + row + mm(att[rows[s]], w.so[...])

        def norm():
            xhat, rstd, normed = norm_forward(held.pop((0, s)), gain[0:1], nbias[0:1])
            xhat1[rows[s]] = xhat
            rstd1[rows[s]] = jnp.broadcast_to(rstd, (length, 128))
            flow[rows[s]] = normed.astype(BF)

        def query():
            cq[rows[s]] = (mm(flow[rows[s]], w.cq[...]) * 0.125).astype(BF)

        return [project, norm, query]

    def after_cross(s):
        def project():
            held[1, s] = xhat1[rows[s]] * gain[0:1] + nbias[0:1] + mm(crossed[rows[s]], w.co[...])

        def norm():
            xhat, rstd, normed = norm_forward(held.pop((1, s)), gain[1:2], nbias[1:2])
            xhat2[rows[s]] = xhat
            rstd2[rows[s]] = jnp.broadcast_to(rstd, (length, 128))
            third[rows[s]] = normed
            slow[rows[s]] = normed.astype(BF)

        def turn():
            slow_t[:, rows[s]] = slow[rows[s]].T

        return [project, norm, turn]

    step = 256

    def feed(s):
        def grow(index, _):
            return mm(slow[rows[s]], w.fi[:, index * step : (index + 1) * step])

        def bend(index, v):
            cols = slice(index * step, (index + 1) * step)
            square = v * v
            bent = jnp.tanh(v * (0.7978845608028654 + (0.7978845608028654 * 0.044715) * square))
            half = 0.5 + 0.5 * bent
            hidden[rows[s], cols] = (v * half).astype(BF)
            rise = v * (0.7978845608028654 + (3 * 0.7978845608028654 * 0.044715) * square)
            slope[rows[s], cols] = (half + (0.5 - 0.5 * bent * bent) * rise).astype(BF)

        return staged(inner // step, grow, bend)

    gains = {}

    def after_feed(s):
        def shrink(part):
            def run():
                cols = slice(part * (width // 2), (part + 1) * (width // 2))
                third[rows[s], cols] += mm(hidden[rows[s]], w.fo[:, cols])

            return run

        def norm():
            xhat, rstd, normed = norm_forward(third[rows[s]], gain[2:3], nbias[2:3])
            outs[rows[s]] = normed.astype(BF)
            grad, *gains[2, s] = norm_backward(xhat, rstd, gain[2:3], og_s[rows[s]].astype(F32))
            third[rows[s]] = grad
            gff[rows[s]] = grad.astype(BF)

        def turn():
            gff_t[:, rows[s]] = gff[rows[s]].T
            out_own[s] = outs[where[s][0], :]
            out_oth[:, s * width : (s + 1) * width] = outs[where[s][1], :]

        return [shrink(0), shrink(1), norm, turn]

    def feed_back(s):
        def shrink(index, _):
            return mm_bt(gff[rows[s]], w.fo[index * step : (index + 1) * step, :]).astype(BF)

        def bend(index, grad_hidden):
            cols = slice(index * step, (index + 1) * step)
            ginner[rows[s], cols] = (grad_hidden.astype(F32) * slope[rows[s], cols].astype(F32)).astype(BF)

        return staged(inner // step, shrink, bend)

    def after_feed_back(s):
        def shrink(part):
            def run():
                cols = slice(part * (width // 2), (part + 1) * (width // 2))
                third[rows[s], cols] += mm_bt(ginner[rows[s]], w.fi[cols, :])

            return run

        def norm():
            gss[rows[s]], *gains[1, s] = norm_backward(xhat2[rows[s]], rstd2[rows[s], 0:1], gain[1:2], third[rows[s]])

        return [shrink(0), shrink(1), norm]

    copies.wait(at.table, at.gain, at.nbias, dec, at.qkv)
    gain = w.gain[...].astype(F32)
    nbias = w.nbias[...].astype(F32)
    picked = lax.broadcasted_iota(jnp.int32, w.table.shape, 0) == numbers_ref[1]
    row = jnp.sum(jnp.where(picked, w.table[...].astype(F32), 0.0), 0, keepdims=True)
    weave([embed(0)])
    weave([pack(0, part) for part in range(3)], [embed(1)])
    copies.wait(enc, at.ckv)
    weave(
        attend_steps(0, length, qkv, qkv, qkv, width, 2 * width, bias_ref, p_self, rl_self, att, att_t),
        [pack(1, part) for part in range(3)] + [pack_cross(0, 0), pack_cross(0, 1)],
    )
    copies.wait(at.so, at.cq, at.co)
    weave(
        attend_steps(1, length, qkv, qkv, qkv, width, 2 * width, bias_ref, p_self, rl_self, att, att_t),
        after_self(0) + [pack_cross(1, 0), pack_cross(1, 1)],
    )
    cross_bias = bias_ref.at[2:4]
    weave(
        attend_steps(0, length, cq, ckv, ckv, 0, width, cross_bias, p_cross, rl_cross, crossed, crossed_t),
        after_self(1),
    )
    copies.wait(at.fi, at.fo, og)
    weave(
        attend_steps(1, length, cq, ckv, ckv, 0, width, cross_bias, p_cross, rl_cross, crossed, crossed_t),
        after_cross(0),
    )
    weave(feed(0), after_cross(1))
    weave(feed(1), after_feed(0))
    weave(feed_back(0), after_feed(1))
    weave(feed_back(1), after_feed_back(0))
    weave(feed_grads(1 - place, send_in, send_out, slow_t, ginner, gff_t, hidden), after_feed_back(1))
    dnorm_ref[...] = jnp.zeros(dnorm_ref.shape, F32)
    for k in (1, 2):
        dnorm_ref[k : k + 1, :] = gains[k, 0][0] + gains[k, 1][0]
        dnorm_ref[3 + k : 4 + k, :] = gains[k, 0][1] + gains[k, 1][1]
    copies.wait()


def cross_kernel(
    gss, dnorm_in, w_gain, w_co, w_cq, ckv, cq, p_cross, rl_cross, crossed_t, xhat1, rstd1,
    branch, gq_t, gkv_t, gfs, dnorm_ref,
    go_t,
):
    tokens, width = gss.shape
    length = tokens // 2
    rows = [slice(s * length, (s + 1) * length) for s in range(2)]
    gain = w_gain[...].astype(F32)
    gains = {}

    def begin(s):
        def run():
            low = gss[rows[s]].astype(BF)
            branch[rows[s]] = low
            go_t[:, rows[s]] = mm_bt(w_co[...], low).astype(BF)

        return run

    def after(s):
        held = {}

        def query():
            held[0] = gss[rows[s]] + mm_bt(gq_t[:, rows[s]].T, w_cq[...])

        def norm():
            gfs[rows[s]], *gains[s] = norm_backward(xhat1[rows[s]], rstd1[rows[s], 0:1], gain[0:1], held[0])

        return [query, norm]

    def attention(s):
        return attend_back_steps(
            s, length, cq, ckv, ckv, 0, width, p_cross, rl_cross, crossed_t, go_t, gq_t, gkv_t, gkv_t, 0, width
        )

    begin(0)()
    weave(attention(0), [begin(1)])
    weave(attention(1), after(0))
    weave(after(1))
    dnorm_ref[...] = dnorm_in[...]
    dnorm_ref[0:1, :] = gains[0][0] + gains[1][0]
    dnorm_ref[3:4, :] = gains[0][1] + gains[1][1]


def give_tall(which, ref, mixed_t, branch):
    width = branch.shape[1]
    half = width // 2
    cols = pl.ds(pl.multiple_of(which * half, half), half)
    grads = mm(mixed_t[...], branch[:, cols]).astype(BF)
    ref[half:width, width : width + half] = grads[0:half]
    ref[half:width, width + half :] = grads[half:]


def cross_grads_kernel(
    numbers_ref, branch, gq_t, gkv_t, crossed_t, flow, encs, w_ckv, out_oth, send_ref, keep_ref, genc_own, genc
):
    place = numbers_ref[0]
    tokens, width = branch.shape
    length = tokens // 2
    half = width // 2
    where = halves(place, length)

    def give(which, ref):
        def out():
            give_tall(which, ref, crossed_t, branch)

        def query():
            feats = pl.ds(pl.multiple_of(which * half, half), half)
            ref[0:half, width:] = mm(gq_t[feats, :], flow[...]).astype(BF)

        def pair():
            feats = pl.ds(pl.multiple_of(which * width, half), width)
            ref[0:width, 0:width] = mm(gkv_t[feats, :], encs[...]).astype(BF)

        return [out, query, pair]

    def encoder(s):
        def run():
            rows = slice(s * length, (s + 1) * length)
            genc[rows] = mm(w_ckv[...], gkv_t[:, rows]).astype(BF).T
            genc_own[s] = genc[where[s][0], :]
            send_ref[width : width + length // 2, s * width : (s + 1) * width] = genc[where[s][1], :]

        return run

    weave(give(1 - place, send_ref) + give(place, keep_ref), [encoder(0), encoder(1)])
    send_ref[width + length // 2 :, :] = out_oth[...]


def self_kernel(gfs, w_so, qkv, p_self, rl_self, att_t, branch, gqkv_t, go_t):
    tokens, width = gfs.shape
    length = tokens // 2
    rows = [slice(s * length, (s + 1) * length) for s in range(2)]

    def begin(s):
        def run():
            low = gfs[rows[s]].astype(BF)
            branch[rows[s]] = low
            go_t[:, rows[s]] = mm_bt(w_so[...], low).astype(BF)

        return run

    def attention(s):
        return attend_back_steps(
            s, length, qkv, qkv, qkv, width, 2 * width, p_self, rl_self, att_t, go_t, gqkv_t, gqkv_t, gqkv_t,
            width, 2 * width,
        )

    begin(0)()
    weave(attention(0), [begin(1)])
    weave(attention(1))


def self_grads_kernel(
    numbers_ref, gfs, dnorm_in, branch, gqkv_t, att_t, elow, w_qkv,
    send_ref, keep_ref, gin_own,
    gin, small,
):
    place = numbers_ref[0]
    tokens, width = gfs.shape
    length = tokens // 2
    half = width // 2
    where = halves(place, length)
    sums, held = {}, {}

    def give(which, ref):
        def out():
            give_tall(which, ref, att_t, branch)

        def part(index):
            def run():
                feats = pl.ds(pl.multiple_of(which * 3 * half + index * half, half), half)
                low, at = ((0, 0), (half, 0), (0, width))[index]
                ref[low : low + half, at : at + width] = mm(gqkv_t[feats, :], elow[...]).astype(BF)

            return run

        return [out, part(0), part(1), part(2)]

    def back(s):
        rows = slice(s * length, (s + 1) * length)

        def start():
            held[s] = mm(w_qkv[...], gqkv_t[:, rows])

        def finish():
            total = gfs[rows] + held.pop(s).T
            gin[rows] = total.astype(BF)
            sums[s] = jnp.sum(total, 0, keepdims=True)
            gin_own[s] = gin[where[s][0], :]
            send_ref[width + 16 :, s * width : (s + 1) * width] = gin[where[s][1], :]

        return [start, finish]

    weave(give(1 - place, send_ref) + give(place, keep_ref), back(0) + back(1))
    small[0:8, :] = dnorm_in[...]
    picked = lax.broadcasted_iota(jnp.int32, (8, width), 0) == numbers_ref[1]
    small[8:16, :] = jnp.where(picked, jnp.broadcast_to(sums[0] + sums[1], (8, width)), 0.0)
    for which, ref in ((1 - place, send_ref), (place, keep_ref)):
        ref[width : width + 16, :] = jnp.zeros((16, ref.shape[1]), BF)
        ref[width : width + 16, 0:half] = small[:, pl.ds(pl.multiple_of(which * half, half), half)].astype(BF)


def add_split_kernel(tail, bit_ref, a_ref, b_ref, send_ref, keep_ref):
    half = send_ref.shape[0] - tail
    bit = bit_ref[0]
    for which, ref in ((1 - bit, send_ref), (bit, keep_ref)):
        rows = pl.ds(pl.multiple_of(which * half, 16), half)
        ref[0:half, :] = (a_ref[rows, :].astype(F32) + b_ref[rows, :].astype(F32)).astype(BF)
        if tail:
            last = pl.ds(2 * half, tail)
            ref[half : half + tail, :] = (a_ref[last, :].astype(F32) + b_ref[last, :].astype(F32)).astype(BF)


def add_kernel(tail, a_ref, b_ref, out_ref, *tail_refs):
    rows = out_ref.shape[0]
    out_ref[...] = (a_ref[0:rows, :].astype(F32) + b_ref[0:rows, :].astype(F32)).astype(BF)
    if tail:
        last = slice(rows, rows + tail)
        tail_refs[0][...] = (a_ref[last, :].astype(F32) + b_ref[last, :].astype(F32)).astype(BF)


def join_kernel(index_ref, *refs):
    out = refs[-1]
    rows = refs[0].shape[0]
    for j, ref in enumerate(refs[:-1]):
        out[pl.ds(pl.multiple_of((index_ref[0] ^ j) * rows, 16), rows), :] = ref[...]


def unpack_kernel(unpack, count, index_ref, mine_ref, got_ref, *refs):
    rest = refs[: len(refs) - count - 1]
    mark_ref, *outs = refs[len(rest) :]
    mark_ref[...] = jnp.zeros(mark_ref.shape, F32)

    @pl.when(index_ref[0] == 0)
    def _():
        unpack(mine_ref, got_ref, *rest, *outs)

    @pl.when(index_ref[0] != 0)
    def _():
        unpack(got_ref, mine_ref, *rest, *outs)


def unpack_in(low_ref, high_ref, in_ref):
    half = low_ref.shape[0]
    in_ref[0:half, :] = low_ref[...].astype(F32)
    in_ref[half:, :] = high_ref[...].astype(F32)


def unpack_out(low_ref, high_ref, out_ref):
    tall = low_ref.shape[1]
    out_ref[0:tall, :] = low_ref[...].T.astype(F32)
    out_ref[tall:, :] = high_ref[...].T.astype(F32)


def unpack_tall(low_ref, high_ref, out_ref):
    half = out_ref.shape[1]
    width = 2 * half
    out_ref[0:half, :] = high_ref[:, width : width + half].astype(F32)
    out_ref[half:width, :] = high_ref[:, width + half :].astype(F32)


def unpack_cross(low_ref, high_ref, kv_ref, query_ref, out_ref):
    half, width = low_ref.shape[0], query_ref.shape[0]
    kv_ref[:, 0:half] = low_ref[:, 0:width].T.astype(F32)
    kv_ref[:, half:] = high_ref[:, 0:width].T.astype(F32)
    query_ref[...] = low_ref[:, width:].T.astype(F32)
    unpack_tall(low_ref, high_ref, out_ref)


def unpack_self(low_ref, high_ref, small_ref, qkv_ref, out_ref, gain_ref, bias_ref, table_ref):
    half, width = low_ref.shape[0], qkv_ref.shape[0]
    qkv_ref[:, 0:half] = low_ref[:, 0:width].T.astype(F32)
    qkv_ref[:, half:width] = high_ref[:, 0:width].T.astype(F32)
    qkv_ref[:, width:] = low_ref[:, width:].T.astype(F32)
    unpack_tall(low_ref, high_ref, out_ref)
    small = small_ref[:, 0 : gain_ref.shape[1]].astype(F32)
    gain_ref[...] = small[0:3]
    bias_ref[...] = small[3:6]
    table_ref[...] = small[8:16]


def place_kernel(numbers_ref, out_own, genc_own, gin_own, got_cross, got_self, *outs):
    place = numbers_ref[0]
    half, width = out_own.shape[1:]
    first = width + 16
    others = (got_cross, width + half), (got_cross, width), (got_self, first)
    for own_ref, (got_ref, at), out_ref in zip((out_own, genc_own, gin_own), others, outs):
        out_ref[place] = own_ref[...]
        for sentence in range(2):
            out_ref[1 - place, sentence] = got_ref[at : at + half, sentence * width : (sentence + 1) * width]


def smem():
    return pl.BlockSpec(memory_space=pltpu.SMEM)


def vmem():
    return pl.BlockSpec(memory_space=pltpu.VMEM)


def call(kernel, scalars, arrays, outs, scratch=(), name=None, far=(), results=(), sems=0, after=()):
    held = [*results, *scratch]
    limit = sum(math.prod(s[:-2]) * -(-s[-2] // 16) * 16 * s[-1] * jnp.dtype(d).itemsize for s, d in held) + 6 * MIB
    taken = len(scalars) + len(arrays) + len(far)
    anywhere = pl.BlockSpec(memory_space=pl.ANY)

    def body(*refs):
        kernel(*refs[:taken], *refs[taken + len(after) :])

    return pl.pallas_call(
        body,
        out_shape=tuple(pltpu.VMEM(s, d) for s, d in outs) + tuple(jax.ShapeDtypeStruct(s, d) for s, d in results),
        in_specs=[smem() for _ in scalars]
        + [vmem() for _ in arrays]
        + [pl.BlockSpec(memory_space=pltpu.HBM) for _ in far]
        + [anywhere for _ in after],
        out_specs=tuple(vmem() for _ in (*outs, *results)),
        scratch_shapes=[pltpu.VMEM(s, d) for s, d in scratch] + ([pltpu.SemaphoreType.DMA((sems,))] if sems else []),
        compiler_params=pltpu.CompilerParams(vmem_limit_bytes=limit),
        cost_estimate=pl.CostEstimate(**COST.get(name, SMALL_COST), transcendentals=0),
        name=name,
    )(
        *scalars,
        *(pltpu.with_memory_space_constraint(a, pltpu.VMEM) for a in arrays),
        *(pltpu.with_memory_space_constraint(a, pltpu.HBM) for a in far),
        *after,
    )


def local(
    dec_in, enc_out, out_grad, tgt_len, src_len, pair_id,
    self_qkv, self_out, cross_q, cross_kv, cross_out, ff_in, ff_out, norm_gain, norm_bias, lang_table,
):
    micro_count, sent_count, local_len, width = dec_in.shape
    seq_count = lax.axis_size("seq")
    dp_count = lax.axis_size("dp")
    place = lax.axis_index("seq")
    dp_place = lax.axis_index("dp")
    inner = ff_in.shape[1]
    length = local_len * seq_count
    tokens = sent_count * length
    half = width // 2
    mine = jnp.arange(micro_count) == place
    numbers = jnp.concatenate(
        [
            place.reshape(1),
            jnp.sum(jnp.where(mine, pair_id, 0)).reshape(1),
            jnp.sum(jnp.where(mine[:, None], tgt_len, 0), 0),
            jnp.sum(jnp.where(mine[:, None], src_len, 0), 0),
        ]
    ).astype(jnp.int32)
    swap = [(0, 1), (1, 0)]

    dec2 = lax.ppermute(dec_in, "seq", swap)
    enc2 = lax.ppermute(enc_out, "seq", swap)
    og2 = lax.ppermute(out_grad, "seq", swap)

    rows = (sent_count, local_len, width)
    whole = (tokens, width)
    probs = (sent_count * HEADS, length, length)
    sums = (sent_count * HEADS, 1, length)
    turned = (width, tokens)
    buffer = (width, LANES)
    like = lambda a: (a.shape, a.dtype)
    params = Weights(
        lang_table, self_qkv, norm_gain, norm_bias, cross_kv, self_out, cross_q, cross_out, ff_in, ff_out
    )
    kinds = Kept(
        out_own=(rows, BF),
        out_oth=((local_len, LANES), BF),
        send_in=(buffer, BF),
        send_out=(buffer, BF),
        gff_t=(turned, BF),
        hidden=((tokens, inner), BF),
        slow_t=(turned, BF),
        ginner=((tokens, inner), BF),
        gss=(whole, F32),
        elow=(whole, BF),
        qkv=((tokens, 3 * width), BF),
        p_self=(probs, BF),
        rl_self=(sums, F32),
        att_t=(turned, BF),
        xhat1=(whole, F32),
        rstd1=((tokens, 128), F32),
        flow=(whole, BF),
        encs=(whole, BF),
        cq=(whole, BF),
        ckv=((tokens, 2 * width), BF),
        p_cross=(probs, BF),
        rl_cross=(sums, F32),
        crossed_t=(turned, BF),
        dnorm=((8, width), F32),
        w_qkv=like(self_qkv),
        w_gain=like(norm_gain),
        w_ckv=like(cross_kv),
        w_so=like(self_out),
        w_cq=like(cross_q),
        w_co=like(cross_out),
    )
    kept = call(
        forward_kernel,
        (numbers,),
        (dec2, enc2, og2),
        list(kinds),
        [like(lang_table), like(norm_bias), like(ff_in), like(ff_out)]
        + [
            (whole, BF), (whole, BF), ((4, length, length), F32), (whole, BF), (whole, F32), ((tokens, 128), F32),
            (whole, F32), (whole, BF), ((tokens, inner), BF), (whole, BF), (whole, BF),
        ],
        name="forward",
        far=(dec_in, enc_out, out_grad, *params),
        sems=32,
    )
    held = SimpleNamespace(**Kept(*kept)._asdict())

    def flips(core_zero, core_one):
        return [(2 * d, 2 * (d ^ core_zero)) for d in range(dp_count)] + [
            (2 * d + 1, 2 * (d ^ core_one) + 1) for d in range(dp_count)
        ]

    def travel(array, core_zero, core_one):
        return lax.ppermute(array, ("dp", "seq"), flips(core_zero, core_one))

    last = []

    def reduce_all(keep, got, outs, unpack, route, tail=0):
        def run(kernel, scalars, arrays, outs, name, results=()):
            got = call(kernel, scalars, arrays, outs, name=name, results=results, after=tuple(last))
            last[:] = [got[0]]
            return got

        rows, lanes = keep.shape
        body = rows - tail
        if dp_count != 16:
            (total,) = run(functools.partial(add_kernel, 0), (), (keep, got), [((rows, lanes), BF)], "add_core")
            total = lax.psum(total, "dp")
            mine, other = total[: body // 2], total[body // 2 : body]
            rest = (total[body:],) if tail else ()
            bit = jnp.zeros((1,), jnp.int32)
            for _ in range(2 * len(route) - 1):
                yield
        else:
            bits = [
                (jnp.where(place == 0, dp_place & zero, dp_place & one) != 0).astype(jnp.int32).reshape(1)
                for zero, one in route
            ]
            held = body
            for bit, flip in zip(bits, route[:-1]):
                held //= 2
                shape = (held + tail, lanes)
                send, keep = run(functools.partial(add_split_kernel, tail), (bit,), (keep, got), [(shape, BF)] * 2, "add_split")
                got = travel(send, *flip)
                yield
            (keep,) = run(functools.partial(add_kernel, 0), (), (keep, got), [(shape, BF)], "add_all")
            got = travel(keep, *route[-1])
            yield
            pieces = [((held, lanes), BF)] + ([((tail, lanes), BF)] if tail else [])
            mine, *rest = run(functools.partial(add_kernel, tail), (), (keep, got), pieces, "add_last")
            for bit, flip in zip(bits[1:-1][::-1], route[1:-1][::-1]):
                other = travel(mine, *flip)
                yield
                held *= 2
                (mine,) = run(join_kernel, (bit,), (mine, other), [((held, lanes), BF)], "join")
            other = travel(mine, *route[0])
            bit = bits[0]
            yield
        _, *unpacked = run(
            functools.partial(unpack_kernel, unpack, len(outs)),
            (bit,),
            (mine, other, *rest),
            [((8, 128), F32)],
            "unpack",
            [(s, F32) for s in outs],
        )
        yield unpacked

    held.keep_in, held.keep_out = call(
        feed_keep_kernel,
        (numbers,),
        [held.gff_t, held.hidden, held.slow_t, held.ginner],
        [(buffer, BF), (buffer, BF)],
        name="feed_keep",
    )
    last[:] = [held.keep_in]

    def cross_back():
        held.cross_branch, held.gq_t, held.gkv_t, held.gfs, held.dnorm = (
            call(
                cross_kernel,
                (),
                [held.gss, held.dnorm, held.w_gain, held.w_co, held.w_cq, held.ckv, held.cq, held.p_cross, held.rl_cross, held.crossed_t, held.xhat1, held.rstd1],
                [(whole, BF), (turned, BF), ((2 * width, tokens), BF), (whole, F32), ((8, width), F32)],
                [(turned, BF)],
                name="cross",
                after=last,
            )
        )
        last[:] = [held.gfs]

    def cross_grads():
        longer = (width + 2 * local_len, LANES)
        send, keep, held.genc_own = call(
            cross_grads_kernel,
            (numbers,),
            [held.cross_branch, held.gq_t, held.gkv_t, held.crossed_t, held.flow, held.encs, held.w_ckv, held.out_oth],
            [(longer, BF), (buffer, BF), (rows, BF)],
            [(whole, BF)],
            name="cross_grads",
            after=last,
        )
        last[:] = [send]
        held.got_cross = lax.ppermute(send, "seq", swap)
        groups["x"] = reduce_all(
            keep, held.got_cross, [(width, width), (width, half), (width, half)], unpack_cross, ROUTES["x"]
        )

    def self_back():
        held.self_branch, held.gqkv_t = (
            call(
                self_kernel,
                (),
                [held.gfs, held.w_so, held.qkv, held.p_self, held.rl_self, held.att_t],
                [(whole, BF), ((3 * width, tokens), BF)],
                [(turned, BF)],
                name="self",
                after=last,
            )
        )
        last[:] = [held.self_branch]

    def self_grads():
        longer = (width + 16 + local_len, LANES)
        send, keep, held.gin_own = call(
            self_grads_kernel,
            (numbers,),
            [held.gfs, held.dnorm, held.self_branch, held.gqkv_t, held.att_t, held.elow, held.w_qkv],
            [(longer, BF), ((width + 16, LANES), BF), (rows, BF)],
            [(whole, BF), ((16, width), F32)],
            name="self_grads",
            after=last,
        )
        last[:] = [send]
        held.got_self = lax.ppermute(send, "seq", swap)
        results = [(width, 3 * half), (width, half), (3, half), (3, half), (8, half)]
        groups["s"] = reduce_all(keep, held.got_self, results, unpack_self, ROUTES["s"], tail=16)

    def place_all():
        held.placed = call(
            place_kernel,
            (numbers,),
            [held.out_own, held.genc_own, held.gin_own, held.got_cross, held.got_self],
            [],
            name="place",
            results=[(dec_in.shape, BF)] * 3,
            after=last,
        )

    groups = {
        "f": reduce_all(held.keep_in, lax.ppermute(held.send_in, "seq", swap), [(width, inner // 2)], unpack_in, ROUTES["f"]),
        "F": reduce_all(held.keep_out, lax.ppermute(held.send_out, "seq", swap), [(inner, half)], unpack_out, ROUTES["F"]),
    }
    kernels = {"X": cross_back, "G": cross_grads, "S": self_back, "T": self_grads, "P": place_all}
    sums = {}
    for letter in ORDER:
        if letter in kernels:
            kernels[letter]()
        else:
            sums[letter] = next(groups[letter])
    (g_ff_in,), (g_ff_out,) = sums["f"], sums["F"]
    g_cross_kv, g_cross_q, g_cross_out = sums["x"]
    g_qkv, g_self_out, g_gain, g_bias, g_table = sums["s"]
    output, grad_encoder, grad_input = held.placed
    return (
        output,
        grad_input,
        grad_encoder,
        g_qkv,
        g_self_out,
        g_cross_q,
        g_cross_kv,
        g_cross_out,
        g_ff_in,
        g_ff_out,
        g_gain,
        g_bias,
        g_table,
    )


def solution(mesh):
    acts = P(None, "dp", "seq", None)
    lens = P(None, "dp")
    cut = P(None, "seq")
    return jax.shard_map(
        local,
        mesh=mesh,
        in_specs=(acts, acts, acts, lens, lens) + (P(),) * 11,
        out_specs=(acts, acts, acts) + (cut,) * 10,
        check_vma=False,
    )
```

```python
import functools
import math
from types import SimpleNamespace
from typing import Any, NamedTuple

import jax
import jax.numpy as jnp
from jax import lax
from jax.experimental import pallas as pl
from jax.experimental.pallas import tpu as pltpu
from jax.sharding import PartitionSpec as P

HEADS = 8
NORM_EPS = 1e-05
NEG_FILL = -1e30
BF = jnp.bfloat16
F32 = jnp.float32
MIB = 1 << 20
ORDER = "JFKfXGSfxTFfsxfFsFxsxfsPFfxFsxfsFxfsxFs"
PLANE_FIRST = ((1, 2), (2, 1), (4, 4), (8, 8))
BETWEEN = ((1, 2), (4, 4), (2, 1), (8, 8))
LINE_FIRST = ((4, 4), (1, 2), (2, 1), (8, 8))
ROUTES = {"f": BETWEEN, "F": LINE_FIRST, "x": BETWEEN, "s": PLANE_FIRST}
SMALL_COST = {"flops": 20_000_000_000, "bytes_accessed": 400_000_000}
COST = {
    name: {"flops": 100_000_000_000, "bytes_accessed": 1000}
    for name in ("forward", "feed_back", "feed_keep", "cross", "cross_grads", "self", "self_grads")
}
LANES = 1024


def mm(a, b):
    return lax.dot_general(a, b, (((1,), (0,)), ((), ())), preferred_element_type=F32)


def mm_bt(a, b):
    return lax.dot_general(a, b, (((1,), (1,)), ((), ())), preferred_element_type=F32)


def norm_forward(values, gain, bias):
    center = values - jnp.mean(values, -1, keepdims=True)
    rstd = lax.rsqrt(jnp.mean(center * center, -1, keepdims=True) + NORM_EPS)
    xhat = center * rstd
    return xhat, rstd, xhat * gain + bias


def norm_backward(xhat, rstd, gain, upstream):
    scaled = upstream * gain
    first = jnp.mean(scaled, -1, keepdims=True)
    second = jnp.mean(scaled * xhat, -1, keepdims=True)
    grad = rstd * (scaled - first - xhat * second)
    return grad, jnp.sum(upstream * xhat, 0, keepdims=True), jnp.sum(upstream, 0, keepdims=True)


def lane_half(shape, half):
    lane = lax.broadcasted_iota(jnp.int32, shape, 1)
    return (lane < 64) if half == 0 else (lane >= 64)


def weave(*lists):
    steps = [((i + 0.5) / len(some), k, step) for k, some in enumerate(lists) for i, step in enumerate(some)]
    for _, _, step in sorted(steps, key=lambda item: item[:2]):
        step()


def staged(count, *stages):
    held = {}

    def step(stage, item):
        def run():
            held[item] = stages[stage](item, held.get(item))

        return run

    return [
        step(k, t - k) for t in range(count + len(stages) - 1) for k in range(len(stages)) if 0 <= t - k < count
    ]


def attend_steps(sentence, length, q_ref, k_ref, v_ref, k_at, v_at, bias_ref, p_ref, rl_ref, out_ref, out_t):
    rows = pl.ds(sentence * length, length)

    def score(pair, _):
        queries = q_ref[rows, pair * 128 : pair * 128 + 128]
        keys = k_ref[rows, k_at + pair * 128 : k_at + pair * 128 + 128]
        zeros = jnp.zeros_like(queries)
        return [
            mm_bt(keys, jnp.where(lane_half(queries.shape, half), queries, zeros)) + bias_ref[sentence]
            for half in range(2)
        ]

    def soften(pair, scores):
        probs = []
        for half in range(2):
            top = jnp.max(scores[half], 0, keepdims=True)
            probs.append(jnp.exp(scores[half] - top).astype(BF))
            p_ref[sentence * HEADS + 2 * pair + half] = probs[half]
        return probs

    def mix(pair, probs):
        values_t = v_ref[rows, v_at + pair * 128 : v_at + pair * 128 + 128].T
        mixed = []
        for half in range(2):
            tall = jnp.concatenate([values_t[half * 64 : half * 64 + 64], jnp.ones((16, length), BF)], 0)
            both = mm(tall, probs[half])
            one_over = 1.0 / both[64:65]
            rl_ref[sentence * HEADS + 2 * pair + half] = one_over
            mixed.append(both[0:64] * one_over)
        joined = jnp.concatenate(mixed, 0).astype(BF)
        out_t[pair * 128 : pair * 128 + 128, rows] = joined
        out_ref[rows, pair * 128 : pair * 128 + 128] = joined.T

    return staged(HEADS // 2, score, soften, mix)


def attend_back_steps(
    sentence, length, q_ref, k_ref, v_ref, k_at, v_at, p_ref, rl_ref, out_t, go_t, gq_t, gk_t, gv_t, gk_at, gv_at
):
    rows = pl.ds(sentence * length, length)

    def start(pair, _):
        feats = slice(pair * 128, pair * 128 + 128)
        values = v_ref[rows, v_at + pair * 128 : v_at + pair * 128 + 128]
        mixed = out_t[feats, rows].astype(F32)
        grads = go_t[feats, rows].astype(F32)
        scaled, dots = [], []
        for half in range(2):
            part = slice(half * 64, half * 64 + 64)
            scaled.append((grads[part] * rl_ref[sentence * HEADS + 2 * pair + half]).astype(BF))
            dots.append(jnp.sum(mixed[part] * scaled[half].astype(F32), 0, keepdims=True))
        both = jnp.concatenate(scaled, 0)
        zeros = jnp.zeros_like(values)
        grad_probs = [mm(jnp.where(lane_half(values.shape, half), values, zeros), both) for half in range(2)]
        return scaled, dots, grad_probs

    def middle(pair, held):
        scaled, dots, grad_probs = held
        grad_scores = []
        for half in range(2):
            probs = p_ref[sentence * HEADS + 2 * pair + half].astype(F32)
            grad_scores.append((probs * (grad_probs[half] - dots[half])).astype(BF))
        return scaled, grad_scores

    def finish(pair, held):
        scaled, grad_scores = held
        queries_t = q_ref[rows, pair * 128 : pair * 128 + 128].T
        keys_t = k_ref[rows, k_at + pair * 128 : k_at + pair * 128 + 128].T
        gq, gk, gv = [], [], []
        for half in range(2):
            part = slice(half * 64, half * 64 + 64)
            gq.append(mm(keys_t[part], grad_scores[half]) * 0.125)
            gk.append(mm_bt(queries_t[part], grad_scores[half]))
            gv.append(mm_bt(scaled[half], p_ref[sentence * HEADS + 2 * pair + half]))
        for ref, at, grads in ((gq_t, 0, gq), (gk_t, gk_at, gk), (gv_t, gv_at, gv)):
            ref[at + pair * 128 : at + pair * 128 + 128, rows] = jnp.concatenate(grads, 0).astype(BF)

    return staged(HEADS // 2, start, middle, finish)


class Copies:
    def __init__(self, sems):
        self.sems, self.used, self.open = sems, 0, {}

    def start(self, name, source, target):
        copy = pltpu.make_async_copy(source, target, self.sems.at[self.used])
        self.used += 1
        copy.start()
        self.open.setdefault(name, []).append(copy)

    def wait(self, *names):
        for name in names or tuple(self.open):
            for copy in self.open.pop(name, ()):
                copy.wait()


def halves(place, length):
    half = length // 2
    return [
        [pl.ds(pl.multiple_of(sentence * length + which * half, half), half) for which in (place, 1 - place)]
        for sentence in range(2)
    ]


def give_out_steps(which, ref, gff_t, hidden):
    half = gff_t.shape[0] // 2

    def give(index):
        def run():
            feats = pl.ds(pl.multiple_of(which * half, half), half)
            low, at = (index // 2) * half, (index % 2) * 512
            ref[low : low + half, at : at + 512] = mm(
                gff_t[feats, :], hidden[:, index * 512 : (index + 1) * 512]
            ).astype(BF)

        return run

    return [give(index) for index in range(hidden.shape[1] // 512)]


def give_in_steps(which, ref, slow_t, ginner):
    length, inner = ginner[0].shape
    half = inner // 2

    def give(index):
        def run():
            cols = pl.ds(pl.multiple_of(which * half + index * 256, 256), 256)
            total = mm(slow_t[:, 0:length], ginner[0][:, cols]) + mm(slow_t[:, length:], ginner[1][:, cols])
            ref[:, index * 256 : (index + 1) * 256] = total.astype(BF)

        return run

    return [give(index) for index in range(half // 256)]


def feed_back_steps(gff, w_fo, slope, ginner):
    step = 256

    def shrink(index, _):
        return mm_bt(gff[...], w_fo[index * step : (index + 1) * step, :]).astype(BF)

    def bend(index, grad_hidden):
        cols = slice(index * step, (index + 1) * step)
        ginner[:, cols] = (grad_hidden.astype(F32) * slope[:, cols].astype(F32)).astype(BF)

    return staged(ginner.shape[1] // step, shrink, bend)


def feed_kernel(numbers_ref, gff, w_fo, slope, slow_t, gff_t, hidden, ginner_first, send_in, keep_out, ginner_last):
    place = numbers_ref[0]
    length = ginner_last.shape[0]
    weave(
        feed_back_steps(gff.at[length:], w_fo, slope.at[length:], ginner_last),
        give_out_steps(place, keep_out, gff_t, hidden),
    )
    weave(give_in_steps(1 - place, send_in, slow_t, (ginner_first, ginner_last)))


def feed_keep_kernel(numbers_ref, slow_t, ginner_first, ginner_last, keep_in):
    weave(give_in_steps(numbers_ref[0], keep_in, slow_t, (ginner_first, ginner_last)))


class Weights(NamedTuple):
    table: Any
    qkv: Any
    gain: Any
    nbias: Any
    ckv: Any
    so: Any
    cq: Any
    co: Any
    fi: Any
    fo: Any


class Kept(NamedTuple):
    out_own: Any
    out_oth: Any
    send_out: Any
    gff: Any
    gff_t: Any
    hidden: Any
    slope: Any
    slow_t: Any
    ginner: Any
    third: Any
    xhat2: Any
    rstd2: Any
    elow: Any
    qkv: Any
    p_self: Any
    rl_self: Any
    att_t: Any
    xhat1: Any
    rstd1: Any
    flow: Any
    encs: Any
    cq: Any
    ckv: Any
    p_cross: Any
    rl_cross: Any
    crossed_t: Any
    dnorm: Any
    w_qkv: Any
    w_gain: Any
    w_ckv: Any
    w_so: Any
    w_cq: Any
    w_co: Any
    w_fi: Any
    w_fo: Any


def forward_kernel(numbers_ref, *refs):
    (dec2_in, enc2_in, og2_in, dec_in, enc_in, og_in), refs = refs[:6], refs[6:]
    weights_in, refs = Weights(*refs[: len(Weights._fields)]), refs[len(Weights._fields) :]
    kept, refs = Kept(*refs[: len(Kept._fields)]), refs[len(Kept._fields) :]
    (out_own, out_oth, send_out, gff, gff_t, hidden, slope, slow_t, ginner, third, xhat2, rstd2, elow, qkv, p_self,
     rl_self, att_t, xhat1, rstd1, flow, encs, cq, ckv, p_cross, rl_cross, crossed_t, dnorm_ref) = kept[:27]
    w = Weights(refs[0], kept.w_qkv, kept.w_gain, refs[1], *kept[29:])
    (dec_s, og_s, bias_ref, att, slow, outs, sems) = refs[2:]
    crossed = att
    at = Weights(*range(len(Weights._fields)))
    dec, enc, og = (-1, -2, -3)
    copies = Copies(sems)
    place = numbers_ref[0]
    tokens, width = dec_s.shape
    length = tokens // 2
    inner = hidden.shape[1]
    where = halves(place, length)
    for s in range(2):
        copies.start(dec, dec_in.at[place, s], dec_s.at[where[s][0]])
        copies.start(dec, dec2_in.at[place, s], dec_s.at[where[s][1]])
    for key in at[:4]:
        copies.start(key, weights_in[key], w[key])
    for s in range(2):
        copies.start(enc, enc_in.at[place, s], encs.at[where[s][0]])
        copies.start(enc, enc2_in.at[place, s], encs.at[where[s][1]])
    for key in at[4:]:
        copies.start(key, weights_in[key], w[key])
    for s in range(2):
        copies.start(og, og_in.at[place, s], og_s.at[where[s][0]])
        copies.start(og, og2_in.at[place, s], og_s.at[where[s][1]])

    rows = [slice(s * length, (s + 1) * length) for s in range(2)]
    keys_at = lax.broadcasted_iota(jnp.int32, (length, length), 0)
    query_at = lax.broadcasted_iota(jnp.int32, (length, length), 1)
    for s in range(2):
        bias_ref[s] = jnp.where((keys_at <= query_at) & (keys_at < numbers_ref[2 + s]), 0.0, NEG_FILL)
        bias_ref[2 + s] = jnp.where(keys_at < numbers_ref[4 + s], 0.0, NEG_FILL)

    def embed(s):
        def run():
            elow[rows[s]] = (dec_s[rows[s]].astype(F32) + row).astype(BF)

        return run

    def pack(s, part):
        def run():
            cols = slice(part * width, (part + 1) * width)
            values = mm(elow[rows[s]], w.qkv[:, cols])
            qkv[rows[s], cols] = (values * 0.125 if part == 0 else values).astype(BF)

        return run

    def pack_cross(s, part):
        def run():
            cols = slice(part * width, (part + 1) * width)
            ckv[rows[s], cols] = mm(encs[rows[s]], w.ckv[:, cols]).astype(BF)

        return run

    held = {}

    def after_self(s):
        def project():
            held[0, s] = dec_s[rows[s]].astype(F32) + row + mm(att[rows[s]], w.so[...])

        def norm():
            xhat, rstd, normed = norm_forward(held.pop((0, s)), gain[0:1], nbias[0:1])
            xhat1[rows[s]] = xhat
            rstd1[rows[s]] = jnp.broadcast_to(rstd, (length, 128))
            flow[rows[s]] = normed.astype(BF)

        def query():
            cq[rows[s]] = (mm(flow[rows[s]], w.cq[...]) * 0.125).astype(BF)

        return [project, norm, query]

    def after_cross(s):
        def project():
            held[1, s] = xhat1[rows[s]] * gain[0:1] + nbias[0:1] + mm(crossed[rows[s]], w.co[...])

        def norm():
            xhat, rstd, normed = norm_forward(held.pop((1, s)), gain[1:2], nbias[1:2])
            xhat2[rows[s]] = xhat
            rstd2[rows[s]] = jnp.broadcast_to(rstd, (length, 128))
            third[rows[s]] = normed
            slow[rows[s]] = normed.astype(BF)

        def turn():
            slow_t[:, rows[s]] = slow[rows[s]].T

        return [project, norm, turn]

    step = 256

    def feed(s):
        def grow(index, _):
            return mm(slow[rows[s]], w.fi[:, index * step : (index + 1) * step])

        def bend(index, v):
            cols = slice(index * step, (index + 1) * step)
            square = v * v
            bent = jnp.tanh(v * (0.7978845608028654 + (0.7978845608028654 * 0.044715) * square))
            half = 0.5 + 0.5 * bent
            hidden[rows[s], cols] = (v * half).astype(BF)
            rise = v * (0.7978845608028654 + (3 * 0.7978845608028654 * 0.044715) * square)
            slope[rows[s], cols] = (half + (0.5 - 0.5 * bent * bent) * rise).astype(BF)

        return staged(inner // step, grow, bend)

    gains = {}

    def after_feed(s):
        def shrink(part):
            def run():
                cols = slice(part * (width // 2), (part + 1) * (width // 2))
                third[rows[s], cols] += mm(hidden[rows[s]], w.fo[:, cols])

            return run

        def norm():
            xhat, rstd, normed = norm_forward(third[rows[s]], gain[2:3], nbias[2:3])
            outs[rows[s]] = normed.astype(BF)
            grad, *gains[2, s] = norm_backward(xhat, rstd, gain[2:3], og_s[rows[s]].astype(F32))
            third[rows[s]] = grad
            gff[rows[s]] = grad.astype(BF)

        def turn():
            gff_t[:, rows[s]] = gff[rows[s]].T
            out_own[s] = outs[where[s][0], :]
            out_oth[:, s * width : (s + 1) * width] = outs[where[s][1], :]

        return [shrink(0), shrink(1), norm, turn]

    copies.wait(at.table, at.gain, at.nbias, dec, at.qkv)
    gain = w.gain[...].astype(F32)
    nbias = w.nbias[...].astype(F32)
    picked = lax.broadcasted_iota(jnp.int32, w.table.shape, 0) == numbers_ref[1]
    row = jnp.sum(jnp.where(picked, w.table[...].astype(F32), 0.0), 0, keepdims=True)
    weave([embed(0)])
    weave([pack(0, part) for part in range(3)], [embed(1)])
    copies.wait(enc, at.ckv)
    weave(
        attend_steps(0, length, qkv, qkv, qkv, width, 2 * width, bias_ref, p_self, rl_self, att, att_t),
        [pack(1, part) for part in range(3)] + [pack_cross(0, 0), pack_cross(0, 1)],
    )
    copies.wait(at.so, at.cq, at.co)
    weave(
        attend_steps(1, length, qkv, qkv, qkv, width, 2 * width, bias_ref, p_self, rl_self, att, att_t),
        after_self(0) + [pack_cross(1, 0), pack_cross(1, 1)],
    )
    cross_bias = bias_ref.at[2:4]
    weave(
        attend_steps(0, length, cq, ckv, ckv, 0, width, cross_bias, p_cross, rl_cross, crossed, crossed_t),
        after_self(1),
    )
    copies.wait(at.fi, at.fo, og)
    weave(
        attend_steps(1, length, cq, ckv, ckv, 0, width, cross_bias, p_cross, rl_cross, crossed, crossed_t),
        after_cross(0),
    )
    weave(feed(0), after_cross(1))
    weave(feed(1), after_feed(0))
    weave(feed_back_steps(gff.at[0:length], w.fo, slope.at[0:length], ginner), after_feed(1))
    weave(give_out_steps(1 - place, send_out, gff_t, hidden))
    dnorm_ref[...] = jnp.zeros(dnorm_ref.shape, F32)
    dnorm_ref[2:3, :] = gains[2, 0][0] + gains[2, 1][0]
    dnorm_ref[5:6, :] = gains[2, 0][1] + gains[2, 1][1]
    copies.wait()


def cross_kernel(
    third, ginner_first, ginner_last, w_fi, xhat2, rstd2, dnorm_in, w_gain, w_co, w_cq, ckv, cq, p_cross, rl_cross, crossed_t, xhat1, rstd1,
    branch, gq_t, gkv_t, gfs, dnorm_ref,
    go_t, gss,
):
    tokens, width = gss.shape
    length = tokens // 2
    rows = [slice(s * length, (s + 1) * length) for s in range(2)]
    gain = w_gain[...].astype(F32)
    gains, seconds = {}, {}
    ginner = (ginner_first, ginner_last)

    def before(s):
        held = []

        def shrink(part):
            def run():
                cols = slice(part * (width // 2), (part + 1) * (width // 2))
                held.append(third[rows[s], cols] + mm_bt(ginner[s][...], w_fi[cols, :]))

            return run

        def norm():
            upstream = jnp.concatenate(held, 1)
            gss[rows[s]], *seconds[s] = norm_backward(xhat2[rows[s]], rstd2[rows[s], 0:1], gain[1:2], upstream)

        return [shrink(0), shrink(1), norm, begin(s)]

    def begin(s):
        def run():
            low = gss[rows[s]].astype(BF)
            branch[rows[s]] = low
            go_t[:, rows[s]] = mm_bt(w_co[...], low).astype(BF)

        return run

    def after(s):
        held = {}

        def query():
            held[0] = gss[rows[s]] + mm_bt(gq_t[:, rows[s]].T, w_cq[...])

        def norm():
            gfs[rows[s]], *gains[s] = norm_backward(xhat1[rows[s]], rstd1[rows[s], 0:1], gain[0:1], held[0])

        return [query, norm]

    def attention(s):
        return attend_back_steps(
            s, length, cq, ckv, ckv, 0, width, p_cross, rl_cross, crossed_t, go_t, gq_t, gkv_t, gkv_t, 0, width
        )

    weave(before(0))
    weave(attention(0), before(1))
    weave(attention(1), after(0))
    weave(after(1))
    dnorm_ref[...] = dnorm_in[...]
    for k, sums in enumerate((gains, seconds)):
        dnorm_ref[k : k + 1, :] = sums[0][0] + sums[1][0]
        dnorm_ref[3 + k : 4 + k, :] = sums[0][1] + sums[1][1]


def give_tall(which, ref, mixed_t, branch):
    width = branch.shape[1]
    half = width // 2
    cols = pl.ds(pl.multiple_of(which * half, half), half)
    grads = mm(mixed_t[...], branch[:, cols]).astype(BF)
    ref[half:width, width : width + half] = grads[0:half]
    ref[half:width, width + half :] = grads[half:]


def cross_grads_kernel(
    numbers_ref, branch, gq_t, gkv_t, crossed_t, flow, encs, w_ckv, out_oth, send_ref, keep_ref, genc_own, genc
):
    place = numbers_ref[0]
    tokens, width = branch.shape
    length = tokens // 2
    half = width // 2
    where = halves(place, length)

    def give(which, ref):
        def out():
            give_tall(which, ref, crossed_t, branch)

        def query():
            feats = pl.ds(pl.multiple_of(which * half, half), half)
            ref[0:half, width:] = mm(gq_t[feats, :], flow[...]).astype(BF)

        def pair():
            feats = pl.ds(pl.multiple_of(which * width, half), width)
            ref[0:width, 0:width] = mm(gkv_t[feats, :], encs[...]).astype(BF)

        return [out, query, pair]

    def encoder(s):
        def run():
            rows = slice(s * length, (s + 1) * length)
            genc[rows] = mm(w_ckv[...], gkv_t[:, rows]).astype(BF).T
            genc_own[s] = genc[where[s][0], :]
            send_ref[width : width + length // 2, s * width : (s + 1) * width] = genc[where[s][1], :]

        return run

    weave(give(1 - place, send_ref) + give(place, keep_ref), [encoder(0), encoder(1)])
    send_ref[width + length // 2 :, :] = out_oth[...]


def self_kernel(gfs, w_so, qkv, p_self, rl_self, att_t, branch, gqkv_t, go_t):
    tokens, width = gfs.shape
    length = tokens // 2
    rows = [slice(s * length, (s + 1) * length) for s in range(2)]

    def begin(s):
        def run():
            low = gfs[rows[s]].astype(BF)
            branch[rows[s]] = low
            go_t[:, rows[s]] = mm_bt(w_so[...], low).astype(BF)

        return run

    def attention(s):
        return attend_back_steps(
            s, length, qkv, qkv, qkv, width, 2 * width, p_self, rl_self, att_t, go_t, gqkv_t, gqkv_t, gqkv_t,
            width, 2 * width,
        )

    begin(0)()
    weave(attention(0), [begin(1)])
    weave(attention(1))


def self_grads_kernel(
    numbers_ref, gfs, dnorm_in, branch, gqkv_t, att_t, elow, w_qkv,
    send_ref, keep_ref, gin_own,
    gin, small,
):
    place = numbers_ref[0]
    tokens, width = gfs.shape
    length = tokens // 2
    half = width // 2
    where = halves(place, length)
    sums, held = {}, {}

    def give(which, ref):
        def out():
            give_tall(which, ref, att_t, branch)

        def part(index):
            def run():
                feats = pl.ds(pl.multiple_of(which * 3 * half + index * half, half), half)
                low, at = ((0, 0), (half, 0), (0, width))[index]
                ref[low : low + half, at : at + width] = mm(gqkv_t[feats, :], elow[...]).astype(BF)

            return run

        return [out, part(0), part(1), part(2)]

    def back(s):
        rows = slice(s * length, (s + 1) * length)

        def start():
            held[s] = mm(w_qkv[...], gqkv_t[:, rows])

        def finish():
            total = gfs[rows] + held.pop(s).T
            gin[rows] = total.astype(BF)
            sums[s] = jnp.sum(total, 0, keepdims=True)
            gin_own[s] = gin[where[s][0], :]
            send_ref[width + 16 :, s * width : (s + 1) * width] = gin[where[s][1], :]

        return [start, finish]

    weave(give(1 - place, send_ref) + give(place, keep_ref), back(0) + back(1))
    small[0:8, :] = dnorm_in[...]
    picked = lax.broadcasted_iota(jnp.int32, (8, width), 0) == numbers_ref[1]
    small[8:16, :] = jnp.where(picked, jnp.broadcast_to(sums[0] + sums[1], (8, width)), 0.0)
    for which, ref in ((1 - place, send_ref), (place, keep_ref)):
        ref[width : width + 16, :] = jnp.zeros((16, ref.shape[1]), BF)
        ref[width : width + 16, 0:half] = small[:, pl.ds(pl.multiple_of(which * half, half), half)].astype(BF)


def add_split_kernel(tail, bit_ref, a_ref, b_ref, send_ref, keep_ref):
    half = send_ref.shape[0] - tail
    bit = bit_ref[0]
    for which, ref in ((1 - bit, send_ref), (bit, keep_ref)):
        rows = pl.ds(pl.multiple_of(which * half, 16), half)
        ref[0:half, :] = (a_ref[rows, :].astype(F32) + b_ref[rows, :].astype(F32)).astype(BF)
        if tail:
            last = pl.ds(2 * half, tail)
            ref[half : half + tail, :] = (a_ref[last, :].astype(F32) + b_ref[last, :].astype(F32)).astype(BF)


def add_kernel(tail, a_ref, b_ref, out_ref, *tail_refs):
    rows = out_ref.shape[0]
    out_ref[...] = (a_ref[0:rows, :].astype(F32) + b_ref[0:rows, :].astype(F32)).astype(BF)
    if tail:
        last = slice(rows, rows + tail)
        tail_refs[0][...] = (a_ref[last, :].astype(F32) + b_ref[last, :].astype(F32)).astype(BF)


def join_kernel(index_ref, *refs):
    out = refs[-1]
    rows = refs[0].shape[0]
    for j, ref in enumerate(refs[:-1]):
        out[pl.ds(pl.multiple_of((index_ref[0] ^ j) * rows, 16), rows), :] = ref[...]


def unpack_kernel(unpack, count, index_ref, mine_ref, got_ref, *refs):
    rest = refs[: len(refs) - count - 1]
    mark_ref, *outs = refs[len(rest) :]
    mark_ref[...] = jnp.zeros(mark_ref.shape, F32)

    @pl.when(index_ref[0] == 0)
    def _():
        unpack(mine_ref, got_ref, *rest, *outs)

    @pl.when(index_ref[0] != 0)
    def _():
        unpack(got_ref, mine_ref, *rest, *outs)


def unpack_in(low_ref, high_ref, in_ref):
    half = low_ref.shape[0]
    in_ref[0:half, :] = low_ref[...].astype(F32)
    in_ref[half:, :] = high_ref[...].astype(F32)


def unpack_out(low_ref, high_ref, out_ref):
    tall = low_ref.shape[1]
    out_ref[0:tall, :] = low_ref[...].T.astype(F32)
    out_ref[tall:, :] = high_ref[...].T.astype(F32)


def unpack_tall(low_ref, high_ref, out_ref):
    half = out_ref.shape[1]
    width = 2 * half
    out_ref[0:half, :] = high_ref[:, width : width + half].astype(F32)
    out_ref[half:width, :] = high_ref[:, width + half :].astype(F32)


def unpack_cross(low_ref, high_ref, kv_ref, query_ref, out_ref):
    half, width = low_ref.shape[0], query_ref.shape[0]
    kv_ref[:, 0:half] = low_ref[:, 0:width].T.astype(F32)
    kv_ref[:, half:] = high_ref[:, 0:width].T.astype(F32)
    query_ref[...] = low_ref[:, width:].T.astype(F32)
    unpack_tall(low_ref, high_ref, out_ref)


def unpack_self(low_ref, high_ref, small_ref, qkv_ref, out_ref, gain_ref, bias_ref, table_ref):
    half, width = low_ref.shape[0], qkv_ref.shape[0]
    qkv_ref[:, 0:half] = low_ref[:, 0:width].T.astype(F32)
    qkv_ref[:, half:width] = high_ref[:, 0:width].T.astype(F32)
    qkv_ref[:, width:] = low_ref[:, width:].T.astype(F32)
    unpack_tall(low_ref, high_ref, out_ref)
    small = small_ref[:, 0 : gain_ref.shape[1]].astype(F32)
    gain_ref[...] = small[0:3]
    bias_ref[...] = small[3:6]
    table_ref[...] = small[8:16]


def place_kernel(numbers_ref, out_own, genc_own, gin_own, got_cross, got_self, *outs):
    place = numbers_ref[0]
    half, width = out_own.shape[1:]
    first = width + 16
    others = (got_cross, width + half), (got_cross, width), (got_self, first)
    for own_ref, (got_ref, at), out_ref in zip((out_own, genc_own, gin_own), others, outs):
        out_ref[place] = own_ref[...]
        for sentence in range(2):
            out_ref[1 - place, sentence] = got_ref[at : at + half, sentence * width : (sentence + 1) * width]


def smem():
    return pl.BlockSpec(memory_space=pltpu.SMEM)


def vmem():
    return pl.BlockSpec(memory_space=pltpu.VMEM)


def call(kernel, scalars, arrays, outs, scratch=(), name=None, far=(), results=(), sems=0, after=()):
    held = [*results, *scratch]
    limit = sum(math.prod(s[:-2]) * -(-s[-2] // 16) * 16 * s[-1] * jnp.dtype(d).itemsize for s, d in held) + 6 * MIB
    taken = len(scalars) + len(arrays) + len(far)
    anywhere = pl.BlockSpec(memory_space=pl.ANY)

    def body(*refs):
        kernel(*refs[:taken], *refs[taken + len(after) :])

    return pl.pallas_call(
        body,
        out_shape=tuple(pltpu.VMEM(s, d) for s, d in outs) + tuple(jax.ShapeDtypeStruct(s, d) for s, d in results),
        in_specs=[smem() for _ in scalars]
        + [vmem() for _ in arrays]
        + [pl.BlockSpec(memory_space=pltpu.HBM) for _ in far]
        + [anywhere for _ in after],
        out_specs=tuple(vmem() for _ in (*outs, *results)),
        scratch_shapes=[pltpu.VMEM(s, d) for s, d in scratch] + ([pltpu.SemaphoreType.DMA((sems,))] if sems else []),
        compiler_params=pltpu.CompilerParams(vmem_limit_bytes=limit),
        cost_estimate=pl.CostEstimate(**COST.get(name, SMALL_COST), transcendentals=0),
        name=name,
    )(
        *scalars,
        *(pltpu.with_memory_space_constraint(a, pltpu.VMEM) for a in arrays),
        *(pltpu.with_memory_space_constraint(a, pltpu.HBM) for a in far),
        *after,
    )


def local(
    dec_in, enc_out, out_grad, tgt_len, src_len, pair_id,
    self_qkv, self_out, cross_q, cross_kv, cross_out, ff_in, ff_out, norm_gain, norm_bias, lang_table,
):
    micro_count, sent_count, local_len, width = dec_in.shape
    seq_count = lax.axis_size("seq")
    dp_count = lax.axis_size("dp")
    place = lax.axis_index("seq")
    dp_place = lax.axis_index("dp")
    inner = ff_in.shape[1]
    length = local_len * seq_count
    tokens = sent_count * length
    half = width // 2
    mine = jnp.arange(micro_count) == place
    numbers = jnp.concatenate(
        [
            place.reshape(1),
            jnp.sum(jnp.where(mine, pair_id, 0)).reshape(1),
            jnp.sum(jnp.where(mine[:, None], tgt_len, 0), 0),
            jnp.sum(jnp.where(mine[:, None], src_len, 0), 0),
        ]
    ).astype(jnp.int32)
    swap = [(0, 1), (1, 0)]

    dec2 = lax.ppermute(dec_in, "seq", swap)
    enc2 = lax.ppermute(enc_out, "seq", swap)
    og2 = lax.ppermute(out_grad, "seq", swap)

    rows = (sent_count, local_len, width)
    whole = (tokens, width)
    probs = (sent_count * HEADS, length, length)
    sums = (sent_count * HEADS, 1, length)
    turned = (width, tokens)
    buffer = (width, LANES)
    like = lambda a: (a.shape, a.dtype)
    params = Weights(
        lang_table, self_qkv, norm_gain, norm_bias, cross_kv, self_out, cross_q, cross_out, ff_in, ff_out
    )
    kinds = Kept(
        out_own=(rows, BF),
        out_oth=((local_len, LANES), BF),
        send_out=(buffer, BF),
        gff=(whole, BF),
        gff_t=(turned, BF),
        hidden=((tokens, inner), BF),
        slope=((tokens, inner), BF),
        slow_t=(turned, BF),
        ginner=((length, inner), BF),
        third=(whole, F32),
        xhat2=(whole, F32),
        rstd2=((tokens, 128), F32),
        elow=(whole, BF),
        qkv=((tokens, 3 * width), BF),
        p_self=(probs, BF),
        rl_self=(sums, F32),
        att_t=(turned, BF),
        xhat1=(whole, F32),
        rstd1=((tokens, 128), F32),
        flow=(whole, BF),
        encs=(whole, BF),
        cq=(whole, BF),
        ckv=((tokens, 2 * width), BF),
        p_cross=(probs, BF),
        rl_cross=(sums, F32),
        crossed_t=(turned, BF),
        dnorm=((8, width), F32),
        w_qkv=like(self_qkv),
        w_gain=like(norm_gain),
        w_ckv=like(cross_kv),
        w_so=like(self_out),
        w_cq=like(cross_q),
        w_co=like(cross_out),
        w_fi=like(ff_in),
        w_fo=like(ff_out),
    )
    kept = call(
        forward_kernel,
        (numbers,),
        (dec2, enc2, og2),
        list(kinds),
        [
            like(lang_table), like(norm_bias), (whole, BF), (whole, BF), ((4, length, length), F32), (whole, BF),
            (whole, BF), (whole, BF),
        ],
        name="forward",
        far=(dec_in, enc_out, out_grad, *params),
        sems=32,
    )
    held = SimpleNamespace(**Kept(*kept)._asdict())

    def flips(core_zero, core_one):
        return [(2 * d, 2 * (d ^ core_zero)) for d in range(dp_count)] + [
            (2 * d + 1, 2 * (d ^ core_one) + 1) for d in range(dp_count)
        ]

    def travel(array, core_zero, core_one):
        return lax.ppermute(array, ("dp", "seq"), flips(core_zero, core_one))

    last = []

    def reduce_all(keep, got, outs, unpack, route, tail=0):
        def run(kernel, scalars, arrays, outs, name, results=()):
            got = call(kernel, scalars, arrays, outs, name=name, results=results, after=tuple(last))
            last[:] = [got[0]]
            return got

        rows, lanes = keep.shape
        body = rows - tail
        if dp_count != 16:
            (total,) = run(functools.partial(add_kernel, 0), (), (keep, got), [((rows, lanes), BF)], "add_core")
            total = lax.psum(total, "dp")
            mine, other = total[: body // 2], total[body // 2 : body]
            rest = (total[body:],) if tail else ()
            bit = jnp.zeros((1,), jnp.int32)
            for _ in range(2 * len(route) - 1):
                yield
        else:
            bits = [
                (jnp.where(place == 0, dp_place & zero, dp_place & one) != 0).astype(jnp.int32).reshape(1)
                for zero, one in route
            ]
            held = body
            for bit, flip in zip(bits, route[:-1]):
                held //= 2
                shape = (held + tail, lanes)
                send, keep = run(functools.partial(add_split_kernel, tail), (bit,), (keep, got), [(shape, BF)] * 2, "add_split")
                got = travel(send, *flip)
                yield
            (keep,) = run(functools.partial(add_kernel, 0), (), (keep, got), [(shape, BF)], "add_all")
            got = travel(keep, *route[-1])
            yield
            pieces = [((held, lanes), BF)] + ([((tail, lanes), BF)] if tail else [])
            mine, *rest = run(functools.partial(add_kernel, tail), (), (keep, got), pieces, "add_last")
            for bit, flip in zip(bits[1:-1][::-1], route[1:-1][::-1]):
                other = travel(mine, *flip)
                yield
                held *= 2
                (mine,) = run(join_kernel, (bit,), (mine, other), [((held, lanes), BF)], "join")
            other = travel(mine, *route[0])
            bit = bits[0]
            yield
        _, *unpacked = run(
            functools.partial(unpack_kernel, unpack, len(outs)),
            (bit,),
            (mine, other, *rest),
            [((8, 128), F32)],
            "unpack",
            [(s, F32) for s in outs],
        )
        yield unpacked

    last[:] = [held.dnorm]

    def feed_back():
        send, held.keep_out, held.ginner_last = call(
            feed_kernel,
            (numbers,),
            [held.gff, held.w_fo, held.slope, held.slow_t, held.gff_t, held.hidden, held.ginner],
            [(buffer, BF), (buffer, BF), ((length, inner), BF)],
            name="feed_back",
            after=last,
        )
        last[:] = [send]
        held.got_in = lax.ppermute(send, "seq", swap)
        groups["F"] = reduce_all(held.keep_out, held.got_out, [(inner, half)], unpack_out, ROUTES["F"])

    def feed_keep():
        (keep,) = call(
            feed_keep_kernel,
            (numbers,),
            [held.slow_t, held.ginner, held.ginner_last],
            [(buffer, BF)],
            name="feed_keep",
            after=last,
        )
        last[:] = [keep]
        groups["f"] = reduce_all(keep, held.got_in, [(width, inner // 2)], unpack_in, ROUTES["f"])

    def cross_back():
        held.cross_branch, held.gq_t, held.gkv_t, held.gfs, held.dnorm = (
            call(
                cross_kernel,
                (),
                [
                    held.third, held.ginner, held.ginner_last, held.w_fi, held.xhat2, held.rstd2, held.dnorm, held.w_gain,
                    held.w_co, held.w_cq, held.ckv, held.cq, held.p_cross, held.rl_cross, held.crossed_t, held.xhat1,
                    held.rstd1,
                ],
                [(whole, BF), (turned, BF), ((2 * width, tokens), BF), (whole, F32), ((8, width), F32)],
                [(turned, BF), (whole, F32)],
                name="cross",
                after=last,
            )
        )
        last[:] = [held.gfs]

    def cross_grads():
        longer = (width + 2 * local_len, LANES)
        send, keep, held.genc_own = call(
            cross_grads_kernel,
            (numbers,),
            [held.cross_branch, held.gq_t, held.gkv_t, held.crossed_t, held.flow, held.encs, held.w_ckv, held.out_oth],
            [(longer, BF), (buffer, BF), (rows, BF)],
            [(whole, BF)],
            name="cross_grads",
            after=last,
        )
        last[:] = [send]
        held.got_cross = lax.ppermute(send, "seq", swap)
        groups["x"] = reduce_all(
            keep, held.got_cross, [(width, width), (width, half), (width, half)], unpack_cross, ROUTES["x"]
        )

    def self_back():
        held.self_branch, held.gqkv_t = (
            call(
                self_kernel,
                (),
                [held.gfs, held.w_so, held.qkv, held.p_self, held.rl_self, held.att_t],
                [(whole, BF), ((3 * width, tokens), BF)],
                [(turned, BF)],
                name="self",
                after=last,
            )
        )
        last[:] = [held.self_branch]

    def self_grads():
        longer = (width + 16 + local_len, LANES)
        send, keep, held.gin_own = call(
            self_grads_kernel,
            (numbers,),
            [held.gfs, held.dnorm, held.self_branch, held.gqkv_t, held.att_t, held.elow, held.w_qkv],
            [(longer, BF), ((width + 16, LANES), BF), (rows, BF)],
            [(whole, BF), ((16, width), F32)],
            name="self_grads",
            after=last,
        )
        last[:] = [send]
        held.got_self = lax.ppermute(send, "seq", swap)
        results = [(width, 3 * half), (width, half), (3, half), (3, half), (8, half)]
        groups["s"] = reduce_all(keep, held.got_self, results, unpack_self, ROUTES["s"], tail=16)

    def place_all():
        held.placed = call(
            place_kernel,
            (numbers,),
            [held.out_own, held.genc_own, held.gin_own, held.got_cross, held.got_self],
            [],
            name="place",
            results=[(dec_in.shape, BF)] * 3,
            after=last,
        )

    groups = {}
    held.got_out = lax.ppermute(held.send_out, "seq", swap)
    kernels = {"J": feed_back, "K": feed_keep, "X": cross_back, "G": cross_grads, "S": self_back, "T": self_grads, "P": place_all}
    sums = {}
    for letter in ORDER:
        if letter in kernels:
            kernels[letter]()
        else:
            sums[letter] = next(groups[letter])
    (g_ff_in,), (g_ff_out,) = sums["f"], sums["F"]
    g_cross_kv, g_cross_q, g_cross_out = sums["x"]
    g_qkv, g_self_out, g_gain, g_bias, g_table = sums["s"]
    output, grad_encoder, grad_input = held.placed
    return (
        output,
        grad_input,
        grad_encoder,
        g_qkv,
        g_self_out,
        g_cross_q,
        g_cross_kv,
        g_cross_out,
        g_ff_in,
        g_ff_out,
        g_gain,
        g_bias,
        g_table,
    )


def solution(mesh):
    acts = P(None, "dp", "seq", None)
    lens = P(None, "dp")
    cut = P(None, "seq")
    return jax.shard_map(
        local,
        mesh=mesh,
        in_specs=(acts, acts, acts, lens, lens) + (P(),) * 11,
        out_specs=(acts, acts, acts) + (cut,) * 10,
        check_vma=False,
    )
```

```python
import functools
import math
from types import SimpleNamespace
from typing import Any, NamedTuple

import jax
import jax.numpy as jnp
from jax import lax
from jax.experimental import pallas as pl
from jax.experimental.pallas import tpu as pltpu
from jax.sharding import PartitionSpec as P

HEADS = 8
NORM_EPS = 1e-05
NEG_FILL = -1e30
BF = jnp.bfloat16
F32 = jnp.float32
MIB = 1 << 20
ORDER = "JFKfXGSfxTFfsxfFsFxsxfsPFfxFsxfsFxfsxFs"
PLANE_FIRST = ((1, 2), (2, 1), (4, 4), (8, 8))
BETWEEN = ((1, 2), (4, 4), (2, 1), (8, 8))
LINE_FIRST = ((4, 4), (1, 2), (2, 1), (8, 8))
ROUTES = {"f": BETWEEN, "F": LINE_FIRST, "x": BETWEEN, "s": PLANE_FIRST}
SMALL_COST = {"flops": 20_000_000_000, "bytes_accessed": 400_000_000}
COST = {
    name: {"flops": 100_000_000_000, "bytes_accessed": 1000}
    for name in ("forward", "feed_back", "feed_keep", "cross", "cross_grads", "self", "self_grads")
}
LANES = 1024


def mm(a, b):
    return lax.dot_general(a, b, (((1,), (0,)), ((), ())), preferred_element_type=F32)


def mm_bt(a, b):
    return lax.dot_general(a, b, (((1,), (1,)), ((), ())), preferred_element_type=F32)


def norm_forward(values, gain, bias):
    center = values - jnp.mean(values, -1, keepdims=True)
    rstd = lax.rsqrt(jnp.mean(center * center, -1, keepdims=True) + NORM_EPS)
    xhat = center * rstd
    return xhat, rstd, xhat * gain + bias


def norm_backward(xhat, rstd, gain, upstream):
    scaled = upstream * gain
    first = jnp.mean(scaled, -1, keepdims=True)
    second = jnp.mean(scaled * xhat, -1, keepdims=True)
    grad = rstd * (scaled - first - xhat * second)
    return grad, jnp.sum(upstream * xhat, 0, keepdims=True), jnp.sum(upstream, 0, keepdims=True)


def lane_half(shape, half):
    lane = lax.broadcasted_iota(jnp.int32, shape, 1)
    return (lane < 64) if half == 0 else (lane >= 64)


def weave(*lists):
    steps = [((i + 0.5) / len(some), k, step) for k, some in enumerate(lists) for i, step in enumerate(some)]
    for _, _, step in sorted(steps, key=lambda item: item[:2]):
        step()


def staged(count, *stages):
    held = {}

    def step(stage, item):
        def run():
            held[item] = stages[stage](item, held.get(item))

        return run

    return [
        step(k, t - k) for t in range(count + len(stages) - 1) for k in range(len(stages)) if 0 <= t - k < count
    ]


def attend_steps(sentence, length, q_ref, k_ref, v_ref, k_at, v_at, bias_ref, p_ref, rl_ref, out_ref, out_t):
    rows = pl.ds(sentence * length, length)

    def score(pair, _):
        queries = q_ref[rows, pair * 128 : pair * 128 + 128]
        keys = k_ref[rows, k_at + pair * 128 : k_at + pair * 128 + 128]
        zeros = jnp.zeros_like(queries)
        return [
            mm_bt(keys, jnp.where(lane_half(queries.shape, half), queries, zeros)) + bias_ref[sentence]
            for half in range(2)
        ]

    def soften(pair, scores):
        probs = []
        for half in range(2):
            top = jnp.max(scores[half], 0, keepdims=True)
            probs.append(jnp.exp(scores[half] - top).astype(BF))
            p_ref[sentence * HEADS + 2 * pair + half] = probs[half]
        return probs

    def mix(pair, probs):
        values_t = v_ref[rows, v_at + pair * 128 : v_at + pair * 128 + 128].T
        mixed = []
        for half in range(2):
            tall = jnp.concatenate([values_t[half * 64 : half * 64 + 64], jnp.ones((16, length), BF)], 0)
            both = mm(tall, probs[half])
            one_over = 1.0 / both[64:65]
            rl_ref[sentence * HEADS + 2 * pair + half] = one_over
            mixed.append(both[0:64] * one_over)
        joined = jnp.concatenate(mixed, 0).astype(BF)
        out_t[pair * 128 : pair * 128 + 128, rows] = joined
        out_ref[rows, pair * 128 : pair * 128 + 128] = joined.T

    return staged(HEADS // 2, score, soften, mix)


def attend_back_steps(
    sentence, length, q_ref, k_ref, v_ref, k_at, v_at, p_ref, rl_ref, out_t, go_t, gq_t, gk_t, gv_t, gk_at, gv_at
):
    rows = pl.ds(sentence * length, length)

    def start(pair, _):
        feats = slice(pair * 128, pair * 128 + 128)
        values = v_ref[rows, v_at + pair * 128 : v_at + pair * 128 + 128]
        mixed = out_t[feats, rows].astype(F32)
        grads = go_t[feats, rows].astype(F32)
        scaled, dots = [], []
        for half in range(2):
            part = slice(half * 64, half * 64 + 64)
            scaled.append((grads[part] * rl_ref[sentence * HEADS + 2 * pair + half]).astype(BF))
            dots.append(jnp.sum(mixed[part] * scaled[half].astype(F32), 0, keepdims=True))
        both = jnp.concatenate(scaled, 0)
        zeros = jnp.zeros_like(values)
        grad_probs = [mm(jnp.where(lane_half(values.shape, half), values, zeros), both) for half in range(2)]
        return scaled, dots, grad_probs

    def middle(pair, held):
        scaled, dots, grad_probs = held
        grad_scores = []
        for half in range(2):
            probs = p_ref[sentence * HEADS + 2 * pair + half].astype(F32)
            grad_scores.append((probs * (grad_probs[half] - dots[half])).astype(BF))
        return scaled, grad_scores

    def finish(pair, held):
        scaled, grad_scores = held
        queries_t = q_ref[rows, pair * 128 : pair * 128 + 128].T
        keys_t = k_ref[rows, k_at + pair * 128 : k_at + pair * 128 + 128].T
        gq, gk, gv = [], [], []
        for half in range(2):
            part = slice(half * 64, half * 64 + 64)
            gq.append(mm(keys_t[part], grad_scores[half]) * 0.125)
            gk.append(mm_bt(queries_t[part], grad_scores[half]))
            gv.append(mm_bt(scaled[half], p_ref[sentence * HEADS + 2 * pair + half]))
        for ref, at, grads in ((gq_t, 0, gq), (gk_t, gk_at, gk), (gv_t, gv_at, gv)):
            ref[at + pair * 128 : at + pair * 128 + 128, rows] = jnp.concatenate(grads, 0).astype(BF)

    return staged(HEADS // 2, start, middle, finish)


class Copies:
    def __init__(self, sems):
        self.sems, self.used, self.open = sems, 0, {}

    def start(self, name, source, target):
        copy = pltpu.make_async_copy(source, target, self.sems.at[self.used])
        self.used += 1
        copy.start()
        self.open.setdefault(name, []).append(copy)

    def wait(self, *names):
        for name in names or tuple(self.open):
            for copy in self.open.pop(name, ()):
                copy.wait()


def halves(place, length):
    half = length // 2
    return [
        [pl.ds(pl.multiple_of(sentence * length + which * half, half), half) for which in (place, 1 - place)]
        for sentence in range(2)
    ]


def give_out_steps(which, ref, gff_t, hidden):
    half = gff_t.shape[0] // 2

    def give(index):
        def run():
            feats = pl.ds(pl.multiple_of(which * half, half), half)
            low, at = (index // 2) * half, (index % 2) * 512
            ref[low : low + half, at : at + 512] = mm(
                gff_t[feats, :], hidden[:, index * 512 : (index + 1) * 512]
            ).astype(BF)

        return run

    return [give(index) for index in range(hidden.shape[1] // 512)]


def give_in_steps(which, ref, slow_t, ginner):
    length, inner = ginner[0].shape
    half = inner // 2

    def give(index):
        def run():
            cols = pl.ds(pl.multiple_of(which * half + index * 256, 256), 256)
            total = mm(slow_t[:, 0:length], ginner[0][:, cols]) + mm(slow_t[:, length:], ginner[1][:, cols])
            ref[:, index * 256 : (index + 1) * 256] = total.astype(BF)

        return run

    return [give(index) for index in range(half // 256)]


def feed_back_steps(gff, w_fo, slope, ginner):
    step = 256

    def shrink(index, _):
        return mm_bt(gff[...], w_fo[index * step : (index + 1) * step, :]).astype(BF)

    def bend(index, grad_hidden):
        cols = slice(index * step, (index + 1) * step)
        ginner[:, cols] = (grad_hidden.astype(F32) * slope[:, cols].astype(F32)).astype(BF)

    return staged(ginner.shape[1] // step, shrink, bend)


def feed_kernel(gff, w_fo, slope, slow_t, gff_t, hidden, ginner_first, send_in, keep_out, ginner_last):
    place = lax.axis_index("seq")
    length = ginner_last.shape[0]
    weave(
        feed_back_steps(gff.at[length:], w_fo, slope.at[length:], ginner_last),
        give_out_steps(place, keep_out, gff_t, hidden),
    )
    weave(give_in_steps(1 - place, send_in, slow_t, (ginner_first, ginner_last)))


def feed_keep_kernel(slow_t, ginner_first, ginner_last, keep_in):
    weave(give_in_steps(lax.axis_index("seq"), keep_in, slow_t, (ginner_first, ginner_last)))


class Weights(NamedTuple):
    table: Any
    qkv: Any
    gain: Any
    nbias: Any
    ckv: Any
    so: Any
    cq: Any
    co: Any
    fi: Any
    fo: Any


class Kept(NamedTuple):
    out_own: Any
    out_oth: Any
    send_out: Any
    gff: Any
    gff_t: Any
    hidden: Any
    slope: Any
    slow_t: Any
    ginner: Any
    third: Any
    xhat2: Any
    rstd2: Any
    elow: Any
    qkv: Any
    p_self: Any
    rl_self: Any
    att_t: Any
    xhat1: Any
    rstd1: Any
    flow: Any
    encs: Any
    cq: Any
    ckv: Any
    p_cross: Any
    rl_cross: Any
    crossed_t: Any
    dnorm: Any
    w_qkv: Any
    w_gain: Any
    w_ckv: Any
    w_so: Any
    w_cq: Any
    w_co: Any
    w_fi: Any
    w_fo: Any


def forward_kernel(numbers_ref, *refs):
    (dec2_in, enc2_in, og2_in, dec_in, enc_in, og_in), refs = refs[:6], refs[6:]
    weights_in, refs = Weights(*refs[: len(Weights._fields)]), refs[len(Weights._fields) :]
    kept, refs = Kept(*refs[: len(Kept._fields)]), refs[len(Kept._fields) :]
    (out_own, out_oth, send_out, gff, gff_t, hidden, slope, slow_t, ginner, third, xhat2, rstd2, elow, qkv, p_self,
     rl_self, att_t, xhat1, rstd1, flow, encs, cq, ckv, p_cross, rl_cross, crossed_t, dnorm_ref) = kept[:27]
    w = Weights(refs[0], kept.w_qkv, kept.w_gain, refs[1], *kept[29:])
    (dec_s, og_s, bias_ref, att, slow, outs, sems) = refs[2:]
    crossed = att
    at = Weights(*range(len(Weights._fields)))
    dec, enc, og = (-1, -2, -3)
    copies = Copies(sems)
    place = lax.axis_index("seq")
    tokens, width = dec_s.shape
    length = tokens // 2
    inner = hidden.shape[1]
    where = halves(place, length)
    copies.start(at.table, weights_in.table, w.table)
    for s in range(2):
        copies.start(dec, dec_in.at[place, s], dec_s.at[where[s][0]])
    parts = [slice(part * width, (part + 1) * width) for part in range(3)]
    for part in parts:
        copies.start((at.qkv, part.start), weights_in.qkv.at[:, part], w.qkv.at[:, part])
    for s in range(2):
        copies.start(enc, enc_in.at[place, s], encs.at[where[s][0]])
    for key in (at.ckv, at.so, at.gain, at.nbias, *at[6:]):
        copies.start(key, weights_in[key], w[key])
    for s in range(2):
        copies.start(og, og_in.at[place, s], og_s.at[where[s][0]])
        copies.start(og, og2_in.at[place, s], og_s.at[where[s][1]])

    rows = [slice(s * length, (s + 1) * length) for s in range(2)]
    keys_at = lax.broadcasted_iota(jnp.int32, (length, length), 0)
    query_at = lax.broadcasted_iota(jnp.int32, (length, length), 1)
    for s in range(2):
        bias_ref[s] = jnp.where((keys_at <= query_at) & (keys_at < numbers_ref[place, s]), 0.0, NEG_FILL)
        bias_ref[2 + s] = jnp.where(keys_at < numbers_ref[place, 2 + s], 0.0, NEG_FILL)

    def embed(s):
        def run():
            dec_s[where[s][1], :] = dec2_in[place, s]
            elow[rows[s]] = (dec_s[rows[s]].astype(F32) + row).astype(BF)
            encs[where[s][1], :] = enc2_in[place, s]

        return run

    def pack(s, part):
        def run():
            if s == 0:
                copies.wait((at.qkv, parts[part].start))
            values = mm(elow[rows[s]], w.qkv[:, parts[part]])
            qkv[rows[s], parts[part]] = (values * 0.125 if part == 0 else values).astype(BF)

        return run

    def pack_cross(s, part):
        def run():
            if s == 0 and part == 0:
                copies.wait(enc, at.ckv)
            ckv[rows[s], parts[part]] = mm(encs[rows[s]], w.ckv[:, parts[part]]).astype(BF)

        return run

    held = {}

    def after_self(s):
        def project():
            held[0, s] = dec_s[rows[s]].astype(F32) + row + mm(att[rows[s]], w.so[...])

        def norm():
            xhat, rstd, normed = norm_forward(held.pop((0, s)), gain[0:1], nbias[0:1])
            xhat1[rows[s]] = xhat
            rstd1[rows[s]] = jnp.broadcast_to(rstd, (length, 128))
            flow[rows[s]] = normed.astype(BF)

        def query():
            cq[rows[s]] = (mm(flow[rows[s]], w.cq[...]) * 0.125).astype(BF)

        return [project, norm, query]

    def after_cross(s):
        def project():
            held[1, s] = xhat1[rows[s]] * gain[0:1] + nbias[0:1] + mm(crossed[rows[s]], w.co[...])

        def norm():
            xhat, rstd, normed = norm_forward(held.pop((1, s)), gain[1:2], nbias[1:2])
            xhat2[rows[s]] = xhat
            rstd2[rows[s]] = jnp.broadcast_to(rstd, (length, 128))
            third[rows[s]] = normed
            slow[rows[s]] = normed.astype(BF)

        def turn():
            slow_t[:, rows[s]] = slow[rows[s]].T

        return [project, norm, turn]

    step = 256

    def feed(s):
        def grow(index, _):
            return mm(slow[rows[s]], w.fi[:, index * step : (index + 1) * step])

        def bend(index, v):
            cols = slice(index * step, (index + 1) * step)
            square = v * v
            bent = jnp.tanh(v * (0.7978845608028654 + (0.7978845608028654 * 0.044715) * square))
            half = 0.5 + 0.5 * bent
            hidden[rows[s], cols] = (v * half).astype(BF)
            rise = v * (0.7978845608028654 + (3 * 0.7978845608028654 * 0.044715) * square)
            slope[rows[s], cols] = (half + (0.5 - 0.5 * bent * bent) * rise).astype(BF)

        return staged(inner // step, grow, bend)

    gains = {}

    def after_feed(s):
        def shrink(part):
            def run():
                cols = slice(part * (width // 2), (part + 1) * (width // 2))
                third[rows[s], cols] += mm(hidden[rows[s]], w.fo[:, cols])

            return run

        def norm():
            xhat, rstd, normed = norm_forward(third[rows[s]], gain[2:3], nbias[2:3])
            outs[rows[s]] = normed.astype(BF)
            grad, *gains[2, s] = norm_backward(xhat, rstd, gain[2:3], og_s[rows[s]].astype(F32))
            third[rows[s]] = grad
            gff[rows[s]] = grad.astype(BF)

        def turn():
            gff_t[:, rows[s]] = gff[rows[s]].T
            out_own[s] = outs[where[s][0], :]
            out_oth[:, s * width : (s + 1) * width] = outs[where[s][1], :]

        return [shrink(0), shrink(1), norm, turn]

    copies.wait(at.table, dec)
    picked = lax.broadcasted_iota(jnp.int32, w.table.shape, 0) == numbers_ref[place, 4]
    row = jnp.sum(jnp.where(picked, w.table[...].astype(F32), 0.0), 0, keepdims=True)
    weave([embed(0)])
    weave([pack(0, part) for part in range(3)], [embed(1)])
    weave(
        attend_steps(0, length, qkv, qkv, qkv, width, 2 * width, bias_ref, p_self, rl_self, att, att_t),
        [pack(1, part) for part in range(3)] + [pack_cross(0, 0), pack_cross(0, 1)],
    )
    copies.wait(at.so, at.cq, at.co, at.gain, at.nbias)
    gain = w.gain[...].astype(F32)
    nbias = w.nbias[...].astype(F32)
    weave(
        attend_steps(1, length, qkv, qkv, qkv, width, 2 * width, bias_ref, p_self, rl_self, att, att_t),
        after_self(0) + [pack_cross(1, 0), pack_cross(1, 1)],
    )
    cross_bias = bias_ref.at[2:4]
    weave(
        attend_steps(0, length, cq, ckv, ckv, 0, width, cross_bias, p_cross, rl_cross, crossed, crossed_t),
        after_self(1),
    )
    copies.wait(at.fi, at.fo, og)
    weave(
        attend_steps(1, length, cq, ckv, ckv, 0, width, cross_bias, p_cross, rl_cross, crossed, crossed_t),
        after_cross(0),
    )
    weave(feed(0), after_cross(1))
    weave(feed(1), after_feed(0))
    weave(feed_back_steps(gff.at[0:length], w.fo, slope.at[0:length], ginner), after_feed(1))
    weave(give_out_steps(1 - place, send_out, gff_t, hidden))
    dnorm_ref[...] = jnp.zeros(dnorm_ref.shape, F32)
    dnorm_ref[2:3, :] = gains[2, 0][0] + gains[2, 1][0]
    dnorm_ref[5:6, :] = gains[2, 0][1] + gains[2, 1][1]
    copies.wait()


def cross_kernel(
    third, ginner_first, ginner_last, w_fi, xhat2, rstd2, dnorm_in, w_gain, w_co, w_cq, ckv, cq, p_cross, rl_cross, crossed_t, xhat1, rstd1,
    branch, gq_t, gkv_t, gfs, dnorm_ref,
    go_t, gss,
):
    tokens, width = gss.shape
    length = tokens // 2
    rows = [slice(s * length, (s + 1) * length) for s in range(2)]
    gain = w_gain[...].astype(F32)
    gains, seconds = {}, {}
    ginner = (ginner_first, ginner_last)

    def before(s):
        held = []

        def shrink(part):
            def run():
                cols = slice(part * (width // 2), (part + 1) * (width // 2))
                held.append(third[rows[s], cols] + mm_bt(ginner[s][...], w_fi[cols, :]))

            return run

        def norm():
            upstream = jnp.concatenate(held, 1)
            gss[rows[s]], *seconds[s] = norm_backward(xhat2[rows[s]], rstd2[rows[s], 0:1], gain[1:2], upstream)

        return [shrink(0), shrink(1), norm, begin(s)]

    def begin(s):
        def run():
            low = gss[rows[s]].astype(BF)
            branch[rows[s]] = low
            go_t[:, rows[s]] = mm_bt(w_co[...], low).astype(BF)

        return run

    def after(s):
        held = {}

        def query():
            held[0] = gss[rows[s]] + mm_bt(gq_t[:, rows[s]].T, w_cq[...])

        def norm():
            gfs[rows[s]], *gains[s] = norm_backward(xhat1[rows[s]], rstd1[rows[s], 0:1], gain[0:1], held[0])

        return [query, norm]

    def attention(s):
        return attend_back_steps(
            s, length, cq, ckv, ckv, 0, width, p_cross, rl_cross, crossed_t, go_t, gq_t, gkv_t, gkv_t, 0, width
        )

    weave(before(0))
    weave(attention(0), before(1))
    weave(attention(1), after(0))
    weave(after(1))
    dnorm_ref[...] = dnorm_in[...]
    for k, sums in enumerate((gains, seconds)):
        dnorm_ref[k : k + 1, :] = sums[0][0] + sums[1][0]
        dnorm_ref[3 + k : 4 + k, :] = sums[0][1] + sums[1][1]


def give_tall(which, ref, mixed_t, branch):
    width = branch.shape[1]
    half = width // 2
    cols = pl.ds(pl.multiple_of(which * half, half), half)
    grads = mm(mixed_t[...], branch[:, cols]).astype(BF)
    ref[half:width, width : width + half] = grads[0:half]
    ref[half:width, width + half :] = grads[half:]


def cross_grads_kernel(
    branch, gq_t, gkv_t, crossed_t, flow, encs, w_ckv, out_oth, send_ref, keep_ref, genc_own, genc
):
    place = lax.axis_index("seq")
    tokens, width = branch.shape
    length = tokens // 2
    half = width // 2
    where = halves(place, length)

    def give(which, ref):
        def out():
            give_tall(which, ref, crossed_t, branch)

        def query():
            feats = pl.ds(pl.multiple_of(which * half, half), half)
            ref[0:half, width:] = mm(gq_t[feats, :], flow[...]).astype(BF)

        def pair():
            feats = pl.ds(pl.multiple_of(which * width, half), width)
            ref[0:width, 0:width] = mm(gkv_t[feats, :], encs[...]).astype(BF)

        return [out, query, pair]

    def encoder(s):
        def run():
            rows = slice(s * length, (s + 1) * length)
            genc[rows] = mm(w_ckv[...], gkv_t[:, rows]).astype(BF).T
            genc_own[s] = genc[where[s][0], :]
            send_ref[width : width + length // 2, s * width : (s + 1) * width] = genc[where[s][1], :]

        return run

    weave(give(1 - place, send_ref) + give(place, keep_ref), [encoder(0), encoder(1)])
    send_ref[width + length // 2 :, :] = out_oth[...]


def self_kernel(gfs, w_so, qkv, p_self, rl_self, att_t, branch, gqkv_t, go_t):
    tokens, width = gfs.shape
    length = tokens // 2
    rows = [slice(s * length, (s + 1) * length) for s in range(2)]

    def begin(s):
        def run():
            low = gfs[rows[s]].astype(BF)
            branch[rows[s]] = low
            go_t[:, rows[s]] = mm_bt(w_so[...], low).astype(BF)

        return run

    def attention(s):
        return attend_back_steps(
            s, length, qkv, qkv, qkv, width, 2 * width, p_self, rl_self, att_t, go_t, gqkv_t, gqkv_t, gqkv_t,
            width, 2 * width,
        )

    begin(0)()
    weave(attention(0), [begin(1)])
    weave(attention(1))


def self_grads_kernel(
    numbers_ref, gfs, dnorm_in, branch, gqkv_t, att_t, elow, w_qkv,
    send_ref, keep_ref, gin_own,
    gin, small,
):
    place = lax.axis_index("seq")
    tokens, width = gfs.shape
    length = tokens // 2
    half = width // 2
    where = halves(place, length)
    sums, held = {}, {}

    def give(which, ref):
        def out():
            give_tall(which, ref, att_t, branch)

        def part(index):
            def run():
                feats = pl.ds(pl.multiple_of(which * 3 * half + index * half, half), half)
                low, at = ((0, 0), (half, 0), (0, width))[index]
                ref[low : low + half, at : at + width] = mm(gqkv_t[feats, :], elow[...]).astype(BF)

            return run

        return [out, part(0), part(1), part(2)]

    def back(s):
        rows = slice(s * length, (s + 1) * length)

        def start():
            held[s] = mm(w_qkv[...], gqkv_t[:, rows])

        def finish():
            total = gfs[rows] + held.pop(s).T
            gin[rows] = total.astype(BF)
            sums[s] = jnp.sum(total, 0, keepdims=True)
            gin_own[s] = gin[where[s][0], :]
            send_ref[width + 16 :, s * width : (s + 1) * width] = gin[where[s][1], :]

        return [start, finish]

    weave(give(1 - place, send_ref) + give(place, keep_ref), back(0) + back(1))
    small[0:8, :] = dnorm_in[...]
    picked = lax.broadcasted_iota(jnp.int32, (8, width), 0) == numbers_ref[place, 4]
    small[8:16, :] = jnp.where(picked, jnp.broadcast_to(sums[0] + sums[1], (8, width)), 0.0)
    for which, ref in ((1 - place, send_ref), (place, keep_ref)):
        ref[width : width + 16, :] = jnp.zeros((16, ref.shape[1]), BF)
        ref[width : width + 16, 0:half] = small[:, pl.ds(pl.multiple_of(which * half, half), half)].astype(BF)


def add_split_kernel(tail, bit_ref, a_ref, b_ref, send_ref, keep_ref):
    half = send_ref.shape[0] - tail
    bit = bit_ref[0]
    for which, ref in ((1 - bit, send_ref), (bit, keep_ref)):
        rows = pl.ds(pl.multiple_of(which * half, 16), half)
        ref[0:half, :] = (a_ref[rows, :].astype(F32) + b_ref[rows, :].astype(F32)).astype(BF)
        if tail:
            last = pl.ds(2 * half, tail)
            ref[half : half + tail, :] = (a_ref[last, :].astype(F32) + b_ref[last, :].astype(F32)).astype(BF)


def add_kernel(tail, a_ref, b_ref, out_ref, *tail_refs):
    rows = out_ref.shape[0]
    out_ref[...] = (a_ref[0:rows, :].astype(F32) + b_ref[0:rows, :].astype(F32)).astype(BF)
    if tail:
        last = slice(rows, rows + tail)
        tail_refs[0][...] = (a_ref[last, :].astype(F32) + b_ref[last, :].astype(F32)).astype(BF)


def join_kernel(index_ref, *refs):
    out = refs[-1]
    rows = refs[0].shape[0]
    for j, ref in enumerate(refs[:-1]):
        out[pl.ds(pl.multiple_of((index_ref[0] ^ j) * rows, 16), rows), :] = ref[...]


def unpack_kernel(unpack, count, index_ref, mine_ref, got_ref, *refs):
    rest = refs[: len(refs) - count - 1]
    mark_ref, *outs = refs[len(rest) :]
    mark_ref[...] = jnp.zeros(mark_ref.shape, F32)

    @pl.when(index_ref[0] == 0)
    def _():
        unpack(mine_ref, got_ref, *rest, *outs)

    @pl.when(index_ref[0] != 0)
    def _():
        unpack(got_ref, mine_ref, *rest, *outs)


def unpack_in(low_ref, high_ref, in_ref):
    half = low_ref.shape[0]
    in_ref[0:half, :] = low_ref[...].astype(F32)
    in_ref[half:, :] = high_ref[...].astype(F32)


def unpack_out(low_ref, high_ref, out_ref):
    tall = low_ref.shape[1]
    out_ref[0:tall, :] = low_ref[...].T.astype(F32)
    out_ref[tall:, :] = high_ref[...].T.astype(F32)


def unpack_tall(low_ref, high_ref, out_ref):
    half = out_ref.shape[1]
    width = 2 * half
    out_ref[0:half, :] = high_ref[:, width : width + half].astype(F32)
    out_ref[half:width, :] = high_ref[:, width + half :].astype(F32)


def unpack_cross(low_ref, high_ref, kv_ref, query_ref, out_ref):
    half, width = low_ref.shape[0], query_ref.shape[0]
    kv_ref[:, 0:half] = low_ref[:, 0:width].T.astype(F32)
    kv_ref[:, half:] = high_ref[:, 0:width].T.astype(F32)
    query_ref[...] = low_ref[:, width:].T.astype(F32)
    unpack_tall(low_ref, high_ref, out_ref)


def unpack_self(low_ref, high_ref, small_ref, qkv_ref, out_ref, gain_ref, bias_ref, table_ref):
    half, width = low_ref.shape[0], qkv_ref.shape[0]
    qkv_ref[:, 0:half] = low_ref[:, 0:width].T.astype(F32)
    qkv_ref[:, half:width] = high_ref[:, 0:width].T.astype(F32)
    qkv_ref[:, width:] = low_ref[:, width:].T.astype(F32)
    unpack_tall(low_ref, high_ref, out_ref)
    small = small_ref[:, 0 : gain_ref.shape[1]].astype(F32)
    gain_ref[...] = small[0:3]
    bias_ref[...] = small[3:6]
    table_ref[...] = small[8:16]


def place_kernel(out_own, genc_own, gin_own, got_cross, got_self, *outs):
    place = lax.axis_index("seq")
    half, width = out_own.shape[1:]
    first = width + 16
    others = (got_cross, width + half), (got_cross, width), (got_self, first)
    for own_ref, (got_ref, at), out_ref in zip((out_own, genc_own, gin_own), others, outs):
        out_ref[place] = own_ref[...]
        for sentence in range(2):
            out_ref[1 - place, sentence] = got_ref[at : at + half, sentence * width : (sentence + 1) * width]


def smem():
    return pl.BlockSpec(memory_space=pltpu.SMEM)


def vmem():
    return pl.BlockSpec(memory_space=pltpu.VMEM)


def call(kernel, scalars, arrays, outs, scratch=(), name=None, far=(), results=(), sems=0, after=()):
    held = [*results, *scratch]
    limit = sum(math.prod(s[:-2]) * -(-s[-2] // 16) * 16 * s[-1] * jnp.dtype(d).itemsize for s, d in held) + 6 * MIB
    taken = len(scalars) + len(arrays) + len(far)
    anywhere = pl.BlockSpec(memory_space=pl.ANY)

    def body(*refs):
        kernel(*refs[:taken], *refs[taken + len(after) :])

    return pl.pallas_call(
        body,
        out_shape=tuple(pltpu.VMEM(s, d) for s, d in outs) + tuple(jax.ShapeDtypeStruct(s, d) for s, d in results),
        in_specs=[smem() for _ in scalars]
        + [vmem() for _ in arrays]
        + [pl.BlockSpec(memory_space=pltpu.HBM) for _ in far]
        + [anywhere for _ in after],
        out_specs=tuple(vmem() for _ in (*outs, *results)),
        scratch_shapes=[pltpu.VMEM(s, d) for s, d in scratch] + ([pltpu.SemaphoreType.DMA((sems,))] if sems else []),
        compiler_params=pltpu.CompilerParams(vmem_limit_bytes=limit),
        cost_estimate=pl.CostEstimate(**COST.get(name, SMALL_COST), transcendentals=0),
        name=name,
    )(
        *scalars,
        *(pltpu.with_memory_space_constraint(a, pltpu.VMEM) for a in arrays),
        *(pltpu.with_memory_space_constraint(a, pltpu.HBM) for a in far),
        *after,
    )


def local(
    dec_in, enc_out, out_grad, tgt_len, src_len, pair_id,
    self_qkv, self_out, cross_q, cross_kv, cross_out, ff_in, ff_out, norm_gain, norm_bias, lang_table,
):
    micro_count, sent_count, local_len, width = dec_in.shape
    seq_count = lax.axis_size("seq")
    dp_count = lax.axis_size("dp")
    place = lax.axis_index("seq")
    dp_place = lax.axis_index("dp")
    inner = ff_in.shape[1]
    length = local_len * seq_count
    tokens = sent_count * length
    half = width // 2
    pairs = lax.broadcast_in_dim(pair_id, (micro_count, 1), (0,))
    numbers = jnp.concatenate([tgt_len, src_len, pairs], 1).astype(jnp.int32)
    swap = [(0, 1), (1, 0)]

    dec2 = lax.ppermute(dec_in, "seq", swap)
    enc2 = lax.ppermute(enc_out, "seq", swap)
    og2 = lax.ppermute(out_grad, "seq", swap)

    rows = (sent_count, local_len, width)
    whole = (tokens, width)
    probs = (sent_count * HEADS, length, length)
    sums = (sent_count * HEADS, 1, length)
    turned = (width, tokens)
    buffer = (width, LANES)
    like = lambda a: (a.shape, a.dtype)
    params = Weights(
        lang_table, self_qkv, norm_gain, norm_bias, cross_kv, self_out, cross_q, cross_out, ff_in, ff_out
    )
    kinds = Kept(
        out_own=(rows, BF),
        out_oth=((local_len, LANES), BF),
        send_out=(buffer, BF),
        gff=(whole, BF),
        gff_t=(turned, BF),
        hidden=((tokens, inner), BF),
        slope=((tokens, inner), BF),
        slow_t=(turned, BF),
        ginner=((length, inner), BF),
        third=(whole, F32),
        xhat2=(whole, F32),
        rstd2=((tokens, 128), F32),
        elow=(whole, BF),
        qkv=((tokens, 3 * width), BF),
        p_self=(probs, BF),
        rl_self=(sums, F32),
        att_t=(turned, BF),
        xhat1=(whole, F32),
        rstd1=((tokens, 128), F32),
        flow=(whole, BF),
        encs=(whole, BF),
        cq=(whole, BF),
        ckv=((tokens, 2 * width), BF),
        p_cross=(probs, BF),
        rl_cross=(sums, F32),
        crossed_t=(turned, BF),
        dnorm=((8, width), F32),
        w_qkv=like(self_qkv),
        w_gain=like(norm_gain),
        w_ckv=like(cross_kv),
        w_so=like(self_out),
        w_cq=like(cross_q),
        w_co=like(cross_out),
        w_fi=like(ff_in),
        w_fo=like(ff_out),
    )
    kept = call(
        forward_kernel,
        (numbers,),
        (dec2, enc2, og2),
        list(kinds),
        [
            like(lang_table), like(norm_bias), (whole, BF), (whole, BF), ((4, length, length), F32), (whole, BF),
            (whole, BF), (whole, BF),
        ],
        name="forward",
        far=(dec_in, enc_out, out_grad, *params),
        sems=32,
    )
    held = SimpleNamespace(**Kept(*kept)._asdict())

    def flips(core_zero, core_one):
        return [(2 * d, 2 * (d ^ core_zero)) for d in range(dp_count)] + [
            (2 * d + 1, 2 * (d ^ core_one) + 1) for d in range(dp_count)
        ]

    def travel(array, core_zero, core_one):
        return lax.ppermute(array, ("dp", "seq"), flips(core_zero, core_one))

    last = []

    def reduce_all(keep, got, outs, unpack, route, tail=0):
        def run(kernel, scalars, arrays, outs, name, results=()):
            got = call(kernel, scalars, arrays, outs, name=name, results=results, after=tuple(last))
            last[:] = [got[0]]
            return got

        rows, lanes = keep.shape
        body = rows - tail
        if dp_count != 16:
            (total,) = run(functools.partial(add_kernel, 0), (), (keep, got), [((rows, lanes), BF)], "add_core")
            total = lax.psum(total, "dp")
            mine, other = total[: body // 2], total[body // 2 : body]
            rest = (total[body:],) if tail else ()
            bit = jnp.zeros((1,), jnp.int32)
            for _ in range(2 * len(route) - 1):
                yield
        else:
            bits = [
                (jnp.where(place == 0, dp_place & zero, dp_place & one) != 0).astype(jnp.int32).reshape(1)
                for zero, one in route
            ]
            held = body
            for bit, flip in zip(bits, route[:-1]):
                held //= 2
                shape = (held + tail, lanes)
                send, keep = run(functools.partial(add_split_kernel, tail), (bit,), (keep, got), [(shape, BF)] * 2, "add_split")
                got = travel(send, *flip)
                yield
            (keep,) = run(functools.partial(add_kernel, 0), (), (keep, got), [(shape, BF)], "add_all")
            got = travel(keep, *route[-1])
            yield
            pieces = [((held, lanes), BF)] + ([((tail, lanes), BF)] if tail else [])
            mine, *rest = run(functools.partial(add_kernel, tail), (), (keep, got), pieces, "add_last")
            for bit, flip in zip(bits[1:-1][::-1], route[1:-1][::-1]):
                other = travel(mine, *flip)
                yield
                held *= 2
                (mine,) = run(join_kernel, (bit,), (mine, other), [((held, lanes), BF)], "join")
            other = travel(mine, *route[0])
            bit = bits[0]
            yield
        _, *unpacked = run(
            functools.partial(unpack_kernel, unpack, len(outs)),
            (bit,),
            (mine, other, *rest),
            [((8, 128), F32)],
            "unpack",
            [(s, F32) for s in outs],
        )
        yield unpacked

    last[:] = [held.dnorm]

    def feed_back():
        send, held.keep_out, held.ginner_last = call(
            feed_kernel,
            (),
            [held.gff, held.w_fo, held.slope, held.slow_t, held.gff_t, held.hidden, held.ginner],
            [(buffer, BF), (buffer, BF), ((length, inner), BF)],
            name="feed_back",
            after=last,
        )
        last[:] = [send]
        held.got_in = lax.ppermute(send, "seq", swap)
        groups["F"] = reduce_all(held.keep_out, held.got_out, [(inner, half)], unpack_out, ROUTES["F"])

    def feed_keep():
        (keep,) = call(
            feed_keep_kernel,
            (),
            [held.slow_t, held.ginner, held.ginner_last],
            [(buffer, BF)],
            name="feed_keep",
            after=last,
        )
        last[:] = [keep]
        groups["f"] = reduce_all(keep, held.got_in, [(width, inner // 2)], unpack_in, ROUTES["f"])

    def cross_back():
        held.cross_branch, held.gq_t, held.gkv_t, held.gfs, held.dnorm = (
            call(
                cross_kernel,
                (),
                [
                    held.third, held.ginner, held.ginner_last, held.w_fi, held.xhat2, held.rstd2, held.dnorm, held.w_gain,
                    held.w_co, held.w_cq, held.ckv, held.cq, held.p_cross, held.rl_cross, held.crossed_t, held.xhat1,
                    held.rstd1,
                ],
                [(whole, BF), (turned, BF), ((2 * width, tokens), BF), (whole, F32), ((8, width), F32)],
                [(turned, BF), (whole, F32)],
                name="cross",
                after=last,
            )
        )
        last[:] = [held.gfs]

    def cross_grads():
        longer = (width + 2 * local_len, LANES)
        send, keep, held.genc_own = call(
            cross_grads_kernel,
            (),
            [held.cross_branch, held.gq_t, held.gkv_t, held.crossed_t, held.flow, held.encs, held.w_ckv, held.out_oth],
            [(longer, BF), (buffer, BF), (rows, BF)],
            [(whole, BF)],
            name="cross_grads",
            after=last,
        )
        last[:] = [send]
        held.got_cross = lax.ppermute(send, "seq", swap)
        groups["x"] = reduce_all(
            keep, held.got_cross, [(width, width), (width, half), (width, half)], unpack_cross, ROUTES["x"]
        )

    def self_back():
        held.self_branch, held.gqkv_t = (
            call(
                self_kernel,
                (),
                [held.gfs, held.w_so, held.qkv, held.p_self, held.rl_self, held.att_t],
                [(whole, BF), ((3 * width, tokens), BF)],
                [(turned, BF)],
                name="self",
                after=last,
            )
        )
        last[:] = [held.self_branch]

    def self_grads():
        longer = (width + 16 + local_len, LANES)
        send, keep, held.gin_own = call(
            self_grads_kernel,
            (numbers,),
            [held.gfs, held.dnorm, held.self_branch, held.gqkv_t, held.att_t, held.elow, held.w_qkv],
            [(longer, BF), ((width + 16, LANES), BF), (rows, BF)],
            [(whole, BF), ((16, width), F32)],
            name="self_grads",
            after=last,
        )
        last[:] = [send]
        held.got_self = lax.ppermute(send, "seq", swap)
        results = [(width, 3 * half), (width, half), (3, half), (3, half), (8, half)]
        groups["s"] = reduce_all(keep, held.got_self, results, unpack_self, ROUTES["s"], tail=16)

    def place_all():
        held.placed = call(
            place_kernel,
            (),
            [held.out_own, held.genc_own, held.gin_own, held.got_cross, held.got_self],
            [],
            name="place",
            results=[(dec_in.shape, BF)] * 3,
            after=last,
        )

    groups = {}
    held.got_out = lax.ppermute(held.send_out, "seq", swap)
    kernels = {"J": feed_back, "K": feed_keep, "X": cross_back, "G": cross_grads, "S": self_back, "T": self_grads, "P": place_all}
    sums = {}
    for letter in ORDER:
        if letter in kernels:
            kernels[letter]()
        else:
            sums[letter] = next(groups[letter])
    (g_ff_in,), (g_ff_out,) = sums["f"], sums["F"]
    g_cross_kv, g_cross_q, g_cross_out = sums["x"]
    g_qkv, g_self_out, g_gain, g_bias, g_table = sums["s"]
    output, grad_encoder, grad_input = held.placed
    return (
        output,
        grad_input,
        grad_encoder,
        g_qkv,
        g_self_out,
        g_cross_q,
        g_cross_kv,
        g_cross_out,
        g_ff_in,
        g_ff_out,
        g_gain,
        g_bias,
        g_table,
    )


def solution(mesh):
    acts = P(None, "dp", "seq", None)
    lens = P(None, "dp")
    cut = P(None, "seq")
    return jax.shard_map(
        local,
        mesh=mesh,
        in_specs=(acts, acts, acts, lens, lens) + (P(),) * 11,
        out_specs=(acts, acts, acts) + (cut,) * 10,
        check_vma=False,
    )
```
